256 devices in a mesh: lon: 16 (over z, y_lo), lat: 16 (over y_hi, x, core).
Axes of the slice: x: 4, y: 4 (y_hi: 2, y_lo: 2; y = y_hi * 2 + y_lo), z: 8, core: 2. Of those that a mesh axis runs over, the one named last changes fastest.
Arguments:
- x_codes: bfloat16 [160, 128, 2048], P(None, 'lat', 'lon'), may hold values from -6 to 6
- x_scale: float32 [160, 128], P(None, 'lat'), may hold values from 0.3 to 3
- h_codes: bfloat16 [160, 128, 2048], P(None, 'lat', 'lon'), may hold values from -6 to 6
- h_scale: float32 [160, 128], P(None, 'lat'), may hold values from 0.3 to 3
- grad_out: bfloat16 [160, 128, 2048], P(None, 'lat', 'lon'), may hold values from -6 to 6
- land: int32 [128, 2048], P('lat', 'lon'), may hold values 0 or 1
- partner: int32 [2048], replicated, may hold values from 0 to 2047, as said below
- w_first: bfloat16 [3, 3, 160, 160], P(None, None, 'lat', 'lon'), may hold values from -0.15625 to 0.15625
- w_second: bfloat16 [3, 3, 160, 160], P(None, None, 'lat', 'lon'), may hold values from -0.15625 to 0.15625
Outputs:
- grad_in: float32 [160, 128, 2048], P(None, 'lat', 'lon')
- grad_first: float32 [3, 3, 160, 160], P(None, None, 'lat', 'lon')
- grad_second: float32 [3, 3, 160, 160], P(None, None, 'lat', 'lon')
The draws below stay inside these ranges and needn't reach their ends.
Inputs may be any that keep to these rules, and one draw needn't show every extreme that they name: partner[i] = (2 p - 1 - i) mod 2048 for one pivot column p, so partner[partner[i]] = i.
All inputs are finite; a program needn't handle non-finite values. No bound on the sum of `land` on one device may be relied on, other than what follows from the above.
Results may differ from the reference program's by a relative error of at most 0.0041.
Values may be sent and summed in bfloat16 or wider, within the bound.
A program may use at most 64 MiB of HBM per device.

```python
import math
import jax
import jax.numpy as jnp

C = 160
NLAT = 128
NLON = 2048


def draw_partner(key, part):
    pivot = jax.random.randint(key, (), 0, NLON, dtype=jnp.int32)
    columns = jnp.arange(NLON, dtype=jnp.int32)
    return ((2 * pivot - 1 - columns) % NLON).astype(jnp.int32)


def set_ends(values, own_key, low, high):
    dims = values.shape
    spot = [jax.random.randint(jax.random.fold_in(own_key, axis), (), 0, dims[axis]) for axis in range(len(dims))]
    values = values.at[tuple(spot)].set(low)
    longest = dims.index(max(dims))
    spot[longest] = (spot[longest] + 1) % dims[longest]
    return values.at[tuple(spot)].set(high)


def steps_of(stream_key, dims, cuts, smallest, largest):
    level, own = 1.0, jax.random.fold_in(stream_key, 6)
    for dim, parts in cuts:
        steps = jnp.exp(jax.random.uniform(jax.random.fold_in(own, dim), (parts,), jnp.float32, smallest / len(cuts), largest / len(cuts)))
        level = level * jnp.repeat(steps, dims[dim] // parts).reshape([-1 if axis == dim else 1 for axis in range(len(dims))])
    return level


def normal_values(rng, dims, spread, bound, pieces=(), kind=jnp.bfloat16):
    drawn = spread * jax.random.normal(rng, dims, jnp.float32)
    if pieces:
        drawn = drawn * steps_of(rng, dims, pieces, -0.22, 0.18)
    return jnp.clip(drawn, -bound, bound).astype(kind)


def setup_inputs(seed: int = 0) -> dict:
    arg_keys = jax.random.split(jax.random.key(seed), 10)
    return {
        "x_codes": normal_values(arg_keys[0], (C, NLAT, NLON), 1.0, 6.0, ((1, 16), (2, 16))),
        "x_scale": jnp.clip(jnp.exp(math.log(3.0) - 2.3025851 * jax.random.uniform(arg_keys[1], (C, NLAT), jnp.float32) ** steps_of(arg_keys[1], (C, NLAT), ((1, 16),), -0.2, 0.2)), 0.3, 3.0),
        "h_codes": normal_values(arg_keys[2], (C, NLAT, NLON), 1.0, 6.0, ((1, 16), (2, 16))),
        "h_scale": jnp.clip(jnp.exp(math.log(3.0) - 2.3025851 * jax.random.uniform(arg_keys[3], (C, NLAT), jnp.float32) ** steps_of(arg_keys[3], (C, NLAT), ((1, 16),), -0.2, 0.2)), 0.3, 3.0),
        "grad_out": normal_values(arg_keys[4], (C, NLAT, NLON), 1.0, 6.0, ((1, 16), (2, 16))),
        "land": set_ends((jax.random.randint(arg_keys[5], (NLAT, NLON), 0, 3) < 2).astype(jnp.int32), jax.random.fold_in(arg_keys[5], 1), 0, 1),
        "partner": draw_partner(jax.random.fold_in(arg_keys[9], 71), 0),
        "w_first": normal_values(arg_keys[7], (3, 3, C, C), (9 * C) ** -0.5, 0.15625, ((2, 16), (3, 16))),
        "w_second": normal_values(arg_keys[8], (3, 3, C, C), (9 * C) ** -0.5, 0.15625, ((2, 16), (3, 16))),
    }


def gelu_parts(h):
    k = math.sqrt(2.0 / math.pi)
    tanh_part = jnp.tanh(k * (h + 0.044715 * h * h * h))
    value = 0.5 * h * (1.0 + tanh_part)
    slope = 0.5 * (1.0 + tanh_part) + 0.5 * h * (1.0 - tanh_part * tanh_part) * k * (1.0 + 3.0 * 0.044715 * h * h)
    return (value, slope)

def extend(field, partner):
    ncols = field.shape[2]
    wide = jnp.concatenate([field[:, :, -1:], field, field[:, :, :1]], axis=2)
    index = (jnp.arange(ncols + 2, dtype=jnp.int32) - 1) % ncols
    north = jnp.take(field[:, -1, :], jnp.take(partner, index), axis=1)
    zeros = jnp.zeros_like(wide[:, :1, :])
    return jnp.concatenate([zeros, wide, north[:, None, :]], axis=1)

def weight_grad(grad, ext):
    height, width = (grad.shape[1], grad.shape[2])
    grad32 = grad.astype(jnp.float32)
    ext32 = ext.astype(jnp.float32)
    rows = []
    for ka in range(3):
        cols = []
        for kb in range(3):
            cols.append(jnp.einsum('ohw,chw->oc', grad32, ext32[:, ka:ka + height, kb:kb + width]))
        rows.append(jnp.stack(cols))
    return jnp.stack(rows)

def input_grad(grad, weight, partner):
    height, width = (grad.shape[1], grad.shape[2])
    padded = jnp.pad(grad.astype(jnp.float32), ((0, 0), (2, 2), (2, 2)))
    total = jnp.zeros((grad.shape[0], height + 2, width + 2), jnp.float32)
    for ka in range(3):
        for kb in range(3):
            total = total + jnp.einsum('oc,ohw->chw', weight[ka, kb].astype(jnp.float32), padded[:, 2 - ka:4 - ka + height, 2 - kb:4 - kb + width])
    zero = jnp.zeros(grad.shape, jnp.float32)
    _, back = jax.vjp(lambda field: extend(field, partner), zero)
    return back(total)[0]

def reference(x_codes, x_scale, h_codes, h_scale, grad_out, land, partner, w_first, w_second):
    ocean = land.astype(jnp.float32)
    x = (x_codes.astype(jnp.float32) * x_scale[:, :, None]).astype(jnp.bfloat16)
    h = h_codes.astype(jnp.float32) * h_scale[:, :, None]
    value, slope = gelu_parts(h)
    act = (ocean * value).astype(jnp.bfloat16)
    grad_y = (ocean * grad_out.astype(jnp.float32)).astype(jnp.bfloat16)
    factor = 1.0 / math.sqrt(NLAT * NLON)
    grad_second = weight_grad(grad_y, extend(act, partner)) * factor
    grad_act = input_grad(grad_y, w_second, partner)
    grad_h = (grad_act * ocean * slope).astype(jnp.bfloat16)
    grad_first = weight_grad(grad_h, extend(x, partner)) * factor
    grad_in = grad_out.astype(jnp.float32) + input_grad(grad_h, w_first, partner)
    return (grad_in, grad_first, grad_second)
```

```python
import functools
import math

import jax
import jax.numpy as jnp
from jax import lax
from jax.experimental import pallas as pl
from jax.experimental.pallas import tpu as pltpu
from jax.sharding import PartitionSpec as P

MESH = pl.DeviceIdType.MESH
F32, BF16 = jnp.float32, jnp.bfloat16
PAD = 16
LANES = 128
SUM_TYPE = jnp.float32


def up(value, unit):
    return -(-value // unit) * unit


def gelu_parts(h):
    k = math.sqrt(2.0 / math.pi)
    tanh_part = jnp.tanh(k * (h + 0.044715 * h * h * h))
    value = 0.5 * h * (1.0 + tanh_part)
    slope = 0.5 * (1.0 + tanh_part) + 0.5 * h * (1.0 - tanh_part * tanh_part) * k * (
        1.0 + 3.0 * 0.044715 * h * h
    )
    return (value, slope)


def dot(a, b):
    return lax.dot_general(a, b, (((1,), (0,)), ((), ())), preferred_element_type=F32)


def dot_nt(a, b):
    return lax.dot_general(a, b, (((1,), (1,)), ((), ())), preferred_element_type=F32)


def put(tiles, lane, source, source_lane, count, target_lane):
    shift = (target_lane - source_lane) % LANES
    moved = pltpu.roll(source, shift, 1) if shift else source
    tile, off = divmod(target_lane, LANES)
    keep = (lane >= off) & (lane < off + count)
    tiles[tile] = jnp.where(keep, moved, tiles[tile])
    over = off + count - LANES
    if over > 0:
        tiles[tile + 1] = jnp.where(lane < over, moved, tiles[tile + 1])


def put_wide(tiles, lane, sources, source_lane, count, target_lane):
    while count > 0:
        tile, off = divmod(source_lane, LANES)
        part = min(count, LANES - off)
        put(tiles, lane, sources[tile], off, part, target_lane)
        source_lane, target_lane, count = source_lane + part, target_lane + part, count - part


def kernel(
    cfg,
    x_ref, xs_ref, h_ref, hs_ref, g_ref, land_ref, partner_ref, w_ref,
    out_ref, first_ref, second_ref,
    cells, slope, wtile, wrow, wfull, wt, fy, fh, sa, sx, gx, ge, edge, edge_in,
    toprow, select, mcat, padder, qs, qe, tap, tap_in, part, part_in, small, small_in,
    st1_s, st1_r, st2_s, st2_r, fw_s, fw_r, ha_s, ha_r, mi_s, mi_r,
    r0_s, r0_r, r1_s, r1_r, r2_s, r2_r,
):
    C, H, NJ, NI = cfg["C"], cfg["H"], cfg["NJ"], cfg["NI"]
    W = LANES
    CJ, CI, NM = C // NJ, C // NI, NJ // 2
    LA = up(3 * C, LANES)
    ROWS = NJ * PAD
    N = H * W
    j, i = lax.axis_index("lat"), lax.axis_index("lon")
    k, m = lax.rem(j, 2), lax.div(j, 2)
    top = j == NJ - 1
    bottom = j == 0

    def rcopy(src, dst, ss, rs, dj, di):
        return pltpu.make_async_remote_copy(
            src_ref=src, dst_ref=dst, send_sem=ss, recv_sem=rs,
            device_id={"lat": dj, "lon": di}, device_id_type=MESH,
        )

    def each(lo, hi, fn):
        lax.fori_loop(lo, hi, lambda d, c: (fn(d), c)[1], 0)

    def lon(d):
        return lax.rem(i + d + NI, NI)

    def lat(d):
        return lax.rem(j + d + NJ, NJ)

    def mate(d):
        return lax.rem(m + d + NM, NM)

    barrier = pltpu.get_barrier_semaphore()

    def greet(dj, di):
        pl.semaphore_signal(barrier, inc=1, device_id={"lat": dj, "lon": di}, device_id_type=MESH)

    each(1, NI, lambda d: greet(j, lon(d)))
    each(1, NJ, lambda d: greet(lat(d), i))
    for dj in (1, -1):
        for di in (1, -1):
            greet(lat(dj), lon(di))

    def blocks(ref):
        cells[...] = ref[...].astype(F32).reshape(C * H, W)
        return [cells[pl.ds(r, C, stride=H), :] for r in range(H)]

    def ocean(r):
        return land_ref[r:r + 1, :].astype(F32)

    def slot(r):
        return pl.ds((r + 1) * W, W)

    lane = lax.broadcasted_iota(jnp.int32, (C, W), 1)

    def add_edges(packed, r, blk, base):
        west, east = base + r, base + H + r
        packed = jnp.where(lane == west, pltpu.roll(blk, west, 1) if west else blk, packed)
        return jnp.where(lane == east, pltpu.roll(blk, east + 1, 1), packed)

    pl.semaphore_wait(barrier, NI - 1 + NJ - 1 + 4)

    def tile_copy(d, other):
        return rcopy(w_ref, wtile.at[i if other is None else other], st1_s.at[d], st1_r.at[d], j, lon(d))

    each(1, NI, lambda d: tile_copy(d, None).start())
    wtile[i] = w_ref[...]

    packed = jnp.zeros((C, W), F32)
    for r, blk in enumerate(blocks(g_ref)):
        value = blk * ocean(r)
        fy[:, slot(r)] = value.astype(BF16)
        packed = add_edges(packed, r, value, 0)

    def top_copy(f, src, d, other):
        at = pl.ds(pl.multiple_of((i if other is None else other) * W, W), W)
        return rcopy(src, toprow.at[f, :, at], mi_s.at[f, d], mi_r.at[f, d], j, lon(d))

    def send_top(f, src):
        @pl.when(top)
        def _():
            each(1, NI, lambda d: top_copy(f, src, d, None).start())
            toprow[f, :, pl.ds(pl.multiple_of(i * W, W), W)] = src[...]

    center = pl.ds(C, C)
    send_top(0, fy.at[:, slot(H - 1)])

    for r, blk in enumerate(blocks(h_ref)):
        h = blk * hs_ref[:, r:r + 1]
        value, deriv = gelu_parts(h)
        act = (ocean(r) * value).astype(BF16)
        sa[center, slot(r)] = act
        slope[:, r * W:(r + 1) * W] = deriv
        packed = add_edges(packed, r, act.astype(F32), 2 * H)
    for r, blk in enumerate(blocks(x_ref)):
        x = (blk * xs_ref[:, r:r + 1]).astype(BF16)
        sx[center, slot(r)] = x
        packed = add_edges(packed, r, x.astype(F32), 4 * H)
    edge[0] = packed.astype(BF16)

    around = ((0, 1), (0, -1), (1, 1), (1, -1), (-1, 1), (-1, -1))

    def halo_copies(phase, fields):
        out = []
        for f, field in enumerate(fields):
            s = 2 * f
            out.append(rcopy(field.at[:, slot(H - 1)], field.at[:, slot(-1)],
                             ha_s.at[phase, s], ha_r.at[phase, s], lat(1), i))
            out.append(rcopy(field.at[:, slot(0)], field.at[:, slot(H)],
                             ha_s.at[phase, s + 1], ha_r.at[phase, s + 1], lat(-1), i))
        for n, (dj, di) in enumerate(around):
            out.append(rcopy(edge.at[phase], edge_in.at[phase, n],
                             ha_s.at[phase, 6 + n], ha_r.at[phase, 6 + n], lat(dj), lon(di)))
        return out

    early = halo_copies(0, (fy, sa.at[center], sx.at[center]))
    for copy in early:
        copy.start()
    send_top(1, sx.at[center, slot(H - 1)])

    row = lax.broadcasted_iota(jnp.int32, (ROWS, C), 0)
    col = lax.broadcasted_iota(jnp.int32, (ROWS, C), 1)
    half, rest = lax.div(row, NM * PAD), lax.rem(row, NM * PAD)
    own = lax.rem(rest, PAD)
    channel = (2 * lax.div(rest, PAD) + half) * CJ + own
    padder[...] = jnp.where((own < CJ) & (channel == col), 1.0, 0.0).astype(BF16)

    @pl.when(top)
    def _():
        ncols = NI * W
        mirror = partner_ref[pl.ds(i, 1), :]

        def fill(s, c):
            u = lax.broadcasted_iota(jnp.int32, (W, W), 0) + s * W
            for b in range(3):
                want = mirror + (1 - b)
                want = jnp.where(want < 0, want + ncols, want)
                want = jnp.where(want >= ncols, want - ncols, want)
                hot = jnp.where(u == want, 1.0, 0.0).astype(BF16)
                select[pl.ds(pl.multiple_of(s * W, W), W), b * W:(b + 1) * W] = hot
            return c

        lax.fori_loop(0, NI, fill, 0)

    each(1, NI, lambda d: tile_copy(d, lon(-d)).wait_recv())
    wlane = lax.broadcasted_iota(jnp.int32, (2 * PAD, W), 1)
    for a in range(3):
        tiles = [jnp.zeros((2 * PAD, W), F32) for _ in range(LA // W)]
        for s in range(NI):
            piece = wtile[s].astype(F32)
            for b in range(3):
                put(tiles, wlane, piece, (3 * a + b) * CI, CI, b * C + s * CI)
        for t, value in enumerate(tiles):
            at = pl.ds(a * LA + t * W, W)
            wrow[0, :, at] = value[:PAD].astype(BF16)
            wrow[1, :, at] = value[PAD:].astype(BF16)

    def slab_copy(w, d, other):
        return rcopy(wrow.at[w], wfull.at[w, k, m if other is None else other],
                     st2_s.at[w, d], st2_r.at[w, d], 2 * mate(d) + k, i)

    def forward_copy(w, d, mine):
        n = mate(-d)
        return rcopy(wfull.at[w, k, n], wfull.at[w, k if mine else 1 - k, n],
                     fw_s.at[w, d], fw_r.at[w, d], j + 1 - 2 * k, i)

    def own_forward(w, mine):
        return rcopy(wrow.at[w], wfull.at[w, k if mine else 1 - k, m], fw_s.at[w, 0], fw_r.at[w, 0],
                     j + 1 - 2 * k, i)

    for w in (1, 0):
        own_forward(w, True).start()
        each(1, NM, lambda d: slab_copy(w, d, None).start())
        wfull[w, k, m] = wrow[w]

    def pass_on(w):
        def step(d):
            slab_copy(w, d, mate(-d)).wait_recv()
            forward_copy(w, d, True).start()

        each(1, NM, step)

    def have_weights(w):
        own_forward(w, False).wait_recv()
        each(1, NM, lambda d: forward_copy(w, d, False).wait_recv())

    def columns(phase, base):
        got = [edge_in[phase, n].astype(F32) for n in range(6)]
        result = []
        for side, (mid, south, north) in ((0, (0, 2, 4)), (1, (1, 3, 5))):
            start = base + (H if side == 0 else 0)
            value = jnp.where((lane >= 1) & (lane <= H), pltpu.roll(got[mid], (1 - start) % W, 1), 0.0)
            lower = pltpu.roll(got[south], (0 - (start + H - 1)) % W, 1)
            upper = pltpu.roll(got[north], (H + 1 - start) % W, 1)
            value = jnp.where((lane == 0) & jnp.logical_not(bottom), lower, value)
            value = jnp.where((lane == H + 1) & jnp.logical_not(top), upper, value)
            result.append(value)
        return result

    def clear_ends(field):
        @pl.when(bottom)
        def _():
            field[:, slot(-1)] = jnp.zeros((C, W), BF16)

        @pl.when(top)
        def _():
            field[:, slot(H)] = jnp.zeros((C, W), BF16)

    def shifted(field, west, east):
        for r in range(-1, H + 1):
            blk = field[center, slot(r)].astype(F32)
            lower = jnp.where(lane == 0, pltpu.roll(west, (-(r + 1)) % W, 1), pltpu.roll(blk, 1, 1))
            upper = jnp.where(lane == W - 1, pltpu.roll(east, (W - 2 - r) % W, 1), pltpu.roll(blk, W - 1, 1))
            field[0:C, slot(r)] = lower.astype(BF16)
            field[2 * C:3 * C, slot(r)] = upper.astype(BF16)
        if LA > 3 * C:
            field[3 * C:LA, :] = jnp.zeros((LA - 3 * C, (H + 2) * W), BF16)

    def padded(field, west, east):
        gx[...] = dot(padder[...], field[...]).astype(BF16)
        for a in range(3):
            at_west = pltpu.roll(west, (a - 2) % W, 1)
            at_east = pltpu.roll(east, (H + a - 2) % W, 1)
            both = jnp.where(lane < H, at_west, jnp.where(lane < 2 * H, at_east, 0.0))
            ge[a] = dot(padder[...], both.astype(BF16)).astype(BF16)

    def mirrored(f):
        each(1, NI, lambda d: top_copy(f, fy.at[:, slot(H - 1)], d, lon(-d)).wait_recv())
        return dot(toprow[f], select[...]).astype(BF16)

    def tap_grad(w, field):
        for a in range(3):
            value = dot_nt(gx[:, W:W + N], field[:, a * W:a * W + N])
            tap[w, :, :, :, a * LA:(a + 1) * LA] = value.reshape(2, NM, PAD, LA)

    def input_grad(w):
        for a in range(3):
            wt[:, a * ROWS:(a + 1) * ROWS] = jnp.transpose(
                wfull[w].reshape(ROWS, 3 * LA)[:, a * LA:(a + 1) * LA].astype(F32)).astype(BF16)
        step = min(2 * W, N)
        for n in range(0, N, step):
            rhs = jnp.concatenate([gx[:, (2 - a) * W + n:(2 - a) * W + n + step] for a in range(3)], axis=0)
            qs[:, n:n + step] = dot(wt[...], rhs)
        qe[...] = dot(wt[...], jnp.concatenate([ge[a] for a in range(3)], axis=0))

        @pl.when(top)
        def _():
            fold = dot(wt[:, 2 * ROWS:3 * ROWS], mcat[...])
            for b in range(3):
                qs[C:2 * C, N - W:N] += fold[b * C:(b + 1) * C, b * W:(b + 1) * W]

        first, last = qe[0:C, :], qe[2 * C:3 * C, :]
        result = []
        for r in range(H):
            at = slice(r * W, (r + 1) * W)
            left = jnp.where(lane == W - 1, pltpu.roll(first, (W - 1 - H - r) % W, 1),
                             pltpu.roll(qs[0:C, at], W - 1, 1))
            right = jnp.where(lane == 0, pltpu.roll(last, (-r) % W, 1), pltpu.roll(qs[2 * C:3 * C, at], 1, 1))
            result.append(qs[C:2 * C, at] + left + right)
        return result

    def pair_copy(w, n, mine):
        return rcopy(tap.at[w, 1 - k, n], tap_in.at[w, n], r0_s.at[w, n], r0_r.at[w, n], j + 1 - 2 * k, i)

    def chip_copy(w, d, other):
        return rcopy(part.at[w, mate(d)], part_in.at[w, m if other is None else other],
                     r1_s.at[w, d], r1_r.at[w, d], 2 * mate(d) + k, i)

    def lon_copy(w, d, other):
        return rcopy(small.at[w, lon(d)], small_in.at[w, i if other is None else other],
                     r2_s.at[w, d], r2_r.at[w, d], j, lon(d))

    def sum_start(w):
        each(1, NM, lambda d: pair_copy(w, mate(d), True).start())
        pair_copy(w, m, True).start()

    def sum_chips(w):
        def step(d):
            n = mate(d)
            pair_copy(w, n, False).wait_recv()
            part[w, n] = (tap[w, k, n] + tap_in[w, n]).astype(SUM_TYPE)
            chip_copy(w, d, None).start()

        each(1, NM, step)
        pair_copy(w, m, False).wait_recv()

    def sum_lon(w):
        total = tap[w, k, m] + tap_in[w, m]
        for d in range(1, NM):
            chip_copy(w, d, mate(-d)).wait_recv()
            total = total + part_in[w, mate(-d)].astype(F32)
        slane = lax.broadcasted_iota(jnp.int32, (PAD, W), 1)
        sources = [total[:, t * W:(t + 1) * W] for t in range(3 * LA // W)]
        for s in range(NI):
            tiles = [jnp.zeros((PAD, W), F32)]
            for a in range(3):
                for b in range(3):
                    put_wide(tiles, slane, sources, a * LA + b * C + s * CI, CI, (3 * a + b) * CI)
            small[w, s] = tiles[0]
        small_in[w, i] = small[w, i]
        each(1, NI, lambda d: lon_copy(w, d, None).start())

    def sum_end(w, ref):
        each(1, NI, lambda d: lon_copy(w, d, lon(-d)).wait_recv())
        total = small_in[w, 0]
        for s in range(1, NI):
            total = total + small_in[w, s]
        total = total * cfg["factor"]
        for a in range(3):
            for b in range(3):
                n = 3 * a + b
                moved = pltpu.roll(total, (-n * CI) % W, 1) if n else total
                ref[a, b] = moved[:CJ, :CI]

    for copy in early:
        copy.wait_recv()
    clear_ends(fy)
    clear_ends(sa.at[center])
    clear_ends(sx.at[center])
    west, east = columns(0, 0)
    padded(fy, west, east)
    west, east = columns(0, 2 * H)
    shifted(sa, west, east)
    pass_on(1)

    tap_grad(1, sa)

    @pl.when(top)
    def _():
        mcat[...] = dot(padder[...], mirrored(0)).astype(BF16)
        act = sa[center, slot(H - 1)]
        for b in range(3):
            place = lax.broadcasted_iota(jnp.int32, (C, LA), 1) == (
                lax.broadcasted_iota(jnp.int32, (C, LA), 0) + b * C)
            spread = lax.dot_general(act, jnp.where(place, 1.0, 0.0).astype(BF16), (((0,), (0,)), ((), ())),
                                     preferred_element_type=F32).astype(BF16)
            value = dot(mcat[:, b * W:(b + 1) * W], spread)
            tap[1, :, :, :, 2 * LA:3 * LA] += value.reshape(2, NM, PAD, LA)

    sum_start(1)
    west, east = columns(0, 4 * H)
    shifted(sx, west, east)

    have_weights(1)
    grad_act = input_grad(1)
    packed = jnp.zeros((C, W), F32)
    for r in range(H):
        value = (grad_act[r] * ocean(r) * slope[:, r * W:(r + 1) * W]).astype(BF16)
        fh[:, slot(r)] = value
        packed = add_edges(packed, r, value.astype(F32), 0)
    edge[1] = packed.astype(BF16)
    late = halo_copies(1, (fh,))
    for copy in late:
        copy.start()
    send_top(2, fh.at[:, slot(H - 1)])

    @pl.when(top)
    def _():
        north = mirrored(1)
        for b in range(3):
            sx[b * C:(b + 1) * C, slot(H)] = north[:, b * W:(b + 1) * W]

    gx[:, W:W + N] = dot(padder[...], fh[:, W:W + N]).astype(BF16)
    tap_grad(0, sx)
    sum_start(0)
    sum_chips(1)
    pass_on(0)
    sum_chips(0)
    sum_lon(1)

    for copy in late:
        copy.wait_recv()
    clear_ends(fh)
    west, east = columns(1, 0)
    padded(fh, west, east)
    have_weights(0)

    @pl.when(top)
    def _():
        mcat[...] = dot(padder[...], mirrored(2)).astype(BF16)

    result = input_grad(0)
    cells[...] = g_ref[...].astype(F32).reshape(C * H, W)
    for r in range(H):
        at = pl.ds(r, C, stride=H)
        out_ref[at, :] = cells[at, :] + result[r]

    sum_end(1, second_ref)
    sum_lon(0)
    sum_end(0, first_ref)

    each(1, NI, lambda d: tile_copy(d, None).wait_send())
    for copy in early + late:
        copy.wait_send()
    for w in range(2):
        own_forward(w, True).wait_send()
        each(1, NM, lambda d: slab_copy(w, d, None).wait_send())
        each(1, NM, lambda d: forward_copy(w, d, True).wait_send())
        each(0, NM, lambda n: pair_copy(w, n, True).wait_send())
        each(1, NM, lambda d: chip_copy(w, d, None).wait_send())
        each(1, NI, lambda d: lon_copy(w, d, None).wait_send())

    @pl.when(top)
    def _():
        for f in range(3):
            each(1, NI, lambda d: top_copy(f, fy.at[:, slot(H - 1)], d, None).wait_send())


def body(x_codes, x_scale, h_codes, h_scale, grad_out, land, partner, w_first, w_second):
    C, H, W = x_codes.shape
    NJ, NI = lax.axis_size("lat"), lax.axis_size("lon")
    CJ, CI, NM = C // NJ, C // NI, NJ // 2
    LA, ROWS, N = up(3 * C, LANES), NJ * PAD, H * W
    cfg = {"C": C, "H": H, "NJ": NJ, "NI": NI, "factor": 1.0 / math.sqrt(NJ * H * NI * W)}
    taps = jnp.stack([w_first, w_second]).reshape(2, 9, CJ, CI).transpose(0, 2, 1, 3).reshape(2, CJ, 9 * CI)
    taps = jnp.pad(taps, ((0, 0), (0, PAD - CJ), (0, LANES - 9 * CI))).reshape(2 * PAD, LANES)
    sem = pltpu.SemaphoreType.DMA
    vm = pltpu.VMEM
    scratch = [
        vm((C * H, W), F32),
        vm((C, N), F32),
        vm((NI, 2 * PAD, LANES), BF16),
        vm((2, PAD, 3 * LA), BF16),
        vm((2, 2, NM, PAD, 3 * LA), BF16),
        vm((LA, 3 * ROWS), BF16),
        vm((C, N + 2 * W), BF16),
        vm((C, N + 2 * W), BF16),
        vm((LA, N + 2 * W), BF16),
        vm((LA, N + 2 * W), BF16),
        vm((ROWS, N + 2 * W), BF16),
        vm((3, ROWS, W), BF16),
        vm((2, C, W), BF16),
        vm((2, 6, C, W), BF16),
        vm((3, C, NI * W), BF16),
        vm((NI * W, 3 * W), BF16),
        vm((ROWS, 3 * W), BF16),
        vm((ROWS, C), BF16),
        vm((LA, N), F32),
        vm((LA, W), F32),
        vm((2, 2, NM, PAD, 3 * LA), F32),
        vm((2, NM, PAD, 3 * LA), F32),
        vm((2, NM, PAD, 3 * LA), SUM_TYPE),
        vm((2, NM, PAD, 3 * LA), SUM_TYPE),
        vm((2, NI, PAD, LANES), F32),
        vm((2, NI, PAD, LANES), F32),
        sem((NI,)), sem((NI,)), sem((2, NM)), sem((2, NM)), sem((2, NM)), sem((2, NM)),
        sem((2, 12)), sem((2, 12)), sem((3, NI)), sem((3, NI)),
        sem((2, NM)), sem((2, NM)), sem((2, NM)), sem((2, NM)), sem((2, NI)), sem((2, NI)),
    ]
    grad_in, first, second = pl.pallas_call(
        functools.partial(kernel, cfg),
        out_shape=(
            jax.ShapeDtypeStruct((C * H, W), F32),
            jax.ShapeDtypeStruct((3, 3, CJ, CI), F32),
            jax.ShapeDtypeStruct((3, 3, CJ, CI), F32),
        ),
        in_specs=[pl.BlockSpec(memory_space=vm)] * 8,
        out_specs=[pl.BlockSpec(memory_space=vm)] * 3,
        scratch_shapes=scratch,
        compiler_params=pltpu.CompilerParams(
            collective_id=0, has_side_effects=True, vmem_limit_bytes=56 * 1024 * 1024
        ),
    )(x_codes, x_scale, h_codes, h_scale, grad_out, land, partner.reshape(NI, W), taps)
    return (grad_in.reshape(C, H, W), first, second)


def solution(mesh):
    placed = (
        P(None, "lat", "lon"),
        P(None, "lat"),
        P(None, "lat", "lon"),
        P(None, "lat"),
        P(None, "lat", "lon"),
        P("lat", "lon"),
        P(),
        P(None, None, "lat", "lon"),
        P(None, None, "lat", "lon"),
    )
    return jax.shard_map(
        body,
        mesh=mesh,
        in_specs=placed,
        out_specs=(P(None, "lat", "lon"), P(None, None, "lat", "lon"), P(None, None, "lat", "lon")),
        check_vma=False,
    )
```

```python
import functools
import math

import jax
import jax.numpy as jnp
from jax import lax
from jax.experimental import pallas as pl
from jax.experimental.pallas import tpu as pltpu
from jax.sharding import PartitionSpec as P

MESH = pl.DeviceIdType.MESH
F32, BF16 = jnp.float32, jnp.bfloat16
PAD = 16
LANES = 128
SUM_TYPE = jnp.bfloat16


def up(value, unit):
    return -(-value // unit) * unit


def gelu_parts(h):
    k = math.sqrt(2.0 / math.pi)
    tanh_part = jnp.tanh(k * (h + 0.044715 * h * h * h))
    value = 0.5 * h * (1.0 + tanh_part)
    slope = 0.5 * (1.0 + tanh_part) + 0.5 * h * (1.0 - tanh_part * tanh_part) * k * (
        1.0 + 3.0 * 0.044715 * h * h
    )
    return (value, slope)


def dot(a, b):
    return lax.dot_general(a, b, (((1,), (0,)), ((), ())), preferred_element_type=F32)


def dot_nt(a, b):
    return lax.dot_general(a, b, (((1,), (1,)), ((), ())), preferred_element_type=F32)


def put(tiles, lane, source, source_lane, count, target_lane):
    shift = (target_lane - source_lane) % LANES
    moved = pltpu.roll(source, shift, 1) if shift else source
    tile, off = divmod(target_lane, LANES)
    keep = (lane >= off) & (lane < off + count)
    tiles[tile] = jnp.where(keep, moved, tiles[tile])
    over = off + count - LANES
    if over > 0:
        tiles[tile + 1] = jnp.where(lane < over, moved, tiles[tile + 1])


def put_wide(tiles, lane, sources, source_lane, count, target_lane):
    while count > 0:
        tile, off = divmod(source_lane, LANES)
        part = min(count, LANES - off)
        put(tiles, lane, sources[tile], off, part, target_lane)
        source_lane, target_lane, count = source_lane + part, target_lane + part, count - part


def kernel(
    cfg,
    x_ref, xs_ref, h_ref, hs_ref, g_ref, land_ref, partner_ref, w0_ref, w1_ref,
    out_ref, first_ref, second_ref,
    cells, slope, wtmp, wown, wtile, wrow, wfull, wt, wp, fy, fh, sa, sx, gq, edge, edge_in,
    mrow, mout, mirr, spread, qs, nat, tap, tap_in, part, part_in, tot, small, small_in,
    st1_s, st1_r, st2_s, st2_r, fw_s, fw_r, ha_s, ha_r, mi_s, mi_r, mo_s, mo_r,
    r0_s, r0_r, r1_s, r1_r, r2_s, r2_r,
):
    C, H, NJ, NI = cfg["C"], cfg["H"], cfg["NJ"], cfg["NI"]
    W = LANES
    CJ, CI, NM, NG = C // NJ, C // NI, NJ // 2, C // PAD
    LA, CL, RB = up(3 * C, LANES), up(C, LANES), up(3 * (C // NJ), PAD)
    ROWS = NJ * RB
    N = H * W
    j, i = lax.axis_index("lat"), lax.axis_index("lon")
    k, m = lax.rem(j, 2), lax.div(j, 2)
    top = j == NJ - 1
    bottom = j == 0
    worker = top & (i < NG)

    def rcopy(src, dst, ss, rs, dj, di):
        return pltpu.make_async_remote_copy(
            src_ref=src, dst_ref=dst, send_sem=ss, recv_sem=rs,
            device_id={"lat": dj, "lon": di}, device_id_type=MESH,
        )

    def each(lo, hi, fn):
        lax.fori_loop(lo, hi, lambda d, c: (fn(d), c)[1], 0)

    def lon(d):
        return lax.rem(i + d + NI, NI)

    def lat(d):
        return lax.rem(j + d + NJ, NJ)

    def mate(d):
        return lax.rem(m + d + NM, NM)

    barrier = pltpu.get_barrier_semaphore()

    def greet(dj, di):
        pl.semaphore_signal(barrier, inc=1, device_id={"lat": dj, "lon": di}, device_id_type=MESH)

    each(1, NI, lambda d: greet(j, lon(d)))
    each(1, NJ, lambda d: greet(lat(d), i))
    for dj in (1, -1):
        for di in (1, -1):
            greet(lat(dj), lon(di))

    for w, ref in ((1, w1_ref), (0, w0_ref)):
        wtmp[...] = jnp.zeros(wtmp.shape, F32)
        for a in range(3):
            block = ref[a].astype(F32)
            for b in range(3):
                wtmp[3 * a + b, 0:CJ, 0:CI] = block[:, b, :]
        value = wtmp[0]
        for n in range(1, 9):
            value = value + pltpu.roll(wtmp[n], n * CI, 1)
        wown[w] = value.astype(BF16)

    def blocks(ref):
        cells[...] = ref[...].astype(F32).reshape(C * H, W)
        return [cells[pl.ds(r, C, stride=H), :] for r in range(H)]

    def ocean(r):
        return land_ref[r:r + 1, :].astype(F32)

    def slot(r):
        return pl.ds((r + 1) * W, W)

    lane = lax.broadcasted_iota(jnp.int32, (C, W), 1)
    center = pl.ds(C, C)

    def add_edges(packed, f, r, blk):
        spots = [f * 8 + r]
        if r == H - 1:
            spots.append(32 + f)
        if r == 0:
            spots.append(48 + f)
        for spot in spots:
            packed = jnp.where(lane == spot, pltpu.roll(blk, spot, 1) if spot else blk, packed)
            packed = jnp.where(lane == 64 + spot, pltpu.roll(blk, 65 + spot, 1), packed)
        return packed

    def turn_edges(phase, packed):
        if CL > C:
            packed = jnp.concatenate([packed, jnp.zeros((CL - C, W), F32)], axis=0)
        edge[phase] = jnp.transpose(packed).astype(BF16)

    scale = jnp.transpose(xs_ref[...])
    packed = jnp.zeros((C, W), F32)
    for r, blk in enumerate(blocks(g_ref)):
        value = blk * ocean(r)
        fy[:, slot(r)] = value.astype(BF16)
        packed = add_edges(packed, 0, r, value)
    for r, blk in enumerate(blocks(x_ref)):
        x = (blk * scale[:, r:r + 1]).astype(BF16)
        sx[center, slot(r)] = x
        packed = add_edges(packed, 2, r, x.astype(F32))

    pl.semaphore_wait(barrier, NI - 1 + NJ - 1 + 4)

    def tile_copy(w, d, other):
        return rcopy(wown.at[w], wtile.at[w, i if other is None else other],
                     st1_s.at[w, d], st1_r.at[w, d], j, lon(d))

    each(1, NI, lambda d: tile_copy(1, d, None).start())
    wtile[1, i] = wown[1]

    def row_copy(f, src, d, other):
        g = lon(d) if other is None else i
        return rcopy(src.at[pl.ds(pl.multiple_of(g * PAD, PAD), PAD), slot(H - 1)],
                     mrow.at[f, i if other is None else other], mi_s.at[f, d], mi_r.at[f, d], j, lon(d))

    def turned_copy(f, d, other):
        g = i if other is None else other
        return rcopy(mout.at[f, lon(d)], mirr.at[f, pl.ds(pl.multiple_of(g * PAD, PAD), PAD)],
                     mo_s.at[f, d], mo_r.at[f, d], j, lon(d))

    def mirror_send(f, src):
        @pl.when(top)
        def _():
            def step(d):
                @pl.when(lon(d) < NG)
                def _():
                    row_copy(f, src, d, None).start()

            each(1, NI, step)

            @pl.when(i < NG)
            def _():
                mrow[f, i] = src[pl.ds(pl.multiple_of(i * PAD, PAD), PAD), slot(H - 1)]

    def mirror_turn(f, src):
        @pl.when(worker)
        def _():
            each(1, NI, lambda d: row_copy(f, src, d, lon(-d)).wait_recv())
            ncols = NI * W
            flip = (lax.broadcasted_iota(jnp.int32, (W, W), 0)
                    + lax.broadcasted_iota(jnp.int32, (W, W), 1)) == W - 1
            rev = dot(mrow[f].reshape(NI * PAD, W), jnp.where(flip, 1.0, 0.0).astype(BF16))
            tiles = [rev[(NI - 1 - v) * PAD:(NI - v) * PAD] for v in range(NI)]
            tlane = lax.broadcasted_iota(jnp.int32, (PAD, W), 1)
            where = partner_ref[pl.ds(i, 1), :] + lax.broadcasted_iota(jnp.int32, (1, W), 1) + i * W
            turn = (ncols - 1) - (where & (ncols - 1))
            turn = jnp.broadcast_to(turn, (PAD, W))

            def left(tiles, by):
                if by % W == 0:
                    return [tiles[(t + by // W) % NI] for t in range(NI)]
                moved = [pltpu.roll(tile, W - by, 1) for tile in tiles]
                return [jnp.where(tlane < W - by, moved[t], moved[(t + 1) % NI]) for t in range(NI)]

            for bit in range(ncols.bit_length() - 1):
                take = (turn & (1 << bit)) != 0
                tiles = [jnp.where(take, new, old) for new, old in zip(left(tiles, 1 << bit), tiles)]
            moved = [pltpu.roll(tile, 1, 1) for tile in tiles]
            before = [jnp.where(tlane == 0, moved[t - 1], moved[t]) for t in range(NI)]
            for b, group in enumerate((before, tiles, left(tiles, 1))):
                for t in range(NI):
                    mout[f, t, :, b * W:(b + 1) * W] = group[t].astype(BF16)
            mirr[f, pl.ds(pl.multiple_of(i * PAD, PAD), PAD), :] = mout[f, i]
            each(1, NI, lambda d: turned_copy(f, d, None).start())

    def mirror_wait(f):
        def step(d):
            @pl.when(lon(-d) < NG)
            def _():
                turned_copy(f, d, lon(-d)).wait_recv()

        each(1, NI, step)

    mirror_send(0, fy)
    mirror_send(1, sx.at[center])

    scale = jnp.transpose(hs_ref[...])
    for r, blk in enumerate(blocks(h_ref)):
        h = blk * scale[:, r:r + 1]
        value, deriv = gelu_parts(h)
        act = (ocean(r) * value).astype(BF16)
        sa[center, slot(r)] = act
        slope[:, r * W:(r + 1) * W] = deriv
        packed = add_edges(packed, 1, r, act.astype(F32))
    turn_edges(0, packed)

    def halo_copies(phase, fields):
        out = []
        for f, field in enumerate(fields):
            s = 2 * f
            out.append(rcopy(field.at[:, slot(H - 1)], field.at[:, slot(-1)],
                             ha_s.at[phase, s], ha_r.at[phase, s], lat(1), i))
            out.append(rcopy(field.at[:, slot(0)], field.at[:, slot(H)],
                             ha_s.at[phase, s + 1], ha_r.at[phase, s + 1], lat(-1), i))
        side = up(8 * len(fields), PAD)
        n = 6
        for di, base, target in ((1, 64, 0), (-1, 0, 64)):
            for dj, off, size in ((0, 0, side), (1, 32, PAD), (-1, 48, PAD)):
                out.append(rcopy(edge.at[phase, pl.ds(base + off, size)],
                                 edge_in.at[phase, pl.ds(target + off, size)],
                                 ha_s.at[phase, n], ha_r.at[phase, n], lat(dj), lon(di)))
                n += 1
        return out

    early = halo_copies(0, (fy, sa.at[center], sx.at[center]))
    for copy in early:
        copy.start()

    at = lax.broadcasted_iota(jnp.int32, (ROWS, 1), 0)
    half, rest = lax.div(at, NM * RB), lax.rem(at, NM * RB)
    own = lax.rem(rest, RB)
    line = lax.div(own, CJ)
    target = line * C + (2 * lax.div(rest, RB) + half) * CJ + own - line * CJ
    target = jnp.where(own < 3 * CJ, target, -1)
    spread[...] = jnp.where(lax.broadcasted_iota(jnp.int32, (ROWS, 3 * C), 1) == target, 1.0, 0.0).astype(BF16)

    def make_slab(w):
        each(1, NI, lambda d: tile_copy(w, d, lon(-d)).wait_recv())
        wlane = lax.broadcasted_iota(jnp.int32, (PAD, W), 1)
        tot[...] = jnp.zeros(tot.shape, F32)
        pieces = [wtile[w, s].astype(F32) for s in range(NI)]
        for a in range(3):
            tiles = [jnp.zeros((PAD, W), F32) for _ in range(LA // W)]
            for s in range(NI):
                for b in range(3):
                    put(tiles, wlane, pieces[s], (3 * a + b) * CI, CI, b * C + s * CI)
            for t, value in enumerate(tiles):
                tot[a * CJ:(a + 1) * CJ, t * W:(t + 1) * W] = value[:CJ]
        wrow[w] = tot[0:RB].astype(BF16)

    def slab_copy(w, d, other):
        return rcopy(wrow.at[w], wfull.at[w, k, m if other is None else other],
                     st2_s.at[w, d], st2_r.at[w, d], 2 * mate(d) + k, i)

    def forward_copy(w, d, mine):
        n = mate(-d)
        return rcopy(wfull.at[w, k, n], wfull.at[w, k if mine else 1 - k, n],
                     fw_s.at[w, d], fw_r.at[w, d], j + 1 - 2 * k, i)

    def own_forward(w, mine):
        return rcopy(wrow.at[w], wfull.at[w, k if mine else 1 - k, m], fw_s.at[w, 0], fw_r.at[w, 0],
                     j + 1 - 2 * k, i)

    def send_slab(w):
        each(1, NM, lambda d: slab_copy(w, d, None).start())
        own_forward(w, True).start()
        wfull[w, k, m] = wrow[w]

    def pass_on(w):
        def step(d):
            slab_copy(w, d, mate(-d)).wait_recv()
            forward_copy(w, d, True).start()

        each(1, NM, step)

    def have_weights(w):
        own_forward(w, False).wait_recv()
        each(1, NM, lambda d: forward_copy(w, d, False).wait_recv())
        wt[...] = jnp.transpose(wfull[w].reshape(ROWS, LA).astype(F32)).astype(BF16)

    def columns(got, f):
        result = []
        for base in (0, 64):
            start = base + f * 8
            value = jnp.where((lane >= 1) & (lane <= H), pltpu.roll(got, (1 - start) % W, 1), 0.0)
            lower = pltpu.roll(got, (-(base + 32 + f)) % W, 1)
            upper = pltpu.roll(got, (H + 1 - (base + 48 + f)) % W, 1)
            value = jnp.where((lane == 0) & jnp.logical_not(bottom), lower, value)
            value = jnp.where((lane == H + 1) & jnp.logical_not(top), upper, value)
            result.append(value)
        return result

    def turned_edges(phase):
        return jnp.transpose(edge_in[phase].astype(F32))[:C]

    def clear_ends(field):
        @pl.when(bottom)
        def _():
            field[:, slot(-1)] = jnp.zeros((C, W), BF16)

        @pl.when(top)
        def _():
            field[:, slot(H)] = jnp.zeros((C, W), BF16)

    def shifted(field, west, east):
        for r in range(-1, H + 1):
            blk = field[center, slot(r)].astype(F32)
            lower = jnp.where(lane == 0, pltpu.roll(west, (-(r + 1)) % W, 1), pltpu.roll(blk, 1, 1))
            upper = jnp.where(lane == W - 1, pltpu.roll(east, (W - 2 - r) % W, 1), pltpu.roll(blk, W - 1, 1))
            field[0:C, slot(r)] = lower.astype(BF16)
            field[2 * C:3 * C, slot(r)] = upper.astype(BF16)
        if LA > 3 * C:
            field[3 * C:LA, :] = jnp.zeros((LA - 3 * C, (H + 2) * W), BF16)

    def tap_rows(field, n, size):
        return jnp.concatenate([field[:, (2 - a) * W + n:(2 - a) * W + n + size] for a in range(3)], axis=0)

    def edge_rows(west, east):
        both = []
        for a in range(3):
            at_west = pltpu.roll(west, (a - 2) % W, 1)
            at_east = pltpu.roll(east, (H + a - 2) % W, 1)
            value = jnp.where(lane < H, at_west, jnp.where(lane < 2 * H, at_east, 0.0))
            both.append(value.astype(BF16))
        return jnp.concatenate(both, axis=0)

    def fold_rows(f):
        return jnp.concatenate([jnp.zeros((2 * C, 3 * W), BF16), mirr[f]], axis=0)

    step = min(2 * W, N)

    def tap_grad(w, grad, field):
        for a in range(3):
            nat[a] = dot_nt(grad[:, W:W + N], field[:, a * W:a * W + N])

    def tap_store(w):
        for a in range(3):
            for jj in range(NJ):
                tap[w, jj % 2, jj // 2, a * CJ:(a + 1) * CJ, :] = nat[a, jj * CJ:(jj + 1) * CJ, :]

    def add_fold(fold):
        for b in range(3):
            qs[C:2 * C, N - W:N] += fold[b * C:(b + 1) * C, b * W:(b + 1) * W]

    def shift_sum():
        first, last = qs[0:C, N:N + W], qs[2 * C:3 * C, N:N + W]
        result = []
        for r in range(H):
            at = slice(r * W, (r + 1) * W)
            left = jnp.where(lane == W - 1, pltpu.roll(first, (W - 1 - H - r) % W, 1),
                             pltpu.roll(qs[0:C, at], W - 1, 1))
            right = jnp.where(lane == 0, pltpu.roll(last, (-r) % W, 1), pltpu.roll(qs[2 * C:3 * C, at], 1, 1))
            result.append(qs[C:2 * C, at] + left + right)
        return result

    def pair_copy(w, n, mine):
        return rcopy(tap.at[w, 1 - k, n], tap_in.at[w, n], r0_s.at[w, n], r0_r.at[w, n], j + 1 - 2 * k, i)

    def chip_copy(w, d, other):
        return rcopy(part.at[w, mate(d)], part_in.at[w, m if other is None else other],
                     r1_s.at[w, d], r1_r.at[w, d], 2 * mate(d) + k, i)

    def lon_copy(w, d, other):
        return rcopy(small.at[w, lon(d)], small_in.at[w, i if other is None else other],
                     r2_s.at[w, d], r2_r.at[w, d], j, lon(d))

    def sum_start(w):
        each(1, NM, lambda d: pair_copy(w, mate(d), True).start())
        pair_copy(w, m, True).start()

    def sum_chips(w):
        def step(d):
            n = mate(d)
            pair_copy(w, n, False).wait_recv()
            part[w, n] = (tap[w, k, n] + tap_in[w, n]).astype(SUM_TYPE)
            chip_copy(w, d, None).start()

        each(1, NM, step)
        pair_copy(w, m, False).wait_recv()

    def sum_lon(w):
        total = tap[w, k, m] + tap_in[w, m]
        for d in range(1, NM):
            chip_copy(w, d, mate(-d)).wait_recv()
            total = total + part_in[w, mate(-d)].astype(F32)
        tot[0:RB] = total
        slane = lax.broadcasted_iota(jnp.int32, (PAD, W), 1)
        sources = [[tot[a * CJ:a * CJ + PAD, t * W:(t + 1) * W] for t in range(LA // W)] for a in range(3)]
        for s in range(NI):
            tiles = [jnp.zeros((PAD, W), F32)]
            for a in range(3):
                for b in range(3):
                    put_wide(tiles, slane, sources[a], b * C + s * CI, CI, (3 * a + b) * CI)
            small[w, s] = tiles[0]
        small_in[w, i] = small[w, i]
        each(1, NI, lambda d: lon_copy(w, d, None).start())

    def sum_end(w, ref):
        each(1, NI, lambda d: lon_copy(w, d, lon(-d)).wait_recv())
        total = small_in[w, 0]
        for s in range(1, NI):
            total = total + small_in[w, s]
        total = total * cfg["factor"]
        for a in range(3):
            for b in range(3):
                n = 3 * a + b
                moved = pltpu.roll(total, (-n * CI) % W, 1) if n else total
                ref[a, :, b, :] = moved[:CJ, :CI]

    make_slab(1)
    send_slab(1)
    each(1, NI, lambda d: tile_copy(0, d, None).start())
    wtile[0, i] = wown[0]
    mirror_turn(0, fy)
    mirror_turn(1, sx.at[center])
    for w in range(2):
        tap[w, :, :, 3 * CJ:RB, :] = jnp.zeros((2, NM, RB - 3 * CJ, LA), F32)

    for copy in early:
        copy.wait_recv()
    clear_ends(fy)
    clear_ends(sa.at[center])
    clear_ends(sx.at[center])
    got = turned_edges(0)
    west, east = columns(got, 0)
    for n in range(0, N, step):
        gq[:, n:n + step] = dot(spread[...], tap_rows(fy, n, step)).astype(BF16)
    gq[:, N:N + W] = dot(spread[...], edge_rows(west, east)).astype(BF16)
    pass_on(1)

    west, east = columns(got, 1)
    shifted(sa, west, east)
    west, east = columns(got, 2)
    shifted(sx, west, east)

    tap_grad(1, fy, sa)

    @pl.when(top)
    def _():
        mirror_wait(0)
        act = sa[center, slot(H - 1)]
        for b in range(3):
            place = lax.broadcasted_iota(jnp.int32, (C, LA), 1) == (
                lax.broadcasted_iota(jnp.int32, (C, LA), 0) + b * C)
            wide = lax.dot_general(act, jnp.where(place, 1.0, 0.0).astype(BF16), (((0,), (0,)), ((), ())),
                                   preferred_element_type=F32).astype(BF16)
            nat[2] += dot(mirr[0, :, b * W:(b + 1) * W], wide)
        mirror_wait(1)
        for b in range(3):
            sx[b * C:(b + 1) * C, slot(H)] = mirr[1, :, b * W:(b + 1) * W]

    tap_store(1)
    make_slab(0)

    have_weights(1)
    sum_start(1)
    send_slab(0)
    for n in range(0, N + W, step):
        size = min(step, N + W - n)
        qs[:, n:n + size] = dot(wt[...], gq[:, n:n + size])

    @pl.when(top)
    def _():
        add_fold(dot(wt[...], dot(spread[...], fold_rows(0)).astype(BF16)))

    packed = jnp.zeros((C, W), F32)
    for r, value in enumerate(shift_sum()):
        value = (value * ocean(r) * slope[:, r * W:(r + 1) * W]).astype(BF16)
        fh[:, slot(r)] = value
        packed = add_edges(packed, 0, r, value.astype(F32))
    turn_edges(1, packed)
    late = halo_copies(1, (fh,))
    for copy in late:
        copy.start()
    mirror_send(2, fh)
    sum_chips(1)

    tap_grad(0, fh, sx)
    tap_store(0)
    sum_start(0)
    pass_on(0)
    mirror_turn(2, fh)
    sum_chips(0)

    have_weights(0)
    wp[...] = dot(wt[...], spread[...]).astype(BF16)
    for copy in late:
        copy.wait_recv()
    clear_ends(fh)
    west, east = columns(turned_edges(1), 0)
    sum_lon(1)
    for n in range(0, N, step):
        qs[:, n:n + step] = dot(wp[...], tap_rows(fh, n, step))
    qs[:, N:N + W] = dot(wp[...], edge_rows(west, east))

    @pl.when(top)
    def _():
        mirror_wait(2)
        add_fold(dot(wp[...], fold_rows(2)))

    for r, value in enumerate(shift_sum()):
        out_ref[pl.ds(r, C, stride=H), :] = value

    sum_lon(0)
    sum_end(1, second_ref)
    sum_end(0, first_ref)

    for copy in early + late:
        copy.wait_send()
    for w in range(2):
        each(1, NI, lambda d: tile_copy(w, d, None).wait_send())
        own_forward(w, True).wait_send()
        each(1, NM, lambda d: slab_copy(w, d, None).wait_send())
        each(1, NM, lambda d: forward_copy(w, d, True).wait_send())
        each(0, NM, lambda n: pair_copy(w, n, True).wait_send())
        each(1, NM, lambda d: chip_copy(w, d, None).wait_send())
        each(1, NI, lambda d: lon_copy(w, d, None).wait_send())

    @pl.when(top)
    def _():
        for f in range(3):
            def sent(d):
                @pl.when(lon(d) < NG)
                def _():
                    row_copy(f, fy, d, None).wait_send()

            each(1, NI, sent)

    @pl.when(worker)
    def _():
        for f in range(3):
            each(1, NI, lambda d: turned_copy(f, d, None).wait_send())


def body(x_codes, x_scale, h_codes, h_scale, grad_out, land, partner, w_first, w_second):
    C, H, W = x_codes.shape
    NJ, NI = lax.axis_size("lat"), lax.axis_size("lon")
    CJ, CI, NM = C // NJ, C // NI, NJ // 2
    LA, CL, RB, N = up(3 * C, LANES), up(C, LANES), up(3 * CJ, PAD), H * W
    ROWS = NJ * RB
    cfg = {"C": C, "H": H, "NJ": NJ, "NI": NI, "factor": 1.0 / math.sqrt(NJ * H * NI * W)}
    sem = pltpu.SemaphoreType.DMA
    vm = pltpu.VMEM
    scratch = [
        vm((C * H, W), F32),
        vm((C, N), F32),
        vm((9, PAD, LANES), F32),
        vm((2, PAD, LANES), BF16),
        vm((2, NI, PAD, LANES), BF16),
        vm((2, RB, LA), BF16),
        vm((2, 2, NM, RB, LA), BF16),
        vm((LA, ROWS), BF16),
        vm((LA, 3 * C), BF16),
        vm((C, N + 2 * W), BF16),
        vm((C, N + 2 * W), BF16),
        vm((LA, N + 2 * W), BF16),
        vm((LA, N + 2 * W), BF16),
        vm((ROWS, N + W), BF16),
        vm((2, W, CL), BF16),
        vm((2, W, CL), BF16),
        vm((3, NI, PAD, W), BF16),
        vm((3, NI, PAD, 3 * W), BF16),
        vm((3, C, 3 * W), BF16),
        vm((ROWS, 3 * C), BF16),
        vm((LA, N + W), F32),
        vm((3, C, LA), F32),
        vm((2, 2, NM, RB, LA), F32),
        vm((2, NM, RB, LA), F32),
        vm((2, NM, RB, LA), SUM_TYPE),
        vm((2, NM, RB, LA), SUM_TYPE),
        vm((RB + PAD, LA), F32),
        vm((2, NI, PAD, LANES), F32),
        vm((2, NI, PAD, LANES), F32),
        sem((2, NI)), sem((2, NI)), sem((2, NM)), sem((2, NM)), sem((2, NM)), sem((2, NM)),
        sem((2, 12)), sem((2, 12)), sem((3, NI)), sem((3, NI)), sem((3, NI)), sem((3, NI)),
        sem((2, NM)), sem((2, NM)), sem((2, NM)), sem((2, NM)), sem((2, NI)), sem((2, NI)),
    ]
    grad_in, first, second = pl.pallas_call(
        functools.partial(kernel, cfg),
        out_shape=(
            jax.ShapeDtypeStruct((C * H, W), F32),
            jax.ShapeDtypeStruct((3, CJ, 3, CI), F32),
            jax.ShapeDtypeStruct((3, CJ, 3, CI), F32),
        ),
        in_specs=[pl.BlockSpec(memory_space=vm)] * 9,
        out_specs=[pl.BlockSpec(memory_space=vm)] * 3,
        scratch_shapes=scratch,
        compiler_params=pltpu.CompilerParams(
            collective_id=0, has_side_effects=True, vmem_limit_bytes=56 * 1024 * 1024
        ),
    )(x_codes, x_scale.T, h_codes, h_scale.T, grad_out, land, partner.reshape(NI, W),
      w_first.transpose(0, 2, 1, 3), w_second.transpose(0, 2, 1, 3))
    grad_in = grad_out.astype(F32) + grad_in.reshape(C, H, W)
    return (grad_in, first.transpose(0, 2, 1, 3), second.transpose(0, 2, 1, 3))


def solution(mesh):
    placed = (
        P(None, "lat", "lon"),
        P(None, "lat"),
        P(None, "lat", "lon"),
        P(None, "lat"),
        P(None, "lat", "lon"),
        P("lat", "lon"),
        P(),
        P(None, None, "lat", "lon"),
        P(None, None, "lat", "lon"),
    )
    return jax.shard_map(
        body,
        mesh=mesh,
        in_specs=placed,
        out_specs=(P(None, "lat", "lon"), P(None, None, "lat", "lon"), P(None, None, "lat", "lon")),
        check_vma=False,
    )
```

```python
import functools
import math

import jax
import jax.numpy as jnp
from jax import lax
from jax.experimental import pallas as pl
from jax.experimental.pallas import tpu as pltpu
from jax.sharding import PartitionSpec as P

MESH = pl.DeviceIdType.MESH
F32, BF16 = jnp.float32, jnp.bfloat16
PAD = 16
LANES = 128
SUM_TYPE = jnp.bfloat16
PARTS = 4
GRANT = 56 * 1024 * 1024


def up(value, unit):
    return -(-value // unit) * unit


def gelu_parts(h):
    k = math.sqrt(2.0 / math.pi)
    tanh_part = jnp.tanh(k * (h + 0.044715 * h * h * h))
    value = 0.5 * h * (1.0 + tanh_part)
    slope = 0.5 * (1.0 + tanh_part) + 0.5 * h * (1.0 - tanh_part * tanh_part) * k * (
        1.0 + 3.0 * 0.044715 * h * h
    )
    return (value, slope)


def dot(a, b):
    return lax.dot_general(a, b, (((1,), (0,)), ((), ())), preferred_element_type=F32)


def dot_nt(a, b):
    return lax.dot_general(a, b, (((1,), (1,)), ((), ())), preferred_element_type=F32)


def put(tiles, lane, source, source_lane, count, target_lane):
    shift = (target_lane - source_lane) % LANES
    moved = pltpu.roll(source, shift, 1) if shift else source
    tile, off = divmod(target_lane, LANES)
    keep = (lane >= off) & (lane < off + count)
    tiles[tile] = jnp.where(keep, moved, tiles[tile])
    over = off + count - LANES
    if over > 0:
        tiles[tile + 1] = jnp.where(lane < over, moved, tiles[tile + 1])


def put_wide(tiles, lane, sources, source_lane, count, target_lane):
    while count > 0:
        tile, off = divmod(source_lane, LANES)
        part = min(count, LANES - off)
        put(tiles, lane, sources[tile], off, part, target_lane)
        source_lane, target_lane, count = source_lane + part, target_lane + part, count - part


def kernel(
    cfg,
    x_hbm, xs_hbm, h_hbm, hs_hbm, g_hbm, land_hbm, partner_hbm, w0_hbm, w1_hbm,
    out_hbm, first_hbm, second_hbm,
    out_ref, first_ref, second_ref, x_ref,
    xs_ref, h_ref, hs_ref, g_ref, land_ref, partner_ref, w0_ref, w1_ref, in_s, out_s,
    cells, slope, wtmp, wown, wtile, wrow, wfull, wt, wp, fy, fh, sa, sx, gq, edge, edge_in,
    mrow, mout, mirr, spread, qs, nat, tap, tap_in, part, part_in, tot, small, small_in,
    st1_s, st1_r, st2_s, st2_r, fw_s, fw_r, ha_s, ha_r, mi_s, mi_r, mo_s, mo_r,
    r0_s, r0_r, r1_s, r1_r, r2_s, r2_r,
):
    C, H, NJ, NI = cfg["C"], cfg["H"], cfg["NJ"], cfg["NI"]
    W = LANES
    CJ, CI, NM, NG = C // NJ, C // NI, NJ // 2, C // PAD
    LA, CL, RB = up(3 * C, LANES), up(C, LANES), up(3 * (C // NJ), PAD)
    ROWS = NJ * RB
    N = H * W
    j, i = lax.axis_index("lat"), lax.axis_index("lon")
    k, m = lax.rem(j, 2), lax.div(j, 2)
    top = j == NJ - 1
    bottom = j == 0
    worker = top & (i < NG)

    def rcopy(src, dst, ss, rs, dj, di):
        return pltpu.make_async_remote_copy(
            src_ref=src, dst_ref=dst, send_sem=ss, recv_sem=rs,
            device_id={"lat": dj, "lon": di}, device_id_type=MESH,
        )

    def each(lo, hi, fn):
        lax.fori_loop(lo, hi, lambda d, c: (fn(d), c)[1], 0)

    def lon(d):
        return jnp.bitwise_xor(i, d)

    def lat(d):
        return jnp.bitwise_xor(j, d)

    def mate(d):
        return jnp.bitwise_xor(m, d)

    def beside(axis, place, d):
        return lax.rem(place + d + axis, axis)

    lon_order = [d for d in (9, 8, 11, 10, 7, 6, 15, 14, 5, 13, 4, 12, 3, 2, 1) if d < NI]
    lat_order = [d for d in (12, 13, 10, 11, 14, 15, 8, 9, 4, 5, 2, 3, 6, 7, 1) if d < NJ]
    mate_order = [d for d in (6, 5, 7, 4, 2, 1, 3) if d < NM]

    barrier = pltpu.get_barrier_semaphore()

    def greet(dj, di):
        pl.semaphore_signal(barrier, inc=1, device_id={"lat": dj, "lon": di}, device_id_type=MESH)

    for d in lon_order:
        greet(j, lon(d))
    for d in lat_order:
        greet(lat(d), i)
    for dj in (1, -1):
        for di in (1, -1):
            greet(beside(NJ, j, dj), beside(NI, i, di))
    loads = [
        pltpu.make_async_copy(src, dst, in_s.at[n])
        for n, (src, dst) in enumerate((
            (w1_hbm, w1_ref), (w0_hbm, w0_ref), (land_hbm, land_ref), (g_hbm, g_ref), (xs_hbm, xs_ref),
            (x_hbm, x_ref), (hs_hbm, hs_ref), (h_hbm, h_ref), (partner_hbm, partner_ref)))
    ]
    for load in loads:
        load.start()

    loads[0].wait()
    loads[1].wait()

    for w, ref in ((1, w1_ref), (0, w0_ref)):
        wtmp[...] = jnp.zeros(wtmp.shape, F32)
        for a in range(3):
            block = ref[a].astype(F32)
            for b in range(3):
                wtmp[3 * a + b, 0:CJ, 0:CI] = block[:, b, :]
        value = wtmp[0]
        for n in range(1, 9):
            value = value + pltpu.roll(wtmp[n], n * CI, 1)
        wown[w] = value.astype(BF16)

    def blocks(ref):
        cells[...] = ref[...].astype(F32).reshape(C * H, W)
        return [cells[pl.ds(r, C, stride=H), :] for r in range(H)]

    def ocean(r):
        return land_ref[r:r + 1, :].astype(F32)

    def slot(r):
        return pl.ds((r + 1) * W, W)

    lane = lax.broadcasted_iota(jnp.int32, (C, W), 1)
    center = pl.ds(C, C)

    def add_edges(packed, f, r, blk):
        spots = [f * 8 + r]
        if r == H - 1:
            spots.append(32 + f)
        if r == 0:
            spots.append(48 + f)
        for spot in spots:
            packed = jnp.where(lane == spot, pltpu.roll(blk, spot, 1) if spot else blk, packed)
            packed = jnp.where(lane == 64 + spot, pltpu.roll(blk, 65 + spot, 1), packed)
        return packed

    def turn_edges(phase, packed):
        if CL > C:
            packed = jnp.concatenate([packed, jnp.zeros((CL - C, W), F32)], axis=0)
        edge[phase] = jnp.transpose(packed).astype(BF16)

    for load in loads[2:6]:
        load.wait()
    scale = jnp.transpose(xs_ref[...])
    packed = jnp.zeros((C, W), F32)
    for r, blk in enumerate(blocks(g_ref)):
        value = blk * ocean(r)
        fy[:, slot(r)] = value.astype(BF16)
        packed = add_edges(packed, 0, r, value)
    for r, blk in enumerate(blocks(x_ref)):
        x = (blk * scale[:, r:r + 1]).astype(BF16)
        sx[center, slot(r)] = x
        packed = add_edges(packed, 2, r, x.astype(F32))

    pl.semaphore_wait(barrier, NI - 1 + NJ - 1 + 4)

    def tile_copy(w, d, other):
        return rcopy(wown.at[w], wtile.at[w, i if other is None else other],
                     st1_s.at[w, d], st1_r.at[w, d], j, lon(d))

    for d in lon_order:
        tile_copy(1, d, None).start()
    wtile[1, i] = wown[1]

    def row_copy(f, src, d, other):
        g = lon(d) if other is None else i
        return rcopy(src.at[pl.ds(pl.multiple_of(g * PAD, PAD), PAD), slot(H - 1)],
                     mrow.at[f, i if other is None else other], mi_s.at[f, d], mi_r.at[f, d], j, lon(d))

    def turned_copy(f, d, other):
        g = i if other is None else other
        return rcopy(mout.at[f, lon(d)], mirr.at[f, pl.ds(pl.multiple_of(g * PAD, PAD), PAD)],
                     mo_s.at[f, d], mo_r.at[f, d], j, lon(d))

    def mirror_send(f, src):
        @pl.when(top)
        def _():
            def step(d):
                @pl.when(lon(d) < NG)
                def _():
                    row_copy(f, src, d, None).start()

            each(1, NI, step)

            @pl.when(i < NG)
            def _():
                mrow[f, i] = src[pl.ds(pl.multiple_of(i * PAD, PAD), PAD), slot(H - 1)]

    def mirror_turn(f, src):
        @pl.when(worker)
        def _():
            each(1, NI, lambda d: row_copy(f, src, d, lon(d)).wait_recv())
            ncols = NI * W
            flip = (lax.broadcasted_iota(jnp.int32, (W, W), 0)
                    + lax.broadcasted_iota(jnp.int32, (W, W), 1)) == W - 1
            rev = dot(mrow[f].reshape(NI * PAD, W), jnp.where(flip, 1.0, 0.0).astype(BF16))
            tiles = [rev[(NI - 1 - v) * PAD:(NI - v) * PAD] for v in range(NI)]
            tlane = lax.broadcasted_iota(jnp.int32, (PAD, W), 1)
            where = partner_ref[pl.ds(i, 1), :] + lax.broadcasted_iota(jnp.int32, (1, W), 1) + i * W
            turn = (ncols - 1) - (where & (ncols - 1))
            turn = jnp.broadcast_to(turn, (PAD, W))

            def left(tiles, by):
                if by % W == 0:
                    return [tiles[(t + by // W) % NI] for t in range(NI)]
                moved = [pltpu.roll(tile, W - by, 1) for tile in tiles]
                return [jnp.where(tlane < W - by, moved[t], moved[(t + 1) % NI]) for t in range(NI)]

            for bit in range(ncols.bit_length() - 1):
                take = (turn & (1 << bit)) != 0
                tiles = [jnp.where(take, new, old) for new, old in zip(left(tiles, 1 << bit), tiles)]
            moved = [pltpu.roll(tile, 1, 1) for tile in tiles]
            before = [jnp.where(tlane == 0, moved[t - 1], moved[t]) for t in range(NI)]
            for b, group in enumerate((before, tiles, left(tiles, 1))):
                for t in range(NI):
                    mout[f, t, :, b * W:(b + 1) * W] = group[t].astype(BF16)
            mirr[f, pl.ds(pl.multiple_of(i * PAD, PAD), PAD), :] = mout[f, i]
            each(1, NI, lambda d: turned_copy(f, d, None).start())

    def mirror_wait(f):
        def step(d):
            @pl.when(lon(d) < NG)
            def _():
                turned_copy(f, d, lon(d)).wait_recv()

        each(1, NI, step)

    mirror_send(0, fy)
    mirror_send(1, sx.at[center])

    for load in loads[6:]:
        load.wait()
    scale = jnp.transpose(hs_ref[...])
    for r, blk in enumerate(blocks(h_ref)):
        h = blk * scale[:, r:r + 1]
        value, deriv = gelu_parts(h)
        act = (ocean(r) * value).astype(BF16)
        sa[center, slot(r)] = act
        slope[:, r * W:(r + 1) * W] = deriv
        packed = add_edges(packed, 1, r, act.astype(F32))
    turn_edges(0, packed)

    def halo_copies(phase, fields):
        out = []
        for f, field in enumerate(fields):
            s = 2 * f
            out.append(rcopy(field.at[:, slot(H - 1)], field.at[:, slot(-1)],
                             ha_s.at[phase, s], ha_r.at[phase, s], beside(NJ, j, 1), i))
            out.append(rcopy(field.at[:, slot(0)], field.at[:, slot(H)],
                             ha_s.at[phase, s + 1], ha_r.at[phase, s + 1], beside(NJ, j, -1), i))
        side = up(8 * len(fields), PAD)
        n = 6
        for di, base, target in ((1, 64, 0), (-1, 0, 64)):
            for dj, off, size in ((0, 0, side), (1, 32, PAD), (-1, 48, PAD)):
                out.append(rcopy(edge.at[phase, pl.ds(base + off, size)],
                                 edge_in.at[phase, pl.ds(target + off, size)],
                                 ha_s.at[phase, n], ha_r.at[phase, n],
                                 beside(NJ, j, dj), beside(NI, i, di)))
                n += 1
        return out

    early = halo_copies(0, (fy, sa.at[center], sx.at[center]))
    for copy in early:
        copy.start()
    for d in lon_order:
        tile_copy(0, d, None).start()
    wtile[0, i] = wown[0]

    at = lax.broadcasted_iota(jnp.int32, (ROWS, 1), 0)
    half, rest = lax.div(at, NM * RB), lax.rem(at, NM * RB)
    own = lax.rem(rest, RB)
    line = lax.div(own, CJ)
    target = line * C + (2 * lax.div(rest, RB) + half) * CJ + own - line * CJ
    target = jnp.where(own < 3 * CJ, target, -1)
    spread[...] = jnp.where(lax.broadcasted_iota(jnp.int32, (ROWS, 3 * C), 1) == target, 1.0, 0.0).astype(BF16)

    def make_slab(w):
        each(1, NI, lambda d: tile_copy(w, d, lon(d)).wait_recv())
        wlane = lax.broadcasted_iota(jnp.int32, (PAD, W), 1)
        tot[...] = jnp.zeros(tot.shape, F32)
        pieces = [wtile[w, s].astype(F32) for s in range(NI)]
        for a in range(3):
            tiles = [jnp.zeros((PAD, W), F32) for _ in range(LA // W)]
            for s in range(NI):
                for b in range(3):
                    put(tiles, wlane, pieces[s], (3 * a + b) * CI, CI, b * C + s * CI)
            for t, value in enumerate(tiles):
                tot[a * CJ:(a + 1) * CJ, t * W:(t + 1) * W] = value[:CJ]
        wrow[w] = tot[0:RB].astype(BF16)

    def slab_copy(w, d, other):
        return rcopy(wrow.at[w], wfull.at[w, k, m if other is None else other],
                     st2_s.at[w, d], st2_r.at[w, d], 2 * mate(d) + k, i)

    def forward_copy(w, d, mine):
        n = mate(d)
        return rcopy(wfull.at[w, k, n], wfull.at[w, k if mine else 1 - k, n],
                     fw_s.at[w, d], fw_r.at[w, d], j + 1 - 2 * k, i)

    def own_forward(w, mine):
        return rcopy(wrow.at[w], wfull.at[w, k if mine else 1 - k, m], fw_s.at[w, 0], fw_r.at[w, 0],
                     j + 1 - 2 * k, i)

    def send_slab(w):
        for d in mate_order:
            slab_copy(w, d, None).start()
        own_forward(w, True).start()
        wfull[w, k, m] = wrow[w]

    def pass_on(w):
        def step(d):
            slab_copy(w, d, mate(d)).wait_recv()
            forward_copy(w, d, True).start()

        each(1, NM, step)

    def have_weights(w):
        own_forward(w, False).wait_recv()
        each(1, NM, lambda d: forward_copy(w, d, False).wait_recv())
        wt[...] = jnp.transpose(wfull[w].reshape(ROWS, LA).astype(F32)).astype(BF16)

    def columns(got, f):
        result = []
        for base in (0, 64):
            start = base + f * 8
            value = jnp.where((lane >= 1) & (lane <= H), pltpu.roll(got, (1 - start) % W, 1), 0.0)
            lower = pltpu.roll(got, (-(base + 32 + f)) % W, 1)
            upper = pltpu.roll(got, (H + 1 - (base + 48 + f)) % W, 1)
            value = jnp.where((lane == 0) & jnp.logical_not(bottom), lower, value)
            value = jnp.where((lane == H + 1) & jnp.logical_not(top), upper, value)
            result.append(value)
        return result

    def turned_edges(phase):
        return jnp.transpose(edge_in[phase].astype(F32))[:C]

    def clear_ends(field):
        @pl.when(bottom)
        def _():
            field[:, slot(-1)] = jnp.zeros((C, W), BF16)

        @pl.when(top)
        def _():
            field[:, slot(H)] = jnp.zeros((C, W), BF16)

    def shifted(field, west, east):
        for r in range(-1, H + 1):
            blk = field[center, slot(r)].astype(F32)
            lower = jnp.where(lane == 0, pltpu.roll(west, (-(r + 1)) % W, 1), pltpu.roll(blk, 1, 1))
            upper = jnp.where(lane == W - 1, pltpu.roll(east, (W - 2 - r) % W, 1), pltpu.roll(blk, W - 1, 1))
            field[0:C, slot(r)] = lower.astype(BF16)
            field[2 * C:3 * C, slot(r)] = upper.astype(BF16)
        if LA > 3 * C:
            field[3 * C:LA, :] = jnp.zeros((LA - 3 * C, (H + 2) * W), BF16)

    def tap_rows(field, n, size):
        return jnp.concatenate([field[:, (2 - a) * W + n:(2 - a) * W + n + size] for a in range(3)], axis=0)

    def edge_rows(west, east):
        both = []
        for a in range(3):
            at_west = pltpu.roll(west, (a - 2) % W, 1)
            at_east = pltpu.roll(east, (H + a - 2) % W, 1)
            value = jnp.where(lane < H, at_west, jnp.where(lane < 2 * H, at_east, 0.0))
            both.append(value.astype(BF16))
        return jnp.concatenate(both, axis=0)

    def fold_rows(f):
        return jnp.concatenate([jnp.zeros((2 * C, 3 * W), BF16), mirr[f]], axis=0)

    step = min(2 * W, N)

    def tap_grad(w, grad, field):
        for a in range(3):
            nat[a] = dot_nt(grad[:, W:W + N], field[:, a * W:a * W + N])

    def tap_store(w):
        for a in range(3):
            for jj in range(NJ):
                tap[w, jj % 2, jj // 2, a * CJ:(a + 1) * CJ, :] = nat[a, jj * CJ:(jj + 1) * CJ, :]

    def add_fold(fold):
        for b in range(3):
            qs[C:2 * C, N - W:N] += fold[b * C:(b + 1) * C, b * W:(b + 1) * W]

    def shift_sum():
        first, last = qs[0:C, N:N + W], qs[2 * C:3 * C, N:N + W]
        result = []
        for r in range(H):
            at = slice(r * W, (r + 1) * W)
            left = jnp.where(lane == W - 1, pltpu.roll(first, (W - 1 - H - r) % W, 1),
                             pltpu.roll(qs[0:C, at], W - 1, 1))
            right = jnp.where(lane == 0, pltpu.roll(last, (-r) % W, 1), pltpu.roll(qs[2 * C:3 * C, at], 1, 1))
            result.append(qs[C:2 * C, at] + left + right)
        return result

    def pair_copy(w, n, mine):
        return rcopy(tap.at[w, 1 - k, n], tap_in.at[w, n], r0_s.at[w, n], r0_r.at[w, n], j + 1 - 2 * k, i)

    def chip_copy(w, d, other):
        return rcopy(part.at[w, mate(d)], part_in.at[w, m if other is None else other],
                     r1_s.at[w, d], r1_r.at[w, d], 2 * mate(d) + k, i)

    def lon_copy(w, d, other):
        return rcopy(small.at[w, lon(d)], small_in.at[w, i if other is None else other],
                     r2_s.at[w, d], r2_r.at[w, d], j, lon(d))

    def sum_start(w):
        for d in mate_order:
            pair_copy(w, mate(d), True).start()
        pair_copy(w, m, True).start()

    def sum_chips(w):
        def step(d):
            n = mate(d)
            pair_copy(w, n, False).wait_recv()
            part[w, n] = (tap[w, k, n] + tap_in[w, n]).astype(SUM_TYPE)
            chip_copy(w, d, None).start()

        for d in mate_order:
            step(d)
        pair_copy(w, m, False).wait_recv()

    def sum_lon(w):
        total = tap[w, k, m] + tap_in[w, m]
        for d in range(1, NM):
            chip_copy(w, d, mate(d)).wait_recv()
            total = total + part_in[w, mate(d)].astype(F32)
        tot[0:RB] = total
        slane = lax.broadcasted_iota(jnp.int32, (PAD, W), 1)
        sources = [[tot[a * CJ:a * CJ + PAD, t * W:(t + 1) * W] for t in range(LA // W)] for a in range(3)]
        for s in range(NI):
            tiles = [jnp.zeros((PAD, W), F32)]
            for a in range(3):
                for b in range(3):
                    put_wide(tiles, slane, sources[a], b * C + s * CI, CI, (3 * a + b) * CI)
            small[w, s] = tiles[0]
        small_in[w, i] = small[w, i]
        for d in lon_order:
            lon_copy(w, d, None).start()

    def sum_end(w, ref):
        each(1, NI, lambda d: lon_copy(w, d, lon(d)).wait_recv())
        total = small_in[w, 0]
        for s in range(1, NI):
            total = total + small_in[w, s]
        total = total * cfg["factor"]
        for a in range(3):
            for b in range(3):
                n = 3 * a + b
                moved = pltpu.roll(total, (-n * CI) % W, 1) if n else total
                ref[a, :, b, :] = moved[:CJ, :CI]

    make_slab(1)
    send_slab(1)
    mirror_turn(0, fy)
    mirror_turn(1, sx.at[center])
    for w in range(2):
        tap[w, :, :, 3 * CJ:RB, :] = jnp.zeros((2, NM, RB - 3 * CJ, LA), F32)

    for copy in early:
        copy.wait_recv()
    clear_ends(fy)
    clear_ends(sa.at[center])
    clear_ends(sx.at[center])
    got = turned_edges(0)
    west, east = columns(got, 0)
    for n in range(0, N, step):
        gq[:, n:n + step] = dot(spread[...], tap_rows(fy, n, step)).astype(BF16)
    gq[:, N:N + W] = dot(spread[...], edge_rows(west, east)).astype(BF16)
    west, east = columns(got, 1)
    shifted(sa, west, east)
    west, east = columns(got, 2)
    shifted(sx, west, east)
    tap_grad(1, fy, sa)
    pass_on(1)
    make_slab(0)
    send_slab(0)

    @pl.when(top)
    def _():
        mirror_wait(0)
        act = sa[center, slot(H - 1)]
        for b in range(3):
            place = lax.broadcasted_iota(jnp.int32, (C, LA), 1) == (
                lax.broadcasted_iota(jnp.int32, (C, LA), 0) + b * C)
            wide = lax.dot_general(act, jnp.where(place, 1.0, 0.0).astype(BF16), (((0,), (0,)), ((), ())),
                                   preferred_element_type=F32).astype(BF16)
            nat[2] += dot(mirr[0, :, b * W:(b + 1) * W], wide)
        mirror_wait(1)
        for b in range(3):
            sx[b * C:(b + 1) * C, slot(H)] = mirr[1, :, b * W:(b + 1) * W]

    tap_store(1)
    sum_start(1)
    have_weights(1)
    for n in range(0, N + W, step):
        size = min(step, N + W - n)
        qs[:, n:n + size] = dot(wt[...], gq[:, n:n + size])

    @pl.when(top)
    def _():
        add_fold(dot(wt[...], dot(spread[...], fold_rows(0)).astype(BF16)))

    for r, value in enumerate(shift_sum()):
        fh[:, slot(r)] = (value * ocean(r) * slope[:, r * W:(r + 1) * W]).astype(BF16)

    tap_grad(0, fh, sx)
    tap_store(0)
    sum_start(0)
    sum_chips(1)

    packed = jnp.zeros((C, W), F32)
    for r in range(H):
        packed = add_edges(packed, 0, r, fh[:, slot(r)].astype(F32))
    turn_edges(1, packed)
    late = halo_copies(1, (fh,))
    for copy in late:
        copy.start()
    mirror_send(2, fh)
    sum_chips(0)

    pass_on(0)
    mirror_turn(2, fh)
    have_weights(0)
    wp[...] = dot(wt[...], spread[...]).astype(BF16)
    for copy in late:
        copy.wait_recv()
    clear_ends(fh)
    west, east = columns(turned_edges(1), 0)
    for n in range(0, N, step):
        qs[:, n:n + step] = dot(wp[...], tap_rows(fh, n, step))
    qs[:, N:N + W] = dot(wp[...], edge_rows(west, east))

    sum_lon(1)
    sum_lon(0)

    @pl.when(top)
    def _():
        mirror_wait(2)
        add_fold(dot(wp[...], fold_rows(2)))

    cells[...] = g_ref[...].astype(F32).reshape(C * H, W)
    for r, value in enumerate(shift_sum()):
        at = pl.ds(r, C, stride=H)
        out_ref[at, :] = cells[at, :] + value
    results = [
        pltpu.make_async_copy(src, dst, out_s.at[n])
        for n, (src, dst) in enumerate(((out_ref, out_hbm), (second_ref, second_hbm), (first_ref, first_hbm)))
    ]
    results[0].start()

    for copy in early + late:
        copy.wait_send()
    for w in range(2):
        each(1, NI, lambda d: tile_copy(w, d, None).wait_send())
        own_forward(w, True).wait_send()
        each(1, NM, lambda d: slab_copy(w, d, None).wait_send())
        each(1, NM, lambda d: forward_copy(w, d, True).wait_send())
        each(0, NM, lambda n: pair_copy(w, n, True).wait_send())
        each(1, NM, lambda d: chip_copy(w, d, None).wait_send())

    @pl.when(top)
    def _():
        for f in range(3):
            def sent(d):
                @pl.when(lon(d) < NG)
                def _():
                    row_copy(f, fy, d, None).wait_send()

            each(1, NI, sent)

    @pl.when(worker)
    def _():
        for f in range(3):
            each(1, NI, lambda d: turned_copy(f, d, None).wait_send())

    sum_end(1, second_ref)
    results[1].start()
    sum_end(0, first_ref)
    results[2].start()
    for w in range(2):
        each(1, NI, lambda d: lon_copy(w, d, None).wait_send())
    for result in results:
        result.wait()


def hand_over(out_in, first_in, second_in, out_ref, first_ref, second_ref, out_mid, first_mid, second_mid, came, went):
    size = out_in.shape[0] // PARTS
    ways = [(out_in.at[pl.ds(n * size, size)], out_mid.at[pl.ds(n * size, size)], out_ref.at[pl.ds(n * size, size)])
            for n in range(PARTS)]
    ways += [(first_in, first_mid, first_ref), (second_in, second_mid, second_ref)]
    first = [pltpu.make_async_copy(a, b, came.at[n]) for n, (a, b, _) in enumerate(ways)]
    then = [pltpu.make_async_copy(b, c, went.at[n]) for n, (_, b, c) in enumerate(ways)]
    for copy in first:
        copy.start()
    for copy, following in zip(first, then):
        copy.wait()
        following.start()
    for copy in then:
        copy.wait()


def body(x_codes, x_scale, h_codes, h_scale, grad_out, land, partner, w_first, w_second):
    C, H, W = x_codes.shape
    NJ, NI = lax.axis_size("lat"), lax.axis_size("lon")
    CJ, CI, NM = C // NJ, C // NI, NJ // 2
    LA, CL, RB, N = up(3 * C, LANES), up(C, LANES), up(3 * CJ, PAD), H * W
    ROWS = NJ * RB
    cfg = {"C": C, "H": H, "NJ": NJ, "NI": NI, "factor": 1.0 / math.sqrt(NJ * H * NI * W)}
    sem = pltpu.SemaphoreType.DMA
    vm = pltpu.VMEM
    args = (x_codes, x_scale.T, h_codes, h_scale.T, grad_out, land, partner.reshape(NI, W),
            w_first.transpose(0, 2, 1, 3), w_second.transpose(0, 2, 1, 3))
    shapes = (
        jax.ShapeDtypeStruct((C * H, W), F32),
        jax.ShapeDtypeStruct((3, CJ, 3, CI), F32),
        jax.ShapeDtypeStruct((3, CJ, 3, CI), F32),
    )
    scratch = [vm(arg.shape, arg.dtype) for arg in shapes + args] + [
        sem((9,)), sem((3,)),
        vm((C * H, W), F32),
        vm((C, N), F32),
        vm((9, PAD, LANES), F32),
        vm((2, PAD, LANES), BF16),
        vm((2, NI, PAD, LANES), BF16),
        vm((2, RB, LA), BF16),
        vm((2, 2, NM, RB, LA), BF16),
        vm((LA, ROWS), BF16),
        vm((LA, 3 * C), BF16),
        vm((C, N + 2 * W), BF16),
        vm((C, N + 2 * W), BF16),
        vm((LA, N + 2 * W), BF16),
        vm((LA, N + 2 * W), BF16),
        vm((ROWS, N + W), BF16),
        vm((2, W, CL), BF16),
        vm((2, W, CL), BF16),
        vm((3, NI, PAD, W), BF16),
        vm((3, NI, PAD, 3 * W), BF16),
        vm((3, C, 3 * W), BF16),
        vm((ROWS, 3 * C), BF16),
        vm((LA, N + W), F32),
        vm((3, C, LA), F32),
        vm((2, 2, NM, RB, LA), F32),
        vm((2, NM, RB, LA), F32),
        vm((2, NM, RB, LA), SUM_TYPE),
        vm((2, NM, RB, LA), SUM_TYPE),
        vm((RB + PAD, LA), F32),
        vm((2, NI, PAD, LANES), F32),
        vm((2, NI, PAD, LANES), F32),
        sem((2, NI)), sem((2, NI)), sem((2, NM)), sem((2, NM)), sem((2, NM)), sem((2, NM)),
        sem((2, 12)), sem((2, 12)), sem((3, NI)), sem((3, NI)), sem((3, NI)), sem((3, NI)),
        sem((2, NM)), sem((2, NM)), sem((2, NM)), sem((2, NM)), sem((2, NI)), sem((2, NI)),
    ]
    results = pl.pallas_call(
        functools.partial(kernel, cfg),
        out_shape=shapes,
        in_specs=[pl.BlockSpec(memory_space=pl.ANY)] * 9,
        out_specs=[pl.BlockSpec(memory_space=pl.ANY)] * 3,
        scratch_shapes=scratch,
        compiler_params=pltpu.CompilerParams(
            collective_id=0, has_side_effects=True, vmem_limit_bytes=GRANT
        ),
    )(*args)
    grad_in, first, second = pl.pallas_call(
        hand_over,
        out_shape=shapes,
        in_specs=[pl.BlockSpec(memory_space=pl.ANY)] * 3,
        out_specs=[pl.BlockSpec(memory_space=pl.ANY)] * 3,
        scratch_shapes=[vm(arg.shape, arg.dtype) for arg in shapes] + [sem((PARTS + 2,))] * 2,
        compiler_params=pltpu.CompilerParams(vmem_limit_bytes=GRANT),
    )(*results)
    return (grad_in.reshape(C, H, W), first.transpose(0, 2, 1, 3), second.transpose(0, 2, 1, 3))


def solution(mesh):
    placed = (
        P(None, "lat", "lon"),
        P(None, "lat"),
        P(None, "lat", "lon"),
        P(None, "lat"),
        P(None, "lat", "lon"),
        P("lat", "lon"),
        P(),
        P(None, None, "lat", "lon"),
        P(None, None, "lat", "lon"),
    )
    return jax.shard_map(
        body,
        mesh=mesh,
        in_specs=placed,
        out_specs=(P(None, "lat", "lon"), P(None, None, "lat", "lon"), P(None, None, "lat", "lon")),
        check_vma=False,
    )
```

```python
import functools
import math

import jax
import jax.numpy as jnp
from jax import lax
from jax.experimental import pallas as pl
from jax.experimental.pallas import tpu as pltpu
from jax.sharding import PartitionSpec as P

MESH = pl.DeviceIdType.MESH
F32, BF16 = jnp.float32, jnp.bfloat16
PAD = 16
LANES = 128
SUM_TYPE = jnp.bfloat16
PARTS = 4
GRANT = 56 * 1024 * 1024


def up(value, unit):
    return -(-value // unit) * unit


def gelu_parts(h):
    k = math.sqrt(2.0 / math.pi)
    tanh_part = jnp.tanh(k * (h + 0.044715 * h * h * h))
    value = 0.5 * h * (1.0 + tanh_part)
    slope = 0.5 * (1.0 + tanh_part) + 0.5 * h * (1.0 - tanh_part * tanh_part) * k * (
        1.0 + 3.0 * 0.044715 * h * h
    )
    return (value, slope)


def dot(a, b):
    return lax.dot_general(a, b, (((1,), (0,)), ((), ())), preferred_element_type=F32)


def dot_nt(a, b):
    return lax.dot_general(a, b, (((1,), (1,)), ((), ())), preferred_element_type=F32)


def put(tiles, lane, source, source_lane, count, target_lane):
    shift = (target_lane - source_lane) % LANES
    moved = pltpu.roll(source, shift, 1) if shift else source
    tile, off = divmod(target_lane, LANES)
    keep = (lane >= off) & (lane < off + count)
    tiles[tile] = jnp.where(keep, moved, tiles[tile])
    over = off + count - LANES
    if over > 0:
        tiles[tile + 1] = jnp.where(lane < over, moved, tiles[tile + 1])


def put_wide(tiles, lane, sources, source_lane, count, target_lane):
    while count > 0:
        tile, off = divmod(source_lane, LANES)
        part = min(count, LANES - off)
        put(tiles, lane, sources[tile], off, part, target_lane)
        source_lane, target_lane, count = source_lane + part, target_lane + part, count - part


def kernel(
    cfg,
    x_hbm, xs_hbm, h_hbm, hs_hbm, g_hbm, land_hbm, partner_hbm, w0_hbm, w1_hbm,
    out_hbm, first_hbm, second_hbm,
    out_ref, first_ref, second_ref, x_ref,
    xs_ref, h_ref, hs_ref, g_ref, land_ref, partner_ref, w0_ref, w1_ref, in_s, out_s,
    cells, slope, wtmp, wown, wtile, wrow, wfull, wt, wp, fh, act, sg, sx, gq, edge, edge_in,
    mrow, mout, mirr, gqm, spread, qs, nat, tap, given, tap_in, part, part_in, tot, small, small_in,
    turned, tapz, givenz, tapz_in, partz, partz_in, smallz, smallz_in,
    st1_s, st1_r, st2_s, st2_r, fw_s, fw_r, ha_s, ha_r, mi_s, mi_r, mo_s, mo_r,
    r0_s, r0_r, r1_s, r1_r, r2_s, r2_r, z0_s, z0_r, z1_s, z1_r, z2_s, z2_r,
):
    C, H, NJ, NI = cfg["C"], cfg["H"], cfg["NJ"], cfg["NI"]
    W = LANES
    CJ, CI, NM, NG = C // NJ, C // NI, NJ // 2, C // PAD
    LA, CL, RB = up(3 * C, LANES), up(C, LANES), up(3 * (C // NJ), PAD)
    ROWS = NJ * RB
    N = H * W
    j, i = lax.axis_index("lat"), lax.axis_index("lon")
    k, m = lax.rem(j, 2), lax.div(j, 2)
    top = j == NJ - 1
    bottom = j == 0
    worker = top & (i < NG)

    def rcopy(src, dst, ss, rs, dj, di):
        return pltpu.make_async_remote_copy(
            src_ref=src, dst_ref=dst, send_sem=ss, recv_sem=rs,
            device_id={"lat": dj, "lon": di}, device_id_type=MESH,
        )

    def each(lo, hi, fn):
        lax.fori_loop(lo, hi, lambda d, c: (fn(d), c)[1], 0)

    def lon(d):
        return jnp.bitwise_xor(i, d)

    def lat(d):
        return jnp.bitwise_xor(j, d)

    def mate(d):
        return jnp.bitwise_xor(m, d)

    def beside(axis, place, d):
        return lax.rem(place + d + axis, axis)

    lon_order = [d for d in (9, 8, 11, 10, 7, 6, 15, 14, 5, 13, 4, 12, 3, 2, 1) if d < NI]
    lat_order = [d for d in (12, 13, 10, 11, 14, 15, 8, 9, 4, 5, 2, 3, 6, 7, 1) if d < NJ]
    mate_order = [d for d in (6, 5, 7, 4, 2, 1, 3) if d < NM]

    barrier = pltpu.get_barrier_semaphore()

    def greet(dj, di):
        pl.semaphore_signal(barrier, inc=1, device_id={"lat": dj, "lon": di}, device_id_type=MESH)

    for d in lon_order:
        greet(j, lon(d))
    for d in lat_order:
        greet(lat(d), i)
    for dj in (1, -1):
        for di in (1, -1):
            greet(beside(NJ, j, dj), beside(NI, i, di))
    loads = [
        pltpu.make_async_copy(src, dst, in_s.at[n])
        for n, (src, dst) in enumerate((
            (w1_hbm, w1_ref), (w0_hbm, w0_ref), (land_hbm, land_ref), (g_hbm, g_ref), (xs_hbm, xs_ref),
            (x_hbm, x_ref), (hs_hbm, hs_ref), (h_hbm, h_ref), (partner_hbm, partner_ref)))
    ]
    for load in loads:
        load.start()

    loads[0].wait()

    def make_tile(ref):
        wtmp[...] = jnp.zeros(wtmp.shape, F32)
        for a in range(3):
            block = ref[a].astype(F32)
            for b in range(3):
                wtmp[3 * a + b, 0:CJ, 0:CI] = block[:, b, :]
        value = wtmp[0]
        for n in range(1, 9):
            value = value + pltpu.roll(wtmp[n], n * CI, 1)
        return value

    wown[1] = make_tile(w1_ref).astype(BF16)

    def blocks(ref):
        cells[...] = ref[...].astype(F32).reshape(C * H, W)
        return [cells[pl.ds(r, C, stride=H), :] for r in range(H)]

    def ocean(r):
        return land_ref[r:r + 1, :].astype(F32)

    def slot(r):
        return pl.ds((r + 1) * W, W)

    lane = lax.broadcasted_iota(jnp.int32, (C, W), 1)
    center = pl.ds(C, C)
    fy = sg.at[center]

    def add_edges(packed, f, r, blk):
        spots = [f * 8 + r]
        if r == H - 1:
            spots.append(32 + f)
        if r == 0:
            spots.append(48 + f)
        for spot in spots:
            packed = jnp.where(lane == spot, pltpu.roll(blk, spot, 1) if spot else blk, packed)
            packed = jnp.where(lane == 64 + spot, pltpu.roll(blk, 65 + spot, 1), packed)
        return packed

    def turn_edges(phase, packed):
        if CL > C:
            packed = jnp.concatenate([packed, jnp.zeros((CL - C, W), F32)], axis=0)
        edge[phase] = jnp.transpose(packed).astype(BF16)

    for load in loads[2:6]:
        load.wait()
    scale = jnp.transpose(xs_ref[...])
    packed = jnp.zeros((C, W), F32)
    for r, blk in enumerate(blocks(g_ref)):
        value = blk * ocean(r)
        fy[:, slot(r)] = value.astype(BF16)
        packed = add_edges(packed, 0, r, value)
    for r, blk in enumerate(blocks(x_ref)):
        x = (blk * scale[:, r:r + 1]).astype(BF16)
        sx[center, slot(r)] = x
        packed = add_edges(packed, 1, r, x.astype(F32))

    pl.semaphore_wait(barrier, NI - 1 + NJ - 1 + 4)

    def tile_copy(w, d, other):
        return rcopy(wown.at[w], wtile.at[w, i if other is None else other],
                     st1_s.at[w, d], st1_r.at[w, d], j, lon(d))

    for d in lon_order:
        tile_copy(1, d, None).start()
    wtile[1, i] = wown[1]
    def row_copy(phase, src, d, other):
        g = lon(d) if other is None else i
        return rcopy(src.at[pl.ds(pl.multiple_of(g * PAD, PAD), PAD), slot(H - 1)],
                     mrow.at[phase, i if other is None else other],
                     mi_s.at[phase, d], mi_r.at[phase, d], j, lon(d))

    def turned_copy(phase, d, other):
        return rcopy(mout.at[phase, lon(d)], mirr.at[phase, i if other is None else other],
                     mo_s.at[phase, d], mo_r.at[phase, d], j, lon(d))

    def mirror_send(phase, src):
        @pl.when(top)
        def _():
            for d in lon_order:
                @pl.when(lon(d) < NG)
                def _():
                    row_copy(phase, src, d, None).start()

            @pl.when(i < NG)
            def _():
                mrow[phase, i] = src[pl.ds(pl.multiple_of(i * PAD, PAD), PAD), slot(H - 1)]

    def mirror_turn(phase, src):
        @pl.when(worker)
        def _():
            ncols = NI * W
            flip = (lax.broadcasted_iota(jnp.int32, (W, W), 0)
                    + lax.broadcasted_iota(jnp.int32, (W, W), 1)) == W - 1
            flip = jnp.where(flip, 1.0, 0.0).astype(BF16)
            tlane = lax.broadcasted_iota(jnp.int32, (PAD, W), 1)
            where = partner_ref[pl.ds(i, 1), :] + lax.broadcasted_iota(jnp.int32, (1, W), 1) + i * W
            turn = (ncols - 1) - (where & (ncols - 1))
            turn = jnp.broadcast_to(turn, (PAD, W))

            def left(tiles, by):
                if by % W == 0:
                    return [tiles[(t + by // W) % NI] for t in range(NI)]
                moved = [pltpu.roll(tile, W - by, 1) for tile in tiles]
                return [jnp.where(tlane < W - by, moved[t], moved[(t + 1) % NI]) for t in range(NI)]

            each(1, NI, lambda d: row_copy(phase, src, d, lon(d)).wait_recv())
            rev = dot(mrow[phase].reshape(NI * PAD, W), flip)
            tiles = [rev[(NI - 1 - v) * PAD:(NI - v) * PAD] for v in range(NI)]
            for bit in range(ncols.bit_length() - 1):
                take = (turn & (1 << bit)) != 0
                tiles = [jnp.where(take, new, old) for new, old in zip(left(tiles, 1 << bit), tiles)]
            for t in range(NI):
                before, after = pltpu.roll(tiles[t - 1], 1, 1), pltpu.roll(tiles[(t + 1) % NI], 1, 1)
                mout[phase, t, 0] = tiles[t].astype(BF16)
                mout[phase, t, 1] = jnp.where(tlane == 0, before, after).astype(BF16)
            mirr[phase, i] = mout[phase, i]
            for d in lon_order:
                turned_copy(phase, d, None).start()

    def mirror_wait(phase):
        def step(d):
            @pl.when(lon(d) < NG)
            def _():
                turned_copy(phase, d, lon(d)).wait_recv()

        each(1, NI, step)

    def mirrored(phase):
        block = mirr[phase, :, 0].reshape(C, W).astype(F32)
        edges = mirr[phase, :, 1].reshape(C, W).astype(F32)
        before = jnp.where(lane == 0, edges, pltpu.roll(block, 1, 1))
        after = jnp.where(lane == W - 1, pltpu.roll(edges, W - 2, 1), pltpu.roll(block, W - 1, 1))
        return jnp.concatenate([before, block, after], axis=1).astype(BF16)

    mirror_send(0, fy)
    loads[1].wait()
    wown[0] = make_tile(w0_ref).astype(BF16)

    for load in loads[6:]:
        load.wait()
    scale = jnp.transpose(hs_ref[...])
    for r, blk in enumerate(blocks(h_ref)):
        h = blk * scale[:, r:r + 1]
        value, deriv = gelu_parts(h)
        act[:, r * W:(r + 1) * W] = (ocean(r) * value).astype(BF16)
        slope[:, r * W:(r + 1) * W] = deriv
    turn_edges(0, packed)

    def halo_copies(phase, fields):
        north, south = jnp.logical_not(top), jnp.logical_not(bottom)
        out = []
        for f, field in enumerate(fields):
            s = 2 * f
            out.append((rcopy(field.at[:, slot(H - 1)], field.at[:, slot(-1)],
                              ha_s.at[phase, s], ha_r.at[phase, s], beside(NJ, j, 1), i), north, south))
            out.append((rcopy(field.at[:, slot(0)], field.at[:, slot(H)],
                              ha_s.at[phase, s + 1], ha_r.at[phase, s + 1], beside(NJ, j, -1), i), south, north))
        side = up(8 * len(fields), PAD)
        n = 6
        for di, base, target in ((1, 64, 0), (-1, 0, 64)):
            for dj, off, size in ((0, 0, side), (1, 32, PAD), (-1, 48, PAD)):
                sent, comes = {0: (None, None), 1: (north, south), -1: (south, north)}[dj]
                out.append((rcopy(edge.at[phase, pl.ds(base + off, size)],
                                  edge_in.at[phase, pl.ds(target + off, size)],
                                  ha_s.at[phase, n], ha_r.at[phase, n],
                                  beside(NJ, j, dj), beside(NI, i, di)), sent, comes))
                n += 1
        return out

    def only(condition, fn):
        if condition is None:
            fn()
        else:
            pl.when(condition)(fn)

    def halo_start(copies):
        for copy, sent, _ in copies:
            only(sent, copy.start)

    def halo_wait(copies):
        for copy, _, comes in copies:
            only(comes, copy.wait_recv)

    def halo_sent(copies):
        for copy, sent, _ in copies:
            only(sent, copy.wait_send)

    early = halo_copies(0, (fy, sx.at[center]))
    halo_start(early)

    mirror_send(2, sx.at[center])
    at = lax.broadcasted_iota(jnp.int32, (ROWS, 1), 0)
    half, rest = lax.div(at, NM * RB), lax.rem(at, NM * RB)
    own = lax.rem(rest, RB)
    line = lax.div(own, CJ)
    target = line * C + (2 * lax.div(rest, RB) + half) * CJ + own - line * CJ
    target = jnp.where(own < 3 * CJ, target, -1)
    spread[...] = jnp.where(lax.broadcasted_iota(jnp.int32, (ROWS, 3 * C), 1) == target, 1.0, 0.0).astype(BF16)

    def make_slab(w):
        each(1, NI, lambda d: tile_copy(w, d, lon(d)).wait_recv())
        wlane = lax.broadcasted_iota(jnp.int32, (PAD, W), 1)
        tot[...] = jnp.zeros(tot.shape, F32)
        pieces = [wtile[w, s].astype(F32) for s in range(NI)]
        for a in range(3):
            tiles = [jnp.zeros((PAD, W), F32) for _ in range(LA // W)]
            for s in range(NI):
                for b in range(3):
                    put(tiles, wlane, pieces[s], (3 * a + b) * CI, CI, b * C + s * CI)
            for t, value in enumerate(tiles):
                tot[a * CJ:(a + 1) * CJ, t * W:(t + 1) * W] = value[:CJ]
        wrow[w] = tot[0:RB].astype(BF16)

    def slab_copy(w, d, other):
        return rcopy(wrow.at[w], wfull.at[w, k, m if other is None else other],
                     st2_s.at[w, d], st2_r.at[w, d], 2 * mate(d) + k, i)

    def forward_copy(w, d, mine):
        n = mate(d)
        return rcopy(wfull.at[w, k, n], wfull.at[w, k if mine else 1 - k, n],
                     fw_s.at[w, d], fw_r.at[w, d], j + 1 - 2 * k, i)

    def own_forward(w, mine):
        return rcopy(wrow.at[w], wfull.at[w, k if mine else 1 - k, m], fw_s.at[w, 0], fw_r.at[w, 0],
                     j + 1 - 2 * k, i)

    def send_slab(w):
        for d in mate_order:
            slab_copy(w, d, None).start()
        own_forward(w, True).start()
        wfull[w, k, m] = wrow[w]

    def pass_on(w):
        def step(d):
            slab_copy(w, d, mate(d)).wait_recv()
            forward_copy(w, d, True).start()

        each(1, NM, step)

    def have_weights(w):
        own_forward(w, False).wait_recv()
        each(1, NM, lambda d: forward_copy(w, d, False).wait_recv())
        wt[...] = jnp.transpose(wfull[w].reshape(ROWS, LA).astype(F32)).astype(BF16)

    def columns(got, f):
        result = []
        for base in (0, 64):
            start = base + f * 8
            value = jnp.where((lane >= 1) & (lane <= H), pltpu.roll(got, (1 - start) % W, 1), 0.0)
            lower = pltpu.roll(got, (-(base + 32 + f)) % W, 1)
            upper = pltpu.roll(got, (H + 1 - (base + 48 + f)) % W, 1)
            value = jnp.where((lane == 0) & jnp.logical_not(bottom), lower, value)
            value = jnp.where((lane == H + 1) & jnp.logical_not(top), upper, value)
            result.append(value)
        return result

    def turned_edges(phase):
        return jnp.transpose(edge_in[phase].astype(F32))[:C]

    def clear_ends(field):
        @pl.when(bottom)
        def _():
            field[:, slot(-1)] = jnp.zeros((C, W), BF16)

        @pl.when(top)
        def _():
            field[:, slot(H)] = jnp.zeros((C, W), BF16)

    def shifted(field, west, east):
        for r in range(-1, H + 1):
            blk = field[center, slot(r)].astype(F32)
            lower = jnp.where(lane == 0, pltpu.roll(west, (-(r + 1)) % W, 1), pltpu.roll(blk, 1, 1))
            upper = jnp.where(lane == W - 1, pltpu.roll(east, (W - 2 - r) % W, 1), pltpu.roll(blk, W - 1, 1))
            field[0:C, slot(r)] = lower.astype(BF16)
            field[2 * C:3 * C, slot(r)] = upper.astype(BF16)
        if LA > 3 * C:
            field[3 * C:LA, :] = jnp.zeros((LA - 3 * C, (H + 2) * W), BF16)

    def tap_rows(field, n, size):
        return jnp.concatenate([field[:, (2 - a) * W + n:(2 - a) * W + n + size] for a in range(3)], axis=0)

    def edge_rows(west, east):
        both = []
        for a in range(3):
            at_west = pltpu.roll(west, (a - 2) % W, 1)
            at_east = pltpu.roll(east, (H + a - 2) % W, 1)
            value = jnp.where(lane < H, at_west, jnp.where(lane < 2 * H, at_east, 0.0))
            both.append(value.astype(BF16))
        return jnp.concatenate(both, axis=0)

    def fold_rows(mirror):
        return jnp.concatenate([jnp.zeros((2 * C, 3 * W), BF16), mirror], axis=0)

    step = min(2 * W, N)

    def tap_grad(grad, field):
        for a in range(3):
            nat[a * C:(a + 1) * C, :] = dot_nt(grad[:, W:W + N], field[:, a * W:a * W + N])

    def tap_store():
        for a in range(3):
            for jj in range(NJ):
                tap[jj % 2, jj // 2, a * CJ:(a + 1) * CJ, :] = nat[a * C + jj * CJ:a * C + (jj + 1) * CJ, :]

    def side_store():
        for a in range(3):
            for s in range(NI):
                tapz[s, a * CI:(a + 1) * CI, :] = nat[a * C + s * CI:a * C + (s + 1) * CI, :]

    def add_fold(fold):
        for b in range(3):
            qs[C:2 * C, N - W:N] += fold[b * C:(b + 1) * C, b * W:(b + 1) * W]

    def shift_sum():
        first, last = qs[0:C, N:N + W], qs[2 * C:3 * C, N:N + W]
        result = []
        for r in range(H):
            at = slice(r * W, (r + 1) * W)
            left = jnp.where(lane == W - 1, pltpu.roll(first, (W - 1 - H - r) % W, 1),
                             pltpu.roll(qs[0:C, at], W - 1, 1))
            right = jnp.where(lane == 0, pltpu.roll(last, (-r) % W, 1), pltpu.roll(qs[2 * C:3 * C, at], 1, 1))
            result.append(qs[C:2 * C, at] + left + right)
        return result

    def pair_copy(n):
        return rcopy(given.at[n], tap_in.at[n], r0_s.at[n], r0_r.at[n], j + 1 - 2 * k, i)

    def chip_copy(d, other):
        return rcopy(part.at[mate(d)], part_in.at[m if other is None else other],
                     r1_s.at[d], r1_r.at[d], 2 * mate(d) + k, i)

    def lon_copy(d, other):
        return rcopy(small.at[lon(d)], small_in.at[i if other is None else other], r2_s.at[d], r2_r.at[d], j, lon(d))

    def sum_start():
        given[...] = tap[1 - k].astype(SUM_TYPE)
        for d in mate_order:
            pair_copy(mate(d)).start()
        pair_copy(m).start()

    def sum_chips():
        for d in mate_order:
            n = mate(d)
            pair_copy(n).wait_recv()
            part[n] = (tap[k, n] + tap_in[n].astype(F32)).astype(SUM_TYPE)
            chip_copy(d, None).start()
        pair_copy(m).wait_recv()

    def sum_lon():
        total = tap[k, m] + tap_in[m].astype(F32)
        for d in range(1, NM):
            chip_copy(d, mate(d)).wait_recv()
            total = total + part_in[mate(d)].astype(F32)
        tot[0:RB] = total
        slane = lax.broadcasted_iota(jnp.int32, (PAD, W), 1)
        sources = [[tot[a * CJ:a * CJ + PAD, t * W:(t + 1) * W] for t in range(LA // W)] for a in range(3)]
        for s in range(NI):
            tiles = [jnp.zeros((PAD, W), F32)]
            for a in range(3):
                for b in range(3):
                    put_wide(tiles, slane, sources[a], b * C + s * CI, CI, (3 * a + b) * CI)
            small[s] = tiles[0]
        small_in[i] = small[i]
        for d in lon_order:
            lon_copy(d, None).start()

    def sum_end():
        each(1, NI, lambda d: lon_copy(d, lon(d)).wait_recv())
        total = small_in[0]
        for s in range(1, NI):
            total = total + small_in[s]
        total = total * cfg["factor"]
        for a in range(3):
            for b in range(3):
                n = 3 * a + b
                moved = pltpu.roll(total, (-n * CI) % W, 1) if n else total
                first_ref[a, :, b, :] = moved[:CJ, :CI]

    HR = RB // 2
    mine = pl.ds(pl.multiple_of(k * HR, HR), HR)
    others = pl.ds(pl.multiple_of((1 - k) * HR, HR), HR)

    def side_pair():
        return rcopy(givenz, tapz_in, z0_s, z0_r, j + 1 - 2 * k, i)

    def side_lon(d, other):
        return rcopy(partz.at[lon(d)], partz_in.at[i if other is None else other], z1_s.at[d], z1_r.at[d], j, lon(d))

    def side_lat(d, other):
        return rcopy(smallz.at[lat(d)], smallz_in.at[j if other is None else other], z2_s.at[d], z2_r.at[d], lat(d), i)

    def side_start():
        givenz[...] = tapz[:, others].astype(SUM_TYPE)
        side_pair().start()

    def side_sum_lon():
        side_pair().wait_recv()
        for s in range(NI):
            partz[s] = (tapz[s, mine] + tapz_in[s].astype(F32)).astype(SUM_TYPE)
        for d in lon_order:
            side_lon(d, None).start()

    def side_sum_lat():
        total = tapz[i, mine] + tapz_in[i].astype(F32)
        for d in range(1, NI):
            side_lon(d, lon(d)).wait_recv()
            total = total + partz_in[lon(d)].astype(F32)
        slane = lax.broadcasted_iota(jnp.int32, (HR, W), 1)
        sources = [total[:, t * W:(t + 1) * W] for t in range(LA // W)]
        for s in range(NJ):
            tiles = [jnp.zeros((HR, W), F32)]
            for a in range(3):
                put_wide(tiles, slane, sources, a * C + s * CJ, CJ, a * CJ)
            smallz[s] = tiles[0]
        smallz_in[j] = smallz[j]
        for d in lat_order:
            side_lat(d, None).start()

    def side_end():
        each(1, NJ, lambda d: side_lat(d, lat(d)).wait_recv())
        halves = []
        for h in range(2):
            total = smallz_in[h]
            for s in range(h + 2, NJ, 2):
                total = total + smallz_in[s]
            halves.append(total)
        total = jnp.concatenate(halves + [jnp.zeros((W - RB, W), F32)], axis=0) * cfg["factor"]
        turned[...] = jnp.transpose(total)
        for b in range(3):
            block = turned[(2 - b) * CJ:(3 - b) * CJ, :]
            for a in range(3):
                moved = pltpu.roll(block, (-a * CI) % W, 1) if a else block
                second_ref[a, :, b, :] = moved[:, :CI]

    make_slab(1)
    send_slab(1)
    for d in lon_order:
        tile_copy(0, d, None).start()
    wtile[0, i] = wown[0]
    mirror_turn(0, fy)
    tap[:, :, 3 * CJ:RB, :] = jnp.zeros((2, NM, RB - 3 * CJ, LA), F32)
    tapz[:, 3 * CI:RB, :] = jnp.zeros((NI, RB - 3 * CI, LA), F32)

    halo_wait(early)
    clear_ends(fy)
    clear_ends(sx.at[center])
    got = turned_edges(0)
    west, east = columns(got, 0)
    for n in range(0, N, step):
        gq[:, n:n + step] = dot(spread[...], tap_rows(fy, n, step)).astype(BF16)
    gq[:, N:N + W] = dot(spread[...], edge_rows(west, east)).astype(BF16)
    mirror_turn(2, sx.at[center])
    shifted(sg, west, east)
    west, east = columns(got, 1)
    shifted(sx, west, east)
    for a in range(3):
        nat[a * C:(a + 1) * C, :] = dot_nt(act[...], sg[:, (2 - a) * W:(2 - a) * W + N])
    pass_on(1)
    make_slab(0)
    send_slab(0)
    side_store()
    @pl.when(top)
    def _():
        mirror_wait(0)
        mirror = mirrored(0)
        stacked = jnp.concatenate([mirror[:, 2 * W:3 * W], mirror[:, W:2 * W], mirror[:, 0:W],
                                   jnp.zeros((LA - 3 * C, W), BF16)], axis=0)
        nat[0:C, :] = dot_nt(act[:, N - W:N], stacked)
        for s in range(NI):
            tapz[s, 2 * CI:3 * CI, :] += nat[s * CI:(s + 1) * CI, :]
        gqm[...] = dot(spread[...], fold_rows(mirror)).astype(BF16)

    side_start()
    have_weights(1)
    for n in range(0, N + W, step):
        size = min(step, N + W - n)
        qs[:, n:n + size] = dot(wt[...], gq[:, n:n + size])

    @pl.when(top)
    def _():
        add_fold(dot(wt[...], gqm[...]))
        mirror_wait(2)
        north = mirrored(2)
        for b in range(3):
            sx[b * C:(b + 1) * C, slot(H)] = north[:, b * W:(b + 1) * W]

    side_sum_lon()
    for r, value in enumerate(shift_sum()):
        fh[:, slot(r)] = (value * ocean(r) * slope[:, r * W:(r + 1) * W]).astype(BF16)

    mirror_send(1, fh)
    tap_grad(fh, sx)
    tap_store()
    sum_start()
    packed = jnp.zeros((C, W), F32)
    for r in range(H):
        packed = add_edges(packed, 0, r, fh[:, slot(r)].astype(F32))
    turn_edges(1, packed)
    late = halo_copies(1, (fh,))
    halo_start(late)
    sum_chips()


    pass_on(0)
    have_weights(0)
    wp[...] = dot(wt[...], spread[...]).astype(BF16)
    mirror_turn(1, fh)
    side_sum_lat()
    sum_lon()

    halo_wait(late)
    clear_ends(fh)
    west, east = columns(turned_edges(1), 0)
    for n in range(0, N, step):
        qs[:, n:n + step] = dot(wp[...], tap_rows(fh, n, step))
    qs[:, N:N + W] = dot(wp[...], edge_rows(west, east))

    @pl.when(top)
    def _():
        mirror_wait(1)
        add_fold(dot(wp[...], fold_rows(mirrored(1))))

    cells[...] = g_ref[...].astype(F32).reshape(C * H, W)
    for r, value in enumerate(shift_sum()):
        at = pl.ds(r, C, stride=H)
        out_ref[at, :] = cells[at, :] + value
    results = [
        pltpu.make_async_copy(src, dst, out_s.at[n])
        for n, (src, dst) in enumerate(((out_ref, out_hbm), (second_ref, second_hbm), (first_ref, first_hbm)))
    ]
    results[0].start()

    halo_sent(early + late)
    for w in range(2):
        each(1, NI, lambda d: tile_copy(w, d, None).wait_send())
        own_forward(w, True).wait_send()
        each(1, NM, lambda d: slab_copy(w, d, None).wait_send())
        each(1, NM, lambda d: forward_copy(w, d, True).wait_send())
    each(0, NM, lambda n: pair_copy(n).wait_send())
    each(1, NM, lambda d: chip_copy(d, None).wait_send())
    side_pair().wait_send()
    each(1, NI, lambda d: side_lon(d, None).wait_send())

    @pl.when(top)
    def _():
        for phase in range(3):
            def sent(d):
                @pl.when(lon(d) < NG)
                def _():
                    row_copy(phase, fy, d, None).wait_send()

            each(1, NI, sent)

    @pl.when(worker)
    def _():
        for phase in range(3):
            each(1, NI, lambda d: turned_copy(phase, d, None).wait_send())

    side_end()
    results[1].start()
    sum_end()
    results[2].start()
    each(1, NI, lambda d: lon_copy(d, None).wait_send())
    each(1, NJ, lambda d: side_lat(d, None).wait_send())
    for result in results:
        result.wait()


def hand_over(out_in, first_in, second_in, out_ref, first_ref, second_ref, out_mid, first_mid, second_mid, came, went):
    size = out_in.shape[0] // PARTS
    ways = [(out_in.at[pl.ds(n * size, size)], out_mid.at[pl.ds(n * size, size)], out_ref.at[pl.ds(n * size, size)])
            for n in range(PARTS)]
    ways += [(first_in, first_mid, first_ref), (second_in, second_mid, second_ref)]
    first = [pltpu.make_async_copy(a, b, came.at[n]) for n, (a, b, _) in enumerate(ways)]
    then = [pltpu.make_async_copy(b, c, went.at[n]) for n, (_, b, c) in enumerate(ways)]
    for copy in first:
        copy.start()
    for copy, following in zip(first, then):
        copy.wait()
        following.start()
    for copy in then:
        copy.wait()


def body(x_codes, x_scale, h_codes, h_scale, grad_out, land, partner, w_first, w_second):
    C, H, W = x_codes.shape
    NJ, NI = lax.axis_size("lat"), lax.axis_size("lon")
    CJ, CI, NM = C // NJ, C // NI, NJ // 2
    LA, CL, RB, N = up(3 * C, LANES), up(C, LANES), up(3 * CJ, PAD), H * W
    ROWS = NJ * RB
    cfg = {"C": C, "H": H, "NJ": NJ, "NI": NI, "factor": 1.0 / math.sqrt(NJ * H * NI * W)}
    sem = pltpu.SemaphoreType.DMA
    vm = pltpu.VMEM
    args = (x_codes, x_scale.T, h_codes, h_scale.T, grad_out, land, partner.reshape(NI, W),
            w_first.transpose(0, 2, 1, 3), w_second.transpose(0, 2, 1, 3))
    shapes = (
        jax.ShapeDtypeStruct((C * H, W), F32),
        jax.ShapeDtypeStruct((3, CJ, 3, CI), F32),
        jax.ShapeDtypeStruct((3, CJ, 3, CI), F32),
    )
    scratch = [vm(arg.shape, arg.dtype) for arg in shapes + args] + [
        sem((9,)), sem((3,)),
        vm((C * H, W), F32),
        vm((C, N), F32),
        vm((9, PAD, LANES), F32),
        vm((2, PAD, LANES), BF16),
        vm((2, NI, PAD, LANES), BF16),
        vm((2, RB, LA), BF16),
        vm((2, 2, NM, RB, LA), BF16),
        vm((LA, ROWS), BF16),
        vm((LA, 3 * C), BF16),
        vm((C, N + 2 * W), BF16),
        vm((C, N), BF16),
        vm((LA, N + 2 * W), BF16),
        vm((LA, N + 2 * W), BF16),
        vm((ROWS, N + W), BF16),
        vm((2, W, CL), BF16),
        vm((2, W, CL), BF16),
        vm((3, NI, PAD, W), BF16),
        vm((3, NI, 2, PAD, W), BF16),
        vm((3, C // PAD, 2, PAD, W), BF16),
        vm((ROWS, 3 * W), BF16),
        vm((ROWS, 3 * C), BF16),
        vm((LA, N + W), F32),
        vm((3 * C, LA), F32),
        vm((2, NM, RB, LA), F32),
        vm((NM, RB, LA), SUM_TYPE),
        vm((NM, RB, LA), SUM_TYPE),
        vm((NM, RB, LA), SUM_TYPE),
        vm((NM, RB, LA), SUM_TYPE),
        vm((RB + PAD, LA), F32),
        vm((NI, PAD, LANES), F32),
        vm((NI, PAD, LANES), F32),
        vm((LANES, LANES), F32),
        vm((NI, RB, LA), F32),
        vm((NI, RB // 2, LA), SUM_TYPE),
        vm((NI, RB // 2, LA), SUM_TYPE),
        vm((NI, RB // 2, LA), SUM_TYPE),
        vm((NI, RB // 2, LA), SUM_TYPE),
        vm((NJ, RB // 2, LANES), F32),
        vm((NJ, RB // 2, LANES), F32),
        sem((2, NI)), sem((2, NI)), sem((2, NM)), sem((2, NM)), sem((2, NM)), sem((2, NM)),
        sem((2, 12)), sem((2, 12)), sem((3, NI)), sem((3, NI)), sem((3, NI)), sem((3, NI)),
        sem((NM,)), sem((NM,)), sem((NM,)), sem((NM,)), sem((NI,)), sem((NI,)),
        sem, sem, sem((NI,)), sem((NI,)), sem((NJ,)), sem((NJ,)),
    ]
    results = pl.pallas_call(
        functools.partial(kernel, cfg),
        out_shape=shapes,
        in_specs=[pl.BlockSpec(memory_space=pl.ANY)] * 9,
        out_specs=[pl.BlockSpec(memory_space=pl.ANY)] * 3,
        scratch_shapes=scratch,
        compiler_params=pltpu.CompilerParams(
            collective_id=0, has_side_effects=True, vmem_limit_bytes=GRANT
        ),
    )(*args)
    grad_in, first, second = pl.pallas_call(
        hand_over,
        out_shape=shapes,
        in_specs=[pl.BlockSpec(memory_space=pl.ANY)] * 3,
        out_specs=[pl.BlockSpec(memory_space=pl.ANY)] * 3,
        scratch_shapes=[vm(arg.shape, arg.dtype) for arg in shapes] + [sem((PARTS + 2,))] * 2,
        compiler_params=pltpu.CompilerParams(vmem_limit_bytes=GRANT),
    )(*results)
    return (grad_in.reshape(C, H, W), first.transpose(0, 2, 1, 3), second.transpose(0, 2, 1, 3))


def solution(mesh):
    placed = (
        P(None, "lat", "lon"),
        P(None, "lat"),
        P(None, "lat", "lon"),
        P(None, "lat"),
        P(None, "lat", "lon"),
        P("lat", "lon"),
        P(),
        P(None, None, "lat", "lon"),
        P(None, None, "lat", "lon"),
    )
    return jax.shard_map(
        body,
        mesh=mesh,
        in_specs=placed,
        out_specs=(P(None, "lat", "lon"), P(None, None, "lat", "lon"), P(None, None, "lat", "lon")),
        check_vma=False,
    )
```

```python
import functools
import math

import jax
import jax.numpy as jnp
from jax import lax
from jax.experimental import pallas as pl
from jax.experimental.pallas import tpu as pltpu
from jax.sharding import PartitionSpec as P

MESH = pl.DeviceIdType.MESH
F32, BF16 = jnp.float32, jnp.bfloat16
PAD = 16
LANES = 128
SUM_TYPE = jnp.bfloat16
PARTS = 2
GRANT = 56 * 1024 * 1024


def up(value, unit):
    return -(-value // unit) * unit


def gelu_parts(h):
    k = math.sqrt(2.0 / math.pi)
    tanh_part = jnp.tanh(k * (h + 0.044715 * h * h * h))
    value = 0.5 * h * (1.0 + tanh_part)
    slope = 0.5 * (1.0 + tanh_part) + 0.5 * h * (1.0 - tanh_part * tanh_part) * k * (
        1.0 + 3.0 * 0.044715 * h * h
    )
    return (value, slope)


def dot(a, b):
    return lax.dot_general(a, b, (((1,), (0,)), ((), ())), preferred_element_type=F32)


def dot_nt(a, b):
    return lax.dot_general(a, b, (((1,), (1,)), ((), ())), preferred_element_type=F32)


def put(tiles, lane, source, source_lane, count, target_lane):
    shift = (target_lane - source_lane) % LANES
    moved = pltpu.roll(source, shift, 1) if shift else source
    tile, off = divmod(target_lane, LANES)
    keep = (lane >= off) & (lane < off + count)
    tiles[tile] = jnp.where(keep, moved, tiles[tile])
    over = off + count - LANES
    if over > 0:
        tiles[tile + 1] = jnp.where(lane < over, moved, tiles[tile + 1])


def put_wide(tiles, lane, sources, source_lane, count, target_lane):
    while count > 0:
        tile, off = divmod(source_lane, LANES)
        part = min(count, LANES - off)
        put(tiles, lane, sources[tile], off, part, target_lane)
        source_lane, target_lane, count = source_lane + part, target_lane + part, count - part


def kernel(
    cfg,
    x_hbm, xs_hbm, h_hbm, hs_hbm, g_hbm, land_hbm, partner_hbm, w0_hbm, w1_hbm,
    out_hbm, first_hbm, second_hbm,
    out_ref, first_ref, second_ref, x_ref,
    xs_ref, h_ref, hs_ref, g_ref, land_ref, partner_ref, w0_ref, w1_ref, in_s, out_s,
    cells, slope, wtmp, wown, wtile, wrow, wfull, wt, wp, fh, act, sg, sx, gq, edge, edge_in,
    mrow, mout, mirr, gqm, spread, qs, nat, tap, given, tap_in, part, part_in, tot, small, small_in,
    turned, tapz, givenz, tapz_in, partz, partz_in, smallz, smallz_in,
    st1_s, st1_r, st2_s, st2_r, fw_s, fw_r, ha_s, ha_r, mi_s, mi_r, mo_s, mo_r,
    r0_s, r0_r, r1_s, r1_r, r2_s, r2_r, z0_s, z0_r, z1_s, z1_r, z2_s, z2_r,
):
    C, H, NJ, NI = cfg["C"], cfg["H"], cfg["NJ"], cfg["NI"]
    W = LANES
    CJ, CI, NM, NG = C // NJ, C // NI, NJ // 2, C // PAD
    LA, CL, RB = up(3 * C, LANES), up(C, LANES), up(3 * (C // NJ), PAD)
    ROWS = NJ * RB
    N = H * W
    j, i = lax.axis_index("lat"), lax.axis_index("lon")
    k, m = lax.rem(j, 2), lax.div(j, 2)
    top = j == NJ - 1
    bottom = j == 0
    worker = top & (i < NG)

    def rcopy(src, dst, ss, rs, dj, di):
        return pltpu.make_async_remote_copy(
            src_ref=src, dst_ref=dst, send_sem=ss, recv_sem=rs,
            device_id={"lat": dj, "lon": di}, device_id_type=MESH,
        )

    def each(lo, hi, fn):
        lax.fori_loop(lo, hi, lambda d, c: (fn(d), c)[1], 0)

    def lon(d):
        return jnp.bitwise_xor(i, d)

    def lat(d):
        return jnp.bitwise_xor(j, d)

    def mate(d):
        return jnp.bitwise_xor(m, d)

    def beside(axis, place, d):
        return lax.rem(place + d + axis, axis)

    lon_order = [d for d in (9, 8, 11, 10, 7, 6, 15, 14, 5, 13, 4, 12, 3, 2, 1) if d < NI]
    lat_order = [d for d in (12, 13, 10, 11, 14, 15, 8, 9, 4, 5, 2, 3, 6, 7, 1) if d < NJ]
    mate_order = [d for d in (6, 5, 7, 4, 2, 1, 3) if d < NM]

    barrier = pltpu.get_barrier_semaphore()

    def greet(dj, di):
        pl.semaphore_signal(barrier, inc=1, device_id={"lat": dj, "lon": di}, device_id_type=MESH)

    for d in lon_order:
        greet(j, lon(d))
    for d in lat_order:
        greet(lat(d), i)
    for dj in (1, -1):
        for di in (1, -1):
            greet(beside(NJ, j, dj), beside(NI, i, di))
    loads = [
        pltpu.make_async_copy(src, dst, in_s.at[n])
        for n, (src, dst) in enumerate((
            (w1_hbm, w1_ref), (w0_hbm, w0_ref), (land_hbm, land_ref), (g_hbm, g_ref), (xs_hbm, xs_ref),
            (x_hbm, x_ref), (hs_hbm, hs_ref), (h_hbm, h_ref), (partner_hbm, partner_ref)))
    ]
    for load in loads:
        load.start()

    loads[0].wait()

    def make_tile(ref):
        wtmp[...] = jnp.zeros(wtmp.shape, F32)
        for a in range(3):
            block = ref[a].astype(F32)
            for b in range(3):
                wtmp[3 * a + b, 0:CJ, 0:CI] = block[:, b, :]
        value = wtmp[0]
        for n in range(1, 9):
            value = value + pltpu.roll(wtmp[n], n * CI, 1)
        return value

    wown[1] = make_tile(w1_ref).astype(BF16)

    def blocks(ref):
        cells[...] = ref[...].astype(F32).reshape(C * H, W)
        return [cells[pl.ds(r, C, stride=H), :] for r in range(H)]

    def ocean(r):
        return land_ref[r:r + 1, :].astype(F32)

    def slot(r):
        return pl.ds((r + 1) * W, W)

    lane = lax.broadcasted_iota(jnp.int32, (C, W), 1)
    center = pl.ds(C, C)
    fy = sg.at[center]

    def add_edges(packed, f, r, blk):
        spots = [f * 8 + r]
        if r == H - 1:
            spots.append(32 + f)
        if r == 0:
            spots.append(48 + f)
        for spot in spots:
            packed = jnp.where(lane == spot, pltpu.roll(blk, spot, 1) if spot else blk, packed)
            packed = jnp.where(lane == 64 + spot, pltpu.roll(blk, 65 + spot, 1), packed)
        return packed

    def turn_edges(phase, packed):
        if CL > C:
            packed = jnp.concatenate([packed, jnp.zeros((CL - C, W), F32)], axis=0)
        edge[phase] = jnp.transpose(packed).astype(BF16)

    for load in loads[2:6]:
        load.wait()
    scale = jnp.transpose(xs_ref[...])
    packed = jnp.zeros((C, W), F32)
    for r, blk in enumerate(blocks(g_ref)):
        value = blk * ocean(r)
        fy[:, slot(r)] = value.astype(BF16)
        packed = add_edges(packed, 0, r, value)
    for r, blk in enumerate(blocks(x_ref)):
        x = (blk * scale[:, r:r + 1]).astype(BF16)
        sx[center, slot(r)] = x
        packed = add_edges(packed, 1, r, x.astype(F32))

    pl.semaphore_wait(barrier, NI - 1 + NJ - 1 + 4)

    def tile_copy(w, d, other):
        return rcopy(wown.at[w], wtile.at[w, i if other is None else other],
                     st1_s.at[w, d], st1_r.at[w, d], j, lon(d))

    for d in lon_order:
        tile_copy(1, d, None).start()
    wtile[1, i] = wown[1]
    def row_copy(phase, src, d, other):
        g = lon(d) if other is None else i
        return rcopy(src.at[pl.ds(pl.multiple_of(g * PAD, PAD), PAD), slot(H - 1)],
                     mrow.at[phase, i if other is None else other],
                     mi_s.at[phase, d], mi_r.at[phase, d], j, lon(d))

    def turned_copy(phase, d, other):
        return rcopy(mout.at[phase, lon(d)], mirr.at[phase, i if other is None else other],
                     mo_s.at[phase, d], mo_r.at[phase, d], j, lon(d))

    def mirror_send(phase, src):
        @pl.when(top)
        def _():
            for d in lon_order:
                @pl.when(lon(d) < NG)
                def _():
                    row_copy(phase, src, d, None).start()

            @pl.when(i < NG)
            def _():
                mrow[phase, i] = src[pl.ds(pl.multiple_of(i * PAD, PAD), PAD), slot(H - 1)]

    def mirror_turn(phase, src):
        @pl.when(worker)
        def _():
            ncols = NI * W
            flip = (lax.broadcasted_iota(jnp.int32, (W, W), 0)
                    + lax.broadcasted_iota(jnp.int32, (W, W), 1)) == W - 1
            flip = jnp.where(flip, 1.0, 0.0).astype(BF16)
            tlane = lax.broadcasted_iota(jnp.int32, (PAD, W), 1)
            where = partner_ref[pl.ds(i, 1), :] + lax.broadcasted_iota(jnp.int32, (1, W), 1) + i * W
            turn = (ncols - 1) - (where & (ncols - 1))
            turn = jnp.broadcast_to(turn, (PAD, W))

            def left(tiles, by):
                if by % W == 0:
                    return [tiles[(t + by // W) % NI] for t in range(NI)]
                moved = [pltpu.roll(tile, W - by, 1) for tile in tiles]
                return [jnp.where(tlane < W - by, moved[t], moved[(t + 1) % NI]) for t in range(NI)]

            each(1, NI, lambda d: row_copy(phase, src, d, lon(d)).wait_recv())
            rev = dot(mrow[phase].reshape(NI * PAD, W), flip)
            tiles = [rev[(NI - 1 - v) * PAD:(NI - v) * PAD] for v in range(NI)]
            for bit in range(ncols.bit_length() - 1):
                take = (turn & (1 << bit)) != 0
                tiles = [jnp.where(take, new, old) for new, old in zip(left(tiles, 1 << bit), tiles)]
            for t in range(NI):
                before, after = pltpu.roll(tiles[t - 1], 1, 1), pltpu.roll(tiles[(t + 1) % NI], 1, 1)
                mout[phase, t, 0] = tiles[t].astype(BF16)
                mout[phase, t, 1] = jnp.where(tlane == 0, before, after).astype(BF16)
            mirr[phase, i] = mout[phase, i]
            for d in lon_order:
                turned_copy(phase, d, None).start()

    def mirror_wait(phase):
        def step(d):
            @pl.when(lon(d) < NG)
            def _():
                turned_copy(phase, d, lon(d)).wait_recv()

        each(1, NI, step)

    def mirrored(phase):
        block = mirr[phase, :, 0].reshape(C, W).astype(F32)
        edges = mirr[phase, :, 1].reshape(C, W).astype(F32)
        before = jnp.where(lane == 0, edges, pltpu.roll(block, 1, 1))
        after = jnp.where(lane == W - 1, pltpu.roll(edges, W - 2, 1), pltpu.roll(block, W - 1, 1))
        return jnp.concatenate([before, block, after], axis=1).astype(BF16)

    mirror_send(0, fy)
    loads[1].wait()
    wown[0] = make_tile(w0_ref).astype(BF16)

    for load in loads[6:]:
        load.wait()
    scale = jnp.transpose(hs_ref[...])
    for r, blk in enumerate(blocks(h_ref)):
        h = blk * scale[:, r:r + 1]
        value, deriv = gelu_parts(h)
        act[:, r * W:(r + 1) * W] = (ocean(r) * value).astype(BF16)
        slope[:, r * W:(r + 1) * W] = deriv
    turn_edges(0, packed)

    def halo_copies(phase, fields):
        north, south = jnp.logical_not(top), jnp.logical_not(bottom)
        out = []
        for f, field in enumerate(fields):
            s = 2 * f
            out.append((rcopy(field.at[:, slot(H - 1)], field.at[:, slot(-1)],
                              ha_s.at[phase, s], ha_r.at[phase, s], beside(NJ, j, 1), i), north, south))
            out.append((rcopy(field.at[:, slot(0)], field.at[:, slot(H)],
                              ha_s.at[phase, s + 1], ha_r.at[phase, s + 1], beside(NJ, j, -1), i), south, north))
        side = up(8 * len(fields), PAD)
        n = 6
        for di, base, target in ((1, 64, 0), (-1, 0, 64)):
            for dj, off, size in ((0, 0, side), (1, 32, PAD), (-1, 48, PAD)):
                sent, comes = {0: (None, None), 1: (north, south), -1: (south, north)}[dj]
                out.append((rcopy(edge.at[phase, pl.ds(base + off, size)],
                                  edge_in.at[phase, pl.ds(target + off, size)],
                                  ha_s.at[phase, n], ha_r.at[phase, n],
                                  beside(NJ, j, dj), beside(NI, i, di)), sent, comes))
                n += 1
        return out

    def only(condition, fn):
        if condition is None:
            fn()
        else:
            pl.when(condition)(fn)

    def halo_start(copies):
        for copy, sent, _ in copies:
            only(sent, copy.start)

    def halo_wait(copies):
        for copy, _, comes in copies:
            only(comes, copy.wait_recv)

    def halo_sent(copies):
        for copy, sent, _ in copies:
            only(sent, copy.wait_send)

    early = halo_copies(0, (fy, sx.at[center]))
    halo_start(early)

    mirror_send(2, sx.at[center])
    for d in lon_order:
        tile_copy(0, d, None).start()
    wtile[0, i] = wown[0]
    at = lax.broadcasted_iota(jnp.int32, (ROWS, 1), 0)
    half, rest = lax.div(at, NM * RB), lax.rem(at, NM * RB)
    own = lax.rem(rest, RB)
    line = lax.div(own, CJ)
    target = line * C + (2 * lax.div(rest, RB) + half) * CJ + own - line * CJ
    target = jnp.where(own < 3 * CJ, target, -1)
    spread[...] = jnp.where(lax.broadcasted_iota(jnp.int32, (ROWS, 3 * C), 1) == target, 1.0, 0.0).astype(BF16)

    def make_slab(w):
        each(1, NI, lambda d: tile_copy(w, d, lon(d)).wait_recv())
        wlane = lax.broadcasted_iota(jnp.int32, (PAD, W), 1)
        tot[...] = jnp.zeros(tot.shape, F32)
        pieces = [wtile[w, s].astype(F32) for s in range(NI)]
        for a in range(3):
            tiles = [jnp.zeros((PAD, W), F32) for _ in range(LA // W)]
            for s in range(NI):
                for b in range(3):
                    put(tiles, wlane, pieces[s], (3 * a + b) * CI, CI, b * C + s * CI)
            for t, value in enumerate(tiles):
                tot[a * CJ:(a + 1) * CJ, t * W:(t + 1) * W] = value[:CJ]
        wrow[w] = tot[0:RB].astype(BF16)

    def slab_copy(w, d, other):
        return rcopy(wrow.at[w], wfull.at[w, k, m if other is None else other],
                     st2_s.at[w, d], st2_r.at[w, d], 2 * mate(d) + k, i)

    def forward_copy(w, d, mine):
        n = mate(d)
        return rcopy(wfull.at[w, k, n], wfull.at[w, k if mine else 1 - k, n],
                     fw_s.at[w, d], fw_r.at[w, d], j + 1 - 2 * k, i)

    def own_forward(w, mine):
        return rcopy(wrow.at[w], wfull.at[w, k if mine else 1 - k, m], fw_s.at[w, 0], fw_r.at[w, 0],
                     j + 1 - 2 * k, i)

    def send_slab(w):
        for d in mate_order:
            slab_copy(w, d, None).start()
        own_forward(w, True).start()
        wfull[w, k, m] = wrow[w]

    def pass_on(w):
        def step(d):
            slab_copy(w, d, mate(d)).wait_recv()
            forward_copy(w, d, True).start()

        each(1, NM, step)

    def have_weights(w):
        own_forward(w, False).wait_recv()
        each(1, NM, lambda d: forward_copy(w, d, False).wait_recv())
        wt[...] = jnp.transpose(wfull[w].reshape(ROWS, LA).astype(F32)).astype(BF16)

    def columns(got, f):
        result = []
        for base in (0, 64):
            start = base + f * 8
            value = jnp.where((lane >= 1) & (lane <= H), pltpu.roll(got, (1 - start) % W, 1), 0.0)
            lower = pltpu.roll(got, (-(base + 32 + f)) % W, 1)
            upper = pltpu.roll(got, (H + 1 - (base + 48 + f)) % W, 1)
            value = jnp.where((lane == 0) & jnp.logical_not(bottom), lower, value)
            value = jnp.where((lane == H + 1) & jnp.logical_not(top), upper, value)
            result.append(value)
        return result

    def turned_edges(phase):
        return jnp.transpose(edge_in[phase].astype(F32))[:C]

    def clear_ends(field):
        @pl.when(bottom)
        def _():
            field[:, slot(-1)] = jnp.zeros((C, W), BF16)

        @pl.when(top)
        def _():
            field[:, slot(H)] = jnp.zeros((C, W), BF16)

    def shifted(field, west, east):
        for r in range(-1, H + 1):
            blk = field[center, slot(r)].astype(F32)
            lower = jnp.where(lane == 0, pltpu.roll(west, (-(r + 1)) % W, 1), pltpu.roll(blk, 1, 1))
            upper = jnp.where(lane == W - 1, pltpu.roll(east, (W - 2 - r) % W, 1), pltpu.roll(blk, W - 1, 1))
            field[0:C, slot(r)] = lower.astype(BF16)
            field[2 * C:3 * C, slot(r)] = upper.astype(BF16)
        if LA > 3 * C:
            field[3 * C:LA, :] = jnp.zeros((LA - 3 * C, (H + 2) * W), BF16)

    def tap_rows(field, n, size):
        return jnp.concatenate([field[:, (2 - a) * W + n:(2 - a) * W + n + size] for a in range(3)], axis=0)

    def edge_rows(west, east):
        both = []
        for a in range(3):
            at_west = pltpu.roll(west, (a - 2) % W, 1)
            at_east = pltpu.roll(east, (H + a - 2) % W, 1)
            value = jnp.where(lane < H, at_west, jnp.where(lane < 2 * H, at_east, 0.0))
            both.append(value.astype(BF16))
        return jnp.concatenate(both, axis=0)

    def fold_rows(mirror):
        return jnp.concatenate([jnp.zeros((2 * C, 3 * W), BF16), mirror], axis=0)

    step = min(2 * W, N)

    def tap_grad(grad, field):
        for a in range(3):
            nat[a * C:(a + 1) * C, :] = dot_nt(grad[:, W:W + N], field[:, a * W:a * W + N])

    def tap_store():
        for a in range(3):
            for jj in range(NJ):
                tap[jj % 2, jj // 2, a * CJ:(a + 1) * CJ, :] = nat[a * C + jj * CJ:a * C + (jj + 1) * CJ, :]

    def side_store():
        for a in range(3):
            for s in range(NI):
                tapz[s, a * CI:(a + 1) * CI, :] = nat[a * C + s * CI:a * C + (s + 1) * CI, :]

    def add_fold(weight, rows):
        share = dot(weight[0:C, :], rows[:, 0:W])
        for b in (1, 2):
            share = share + dot(weight[b * C:(b + 1) * C, :], rows[:, b * W:(b + 1) * W])
        qs[C:2 * C, N - W:N] += share

    def shift_sum():
        first, last = qs[0:C, N:N + W], qs[2 * C:3 * C, N:N + W]
        result = []
        for r in range(H):
            at = slice(r * W, (r + 1) * W)
            left = jnp.where(lane == W - 1, pltpu.roll(first, (W - 1 - H - r) % W, 1),
                             pltpu.roll(qs[0:C, at], W - 1, 1))
            right = jnp.where(lane == 0, pltpu.roll(last, (-r) % W, 1), pltpu.roll(qs[2 * C:3 * C, at], 1, 1))
            result.append(qs[C:2 * C, at] + left + right)
        return result

    def pair_copy(n):
        return rcopy(given.at[n], tap_in.at[n], r0_s.at[n], r0_r.at[n], j + 1 - 2 * k, i)

    def chip_copy(d, other):
        return rcopy(part.at[mate(d)], part_in.at[m if other is None else other],
                     r1_s.at[d], r1_r.at[d], 2 * mate(d) + k, i)

    def lon_copy(d, other):
        return rcopy(small.at[lon(d)], small_in.at[i if other is None else other], r2_s.at[d], r2_r.at[d], j, lon(d))

    def sum_start():
        given[...] = tap[1 - k].astype(SUM_TYPE)
        for d in mate_order:
            pair_copy(mate(d)).start()
        pair_copy(m).start()

    def sum_chips():
        for d in mate_order:
            n = mate(d)
            pair_copy(n).wait_recv()
            part[n] = (tap[k, n] + tap_in[n].astype(F32)).astype(SUM_TYPE)
            chip_copy(d, None).start()
        pair_copy(m).wait_recv()

    def sum_lon():
        total = tap[k, m] + tap_in[m].astype(F32)
        for d in range(1, NM):
            chip_copy(d, mate(d)).wait_recv()
            total = total + part_in[mate(d)].astype(F32)
        tot[0:RB] = total
        slane = lax.broadcasted_iota(jnp.int32, (PAD, W), 1)
        sources = [[tot[a * CJ:a * CJ + PAD, t * W:(t + 1) * W] for t in range(LA // W)] for a in range(3)]
        for s in range(NI):
            tiles = [jnp.zeros((PAD, W), F32)]
            for a in range(3):
                for b in range(3):
                    put_wide(tiles, slane, sources[a], b * C + s * CI, CI, (3 * a + b) * CI)
            small[s] = tiles[0]
        small_in[i] = small[i]
        for d in lon_order:
            lon_copy(d, None).start()

    def sum_end():
        each(1, NI, lambda d: lon_copy(d, lon(d)).wait_recv())
        total = small_in[0]
        for s in range(1, NI):
            total = total + small_in[s]
        total = total * cfg["factor"]
        for a in range(3):
            for b in range(3):
                n = 3 * a + b
                moved = pltpu.roll(total, (-n * CI) % W, 1) if n else total
                first_ref[a, :, b, :] = moved[:CJ, :CI]

    HR = RB // 2
    mine = pl.ds(pl.multiple_of(k * HR, HR), HR)
    others = pl.ds(pl.multiple_of((1 - k) * HR, HR), HR)

    def side_pair():
        return rcopy(givenz, tapz_in, z0_s, z0_r, j + 1 - 2 * k, i)

    def side_lon(d, other):
        return rcopy(partz.at[lon(d)], partz_in.at[i if other is None else other], z1_s.at[d], z1_r.at[d], j, lon(d))

    def side_lat(d, other):
        return rcopy(smallz.at[lat(d)], smallz_in.at[j if other is None else other], z2_s.at[d], z2_r.at[d], lat(d), i)

    def side_start():
        givenz[...] = tapz[:, others].astype(SUM_TYPE)
        side_pair().start()

    def side_sum_lon():
        side_pair().wait_recv()
        for s in range(NI):
            partz[s] = (tapz[s, mine] + tapz_in[s].astype(F32)).astype(SUM_TYPE)
        side_send(1)

    def side_send(odd):
        for d in lon_order:
            if d % 2 == odd:
                side_lon(d, None).start()

    def side_sum_lat():
        total = tapz[i, mine] + tapz_in[i].astype(F32)
        for d in range(1, NI):
            side_lon(d, lon(d)).wait_recv()
            total = total + partz_in[lon(d)].astype(F32)
        slane = lax.broadcasted_iota(jnp.int32, (HR, W), 1)
        sources = [total[:, t * W:(t + 1) * W] for t in range(LA // W)]
        for s in range(NJ):
            tiles = [jnp.zeros((HR, W), F32)]
            for a in range(3):
                put_wide(tiles, slane, sources, a * C + s * CJ, CJ, a * CJ)
            smallz[s] = tiles[0]
        smallz_in[j] = smallz[j]
        for d in lat_order:
            side_lat(d, None).start()

    def side_end():
        each(1, NJ, lambda d: side_lat(d, lat(d)).wait_recv())
        halves = []
        for h in range(2):
            total = smallz_in[h]
            for s in range(h + 2, NJ, 2):
                total = total + smallz_in[s]
            halves.append(total)
        total = jnp.concatenate(halves + [jnp.zeros((W - RB, W), F32)], axis=0) * cfg["factor"]
        turned[...] = jnp.transpose(total)
        for b in range(3):
            block = turned[(2 - b) * CJ:(3 - b) * CJ, :]
            for a in range(3):
                moved = pltpu.roll(block, (-a * CI) % W, 1) if a else block
                second_ref[a, :, b, :] = moved[:, :CI]

    make_slab(1)
    send_slab(1)
    mirror_turn(0, fy)
    tap[:, :, 3 * CJ:RB, :] = jnp.zeros((2, NM, RB - 3 * CJ, LA), F32)
    tapz[:, 3 * CI:RB, :] = jnp.zeros((NI, RB - 3 * CI, LA), F32)

    halo_wait(early)
    clear_ends(fy)
    clear_ends(sx.at[center])
    got = turned_edges(0)
    west, east = columns(got, 0)
    for n in range(0, N, step):
        gq[:, n:n + step] = dot(spread[...], tap_rows(fy, n, step)).astype(BF16)
    gq[:, N:N + W] = dot(spread[...], edge_rows(west, east)).astype(BF16)
    mirror_turn(2, sx.at[center])
    shifted(sg, west, east)
    west, east = columns(got, 1)
    shifted(sx, west, east)
    for a in range(3):
        nat[a * C:(a + 1) * C, :] = dot_nt(act[...], sg[:, (2 - a) * W:(2 - a) * W + N])
    make_slab(0)
    pass_on(1)
    send_slab(0)
    side_store()
    @pl.when(top)
    def _():
        mirror_wait(0)
        mirror = mirrored(0)
        stacked = jnp.concatenate([mirror[:, 2 * W:3 * W], mirror[:, W:2 * W], mirror[:, 0:W],
                                   jnp.zeros((LA - 3 * C, W), BF16)], axis=0)
        nat[0:C, :] = dot_nt(act[:, N - W:N], stacked)
        for s in range(NI):
            tapz[s, 2 * CI:3 * CI, :] += nat[s * CI:(s + 1) * CI, :]
        gqm[...] = dot(spread[...], fold_rows(mirror)).astype(BF16)

    side_start()
    have_weights(1)
    for n in range(0, N + W, step):
        size = min(step, N + W - n)
        qs[:, n:n + size] = dot(wt[...], gq[:, n:n + size])

    side_sum_lon()

    @pl.when(m != NM - 1)
    def _():
        side_send(0)

    @pl.when(top)
    def _():
        add_fold(wt, gqm)
        mirror_wait(2)
        north = mirrored(2)
        for b in range(3):
            sx[b * C:(b + 1) * C, slot(H)] = north[:, b * W:(b + 1) * W]

    for r, value in enumerate(shift_sum()):
        fh[:, slot(r)] = (value * ocean(r) * slope[:, r * W:(r + 1) * W]).astype(BF16)

    mirror_send(1, fh)

    @pl.when(m == NM - 1)
    def _():
        side_send(0)

    tap_grad(fh, sx)
    tap_store()
    sum_start()
    packed = jnp.zeros((C, W), F32)
    for r in range(H):
        packed = add_edges(packed, 0, r, fh[:, slot(r)].astype(F32))
    turn_edges(1, packed)
    late = halo_copies(1, (fh,))
    halo_start(late)
    sum_chips()


    pass_on(0)
    have_weights(0)
    wp[...] = dot(wt[...], spread[...]).astype(BF16)
    mirror_turn(1, fh)
    side_sum_lat()
    sum_lon()

    halo_wait(late)
    clear_ends(fh)
    west, east = columns(turned_edges(1), 0)
    for n in range(0, N, step):
        qs[:, n:n + step] = dot(wp[...], tap_rows(fh, n, step))
    qs[:, N:N + W] = dot(wp[...], edge_rows(west, east))

    @pl.when(top)
    def _():
        mirror_wait(1)
        add_fold(wp, fold_rows(mirrored(1)))

    cells[...] = g_ref[...].astype(F32).reshape(C * H, W)
    for r, value in enumerate(shift_sum()):
        at = pl.ds(r, C, stride=H)
        out_ref[at, :] = cells[at, :] + value
    results = [
        pltpu.make_async_copy(src, dst, out_s.at[n])
        for n, (src, dst) in enumerate(((out_ref, out_hbm), (second_ref, second_hbm), (first_ref, first_hbm)))
    ]
    results[0].start()

    halo_sent(early + late)
    for w in range(2):
        each(1, NI, lambda d: tile_copy(w, d, None).wait_send())
        own_forward(w, True).wait_send()
        each(1, NM, lambda d: slab_copy(w, d, None).wait_send())
        each(1, NM, lambda d: forward_copy(w, d, True).wait_send())
    each(0, NM, lambda n: pair_copy(n).wait_send())
    each(1, NM, lambda d: chip_copy(d, None).wait_send())
    side_pair().wait_send()
    each(1, NI, lambda d: side_lon(d, None).wait_send())

    @pl.when(top)
    def _():
        for phase in range(3):
            def sent(d):
                @pl.when(lon(d) < NG)
                def _():
                    row_copy(phase, fy, d, None).wait_send()

            each(1, NI, sent)

    @pl.when(worker)
    def _():
        for phase in range(3):
            each(1, NI, lambda d: turned_copy(phase, d, None).wait_send())

    side_end()
    results[1].start()
    sum_end()
    results[2].start()
    each(1, NI, lambda d: lon_copy(d, None).wait_send())
    each(1, NJ, lambda d: side_lat(d, None).wait_send())
    for result in results:
        result.wait()


def hand_over(out_in, first_in, second_in, out_ref, first_ref, second_ref, out_mid, first_mid, second_mid, came, went):
    size = out_in.shape[0] // PARTS
    ways = [(out_in.at[pl.ds(n * size, size)], out_mid.at[pl.ds(n * size, size)], out_ref.at[pl.ds(n * size, size)])
            for n in range(PARTS)]
    ways += [(first_in, first_mid, first_ref), (second_in, second_mid, second_ref)]
    first = [pltpu.make_async_copy(a, b, came.at[n]) for n, (a, b, _) in enumerate(ways)]
    then = [pltpu.make_async_copy(b, c, went.at[n]) for n, (_, b, c) in enumerate(ways)]
    for copy in first:
        copy.start()
    for copy, following in zip(first, then):
        copy.wait()
        following.start()
    for copy in then:
        copy.wait()


def body(x_codes, x_scale, h_codes, h_scale, grad_out, land, partner, w_first, w_second):
    C, H, W = x_codes.shape
    NJ, NI = lax.axis_size("lat"), lax.axis_size("lon")
    CJ, CI, NM = C // NJ, C // NI, NJ // 2
    LA, CL, RB, N = up(3 * C, LANES), up(C, LANES), up(3 * CJ, PAD), H * W
    ROWS = NJ * RB
    cfg = {"C": C, "H": H, "NJ": NJ, "NI": NI, "factor": 1.0 / math.sqrt(NJ * H * NI * W)}
    sem = pltpu.SemaphoreType.DMA
    vm = pltpu.VMEM
    args = (x_codes, x_scale.T, h_codes, h_scale.T, grad_out, land, partner.reshape(NI, W),
            w_first.transpose(0, 2, 1, 3), w_second.transpose(0, 2, 1, 3))
    shapes = (
        jax.ShapeDtypeStruct((C * H, W), F32),
        jax.ShapeDtypeStruct((3, CJ, 3, CI), F32),
        jax.ShapeDtypeStruct((3, CJ, 3, CI), F32),
    )
    scratch = [vm(arg.shape, arg.dtype) for arg in shapes + args] + [
        sem((9,)), sem((3,)),
        vm((C * H, W), F32),
        vm((C, N), F32),
        vm((9, PAD, LANES), F32),
        vm((2, PAD, LANES), BF16),
        vm((2, NI, PAD, LANES), BF16),
        vm((2, RB, LA), BF16),
        vm((2, 2, NM, RB, LA), BF16),
        vm((LA, ROWS), BF16),
        vm((LA, 3 * C), BF16),
        vm((C, N + 2 * W), BF16),
        vm((C, N), BF16),
        vm((LA, N + 2 * W), BF16),
        vm((LA, N + 2 * W), BF16),
        vm((ROWS, N + W), BF16),
        vm((2, W, CL), BF16),
        vm((2, W, CL), BF16),
        vm((3, NI, PAD, W), BF16),
        vm((3, NI, 2, PAD, W), BF16),
        vm((3, C // PAD, 2, PAD, W), BF16),
        vm((ROWS, 3 * W), BF16),
        vm((ROWS, 3 * C), BF16),
        vm((LA, N + W), F32),
        vm((3 * C, LA), F32),
        vm((2, NM, RB, LA), F32),
        vm((NM, RB, LA), SUM_TYPE),
        vm((NM, RB, LA), SUM_TYPE),
        vm((NM, RB, LA), SUM_TYPE),
        vm((NM, RB, LA), SUM_TYPE),
        vm((RB + PAD, LA), F32),
        vm((NI, PAD, LANES), F32),
        vm((NI, PAD, LANES), F32),
        vm((LANES, LANES), F32),
        vm((NI, RB, LA), F32),
        vm((NI, RB // 2, LA), SUM_TYPE),
        vm((NI, RB // 2, LA), SUM_TYPE),
        vm((NI, RB // 2, LA), SUM_TYPE),
        vm((NI, RB // 2, LA), SUM_TYPE),
        vm((NJ, RB // 2, LANES), F32),
        vm((NJ, RB // 2, LANES), F32),
        sem((2, NI)), sem((2, NI)), sem((2, NM)), sem((2, NM)), sem((2, NM)), sem((2, NM)),
        sem((2, 12)), sem((2, 12)), sem((3, NI)), sem((3, NI)), sem((3, NI)), sem((3, NI)),
        sem((NM,)), sem((NM,)), sem((NM,)), sem((NM,)), sem((NI,)), sem((NI,)),
        sem, sem, sem((NI,)), sem((NI,)), sem((NJ,)), sem((NJ,)),
    ]
    results = pl.pallas_call(
        functools.partial(kernel, cfg),
        out_shape=shapes,
        in_specs=[pl.BlockSpec(memory_space=pl.ANY)] * 9,
        out_specs=[pl.BlockSpec(memory_space=pl.ANY)] * 3,
        scratch_shapes=scratch,
        compiler_params=pltpu.CompilerParams(
            collective_id=0, has_side_effects=True, vmem_limit_bytes=GRANT
        ),
    )(*args)
    grad_in, first, second = pl.pallas_call(
        hand_over,
        out_shape=shapes,
        in_specs=[pl.BlockSpec(memory_space=pl.ANY)] * 3,
        out_specs=[pl.BlockSpec(memory_space=pl.ANY)] * 3,
        scratch_shapes=[vm(arg.shape, arg.dtype) for arg in shapes] + [sem((PARTS + 2,))] * 2,
        compiler_params=pltpu.CompilerParams(vmem_limit_bytes=GRANT),
    )(*results)
    return (grad_in.reshape(C, H, W), first.transpose(0, 2, 1, 3), second.transpose(0, 2, 1, 3))


def solution(mesh):
    placed = (
        P(None, "lat", "lon"),
        P(None, "lat"),
        P(None, "lat", "lon"),
        P(None, "lat"),
        P(None, "lat", "lon"),
        P("lat", "lon"),
        P(),
        P(None, None, "lat", "lon"),
        P(None, None, "lat", "lon"),
    )
    return jax.shard_map(
        body,
        mesh=mesh,
        in_specs=placed,
        out_specs=(P(None, "lat", "lon"), P(None, None, "lat", "lon"), P(None, None, "lat", "lon")),
        check_vma=False,
    )
```

```python
import functools
import math

import jax
import jax.numpy as jnp
from jax import lax
from jax.experimental import pallas as pl
from jax.experimental.pallas import tpu as pltpu
from jax.sharding import PartitionSpec as P

MESH = pl.DeviceIdType.MESH
F32, BF16 = jnp.float32, jnp.bfloat16
PAD = 16
LANES = 128
SUM_TYPE = jnp.bfloat16
PARTS = 2
GRANT = 56 * 1024 * 1024


def up(value, unit):
    return -(-value // unit) * unit


def gelu_parts(h):
    k = math.sqrt(2.0 / math.pi)
    tanh_part = jnp.tanh(k * (h + 0.044715 * h * h * h))
    value = 0.5 * h * (1.0 + tanh_part)
    slope = 0.5 * (1.0 + tanh_part) + 0.5 * h * (1.0 - tanh_part * tanh_part) * k * (
        1.0 + 3.0 * 0.044715 * h * h
    )
    return (value, slope)


def dot(a, b):
    return lax.dot_general(a, b, (((1,), (0,)), ((), ())), preferred_element_type=F32)


def dot_nt(a, b):
    return lax.dot_general(a, b, (((1,), (1,)), ((), ())), preferred_element_type=F32)


def put(tiles, lane, source, source_lane, count, target_lane):
    shift = (target_lane - source_lane) % LANES
    moved = pltpu.roll(source, shift, 1) if shift else source
    tile, off = divmod(target_lane, LANES)
    keep = (lane >= off) & (lane < off + count)
    tiles[tile] = jnp.where(keep, moved, tiles[tile])
    over = off + count - LANES
    if over > 0:
        tiles[tile + 1] = jnp.where(lane < over, moved, tiles[tile + 1])


def put_wide(tiles, lane, sources, source_lane, count, target_lane):
    while count > 0:
        tile, off = divmod(source_lane, LANES)
        part = min(count, LANES - off)
        put(tiles, lane, sources[tile], off, part, target_lane)
        source_lane, target_lane, count = source_lane + part, target_lane + part, count - part


def kernel(
    cfg,
    x_hbm, xs_hbm, h_hbm, hs_hbm, g_hbm, land_hbm, partner_hbm, w0_hbm, w1_hbm,
    out_hbm, first_hbm, second_hbm,
    out_ref, first_ref, second_ref, x_ref,
    xs_ref, h_ref, hs_ref, g_ref, land_ref, partner_ref, w0_ref, w1_ref, in_s, out_s,
    cells, slope, wtmp, wown, wtile, wrow, wfull, wt, wp, fh, act, sg, sx, gq, edge, edge_in,
    mrow, mout, mirr, gqm, spread, qs, nat, tap, given, tap_in, part, part_in, tot, small, small_in,
    turned, tapz, givenz, tapz_in, partz, partz_in, smallz, smallz_in,
    st1_s, st1_r, st2_s, st2_r, fw_s, fw_r, ha_s, ha_r, mi_s, mi_r, mo_s, mo_r,
    r0_s, r0_r, r1_s, r1_r, r2_s, r2_r, z0_s, z0_r, z1_s, z1_r, z2_s, z2_r,
):
    C, H, NJ, NI = cfg["C"], cfg["H"], cfg["NJ"], cfg["NI"]
    W = LANES
    CJ, CI, NM, NG = C // NJ, C // NI, NJ // 2, C // PAD
    LA, CL, RB = up(3 * C, LANES), up(C, LANES), up(3 * (C // NJ), PAD)
    ROWS = NJ * RB
    N = H * W
    j, i = lax.axis_index("lat"), lax.axis_index("lon")
    k, m = lax.rem(j, 2), lax.div(j, 2)
    top = j == NJ - 1
    bottom = j == 0
    worker = top & (i < NG)

    def rcopy(src, dst, ss, rs, dj, di):
        return pltpu.make_async_remote_copy(
            src_ref=src, dst_ref=dst, send_sem=ss, recv_sem=rs,
            device_id={"lat": dj, "lon": di}, device_id_type=MESH,
        )

    def each(lo, hi, fn):
        lax.fori_loop(lo, hi, lambda d, c: (fn(d), c)[1], 0)

    def lon(d):
        return jnp.bitwise_xor(i, d)

    def lat(d):
        return jnp.bitwise_xor(j, d)

    def mate(d):
        return jnp.bitwise_xor(m, d)

    def beside(axis, place, d):
        return lax.rem(place + d + axis, axis)

    lon_order = [d for d in (9, 8, 11, 10, 7, 6, 15, 14, 5, 13, 4, 12, 3, 2, 1) if d < NI]
    lat_order = [d for d in (12, 13, 10, 11, 14, 15, 8, 9, 4, 5, 2, 3, 6, 7, 1) if d < NJ]
    mate_order = [d for d in (6, 5, 7, 4, 2, 1, 3) if d < NM]

    barrier = pltpu.get_barrier_semaphore()

    def greet(dj, di):
        pl.semaphore_signal(barrier, inc=1, device_id={"lat": dj, "lon": di}, device_id_type=MESH)

    for d in lon_order:
        greet(j, lon(d))
    for d in lat_order:
        greet(lat(d), i)
    for dj in (1, -1):
        for di in (1, -1):
            greet(beside(NJ, j, dj), beside(NI, i, di))
    loads = [
        pltpu.make_async_copy(src, dst, in_s.at[n])
        for n, (src, dst) in enumerate((
            (w1_hbm, w1_ref), (w0_hbm, w0_ref), (land_hbm, land_ref), (g_hbm, g_ref), (xs_hbm, xs_ref),
            (x_hbm, x_ref), (hs_hbm, hs_ref), (h_hbm, h_ref), (partner_hbm, partner_ref)))
    ]
    for load in loads:
        load.start()

    loads[0].wait()

    def make_tile(ref):
        wtmp[...] = jnp.zeros(wtmp.shape, F32)
        for a in range(3):
            block = ref[a].astype(F32)
            for b in range(3):
                wtmp[3 * a + b, 0:CJ, 0:CI] = block[:, b, :]
        value = wtmp[0]
        for n in range(1, 9):
            value = value + pltpu.roll(wtmp[n], n * CI, 1)
        return value

    wown[1] = make_tile(w1_ref).astype(BF16)

    def blocks(ref):
        cells[...] = ref[...].astype(F32).reshape(C * H, W)
        return [cells[pl.ds(r, C, stride=H), :] for r in range(H)]

    def ocean(r):
        return land_ref[r:r + 1, :].astype(F32)

    def slot(r):
        return pl.ds((r + 1) * W, W)

    lane = lax.broadcasted_iota(jnp.int32, (C, W), 1)
    center = pl.ds(C, C)
    fy = sg.at[center]

    def add_edges(packed, f, r, blk):
        spots = [f * 8 + r]
        if r == H - 1:
            spots.append(32 + f)
        if r == 0:
            spots.append(48 + f)
        for spot in spots:
            packed = jnp.where(lane == spot, pltpu.roll(blk, spot, 1) if spot else blk, packed)
            packed = jnp.where(lane == 64 + spot, pltpu.roll(blk, 65 + spot, 1), packed)
        return packed

    def turn_edges(phase, packed):
        if CL > C:
            packed = jnp.concatenate([packed, jnp.zeros((CL - C, W), F32)], axis=0)
        edge[phase] = jnp.transpose(packed).astype(BF16)

    for load in loads[2:6]:
        load.wait()
    scale = jnp.transpose(xs_ref[...])
    packed = jnp.zeros((C, W), F32)
    for r, blk in enumerate(blocks(g_ref)):
        value = blk * ocean(r)
        fy[:, slot(r)] = value.astype(BF16)
        packed = add_edges(packed, 0, r, value)
    for r, blk in enumerate(blocks(x_ref)):
        x = (blk * scale[:, r:r + 1]).astype(BF16)
        sx[center, slot(r)] = x
        packed = add_edges(packed, 1, r, x.astype(F32))

    pl.semaphore_wait(barrier, NI - 1 + NJ - 1 + 4)

    def tile_copy(w, d, other):
        return rcopy(wown.at[w], wtile.at[w, i if other is None else other],
                     st1_s.at[w, d], st1_r.at[w, d], j, lon(d))

    for d in lon_order:
        tile_copy(1, d, None).start()
    wtile[1, i] = wown[1]
    def row_copy(phase, src, d, other):
        g = lon(d) if other is None else i
        return rcopy(src.at[pl.ds(pl.multiple_of(g * PAD, PAD), PAD), slot(H - 1)],
                     mrow.at[phase, i if other is None else other],
                     mi_s.at[phase, d], mi_r.at[phase, d], j, lon(d))

    def turned_copy(phase, d, other):
        return rcopy(mout.at[phase, lon(d)], mirr.at[phase, i if other is None else other],
                     mo_s.at[phase, d], mo_r.at[phase, d], j, lon(d))

    def mirror_send(phase, src):
        @pl.when(top)
        def _():
            for d in lon_order:
                @pl.when(lon(d) < NG)
                def _():
                    row_copy(phase, src, d, None).start()

            @pl.when(i < NG)
            def _():
                mrow[phase, i] = src[pl.ds(pl.multiple_of(i * PAD, PAD), PAD), slot(H - 1)]

    def mirror_turn(phase, src):
        @pl.when(worker)
        def _():
            ncols = NI * W
            flip = (lax.broadcasted_iota(jnp.int32, (W, W), 0)
                    + lax.broadcasted_iota(jnp.int32, (W, W), 1)) == W - 1
            flip = jnp.where(flip, 1.0, 0.0).astype(BF16)
            tlane = lax.broadcasted_iota(jnp.int32, (PAD, W), 1)
            where = partner_ref[pl.ds(i, 1), :] + lax.broadcasted_iota(jnp.int32, (1, W), 1) + i * W
            turn = (ncols - 1) - (where & (ncols - 1))
            turn = jnp.broadcast_to(turn, (PAD, W))

            def left(tiles, by):
                if by % W == 0:
                    return [tiles[(t + by // W) % NI] for t in range(NI)]
                moved = [pltpu.roll(tile, W - by, 1) for tile in tiles]
                return [jnp.where(tlane < W - by, moved[t], moved[(t + 1) % NI]) for t in range(NI)]

            each(1, NI, lambda d: row_copy(phase, src, d, lon(d)).wait_recv())
            rev = dot(mrow[phase].reshape(NI * PAD, W), flip)
            tiles = [rev[(NI - 1 - v) * PAD:(NI - v) * PAD] for v in range(NI)]
            for bit in range(ncols.bit_length() - 1):
                take = (turn & (1 << bit)) != 0
                tiles = [jnp.where(take, new, old) for new, old in zip(left(tiles, 1 << bit), tiles)]
            for t in range(NI):
                before, after = pltpu.roll(tiles[t - 1], 1, 1), pltpu.roll(tiles[(t + 1) % NI], 1, 1)
                mout[phase, t, 0] = tiles[t].astype(BF16)
                mout[phase, t, 1] = jnp.where(tlane == 0, before, after).astype(BF16)
            mirr[phase, i] = mout[phase, i]
            for d in lon_order:
                turned_copy(phase, d, None).start()

    def mirror_wait(phase):
        def step(d):
            @pl.when(lon(d) < NG)
            def _():
                turned_copy(phase, d, lon(d)).wait_recv()

        each(1, NI, step)

    def mirrored(phase):
        block = mirr[phase, :, 0].reshape(C, W).astype(F32)
        edges = mirr[phase, :, 1].reshape(C, W).astype(F32)
        before = jnp.where(lane == 0, edges, pltpu.roll(block, 1, 1))
        after = jnp.where(lane == W - 1, pltpu.roll(edges, W - 2, 1), pltpu.roll(block, W - 1, 1))
        return jnp.concatenate([before, block, after], axis=1).astype(BF16)

    mirror_send(0, fy)
    loads[1].wait()
    wown[0] = make_tile(w0_ref).astype(BF16)

    for load in loads[6:]:
        load.wait()
    scale = jnp.transpose(hs_ref[...])
    for r, blk in enumerate(blocks(h_ref)):
        h = blk * scale[:, r:r + 1]
        value, deriv = gelu_parts(h)
        act[:, r * W:(r + 1) * W] = (ocean(r) * value).astype(BF16)
        slope[:, r * W:(r + 1) * W] = deriv
    turn_edges(0, packed)

    def halo_copies(phase, fields):
        north, south = jnp.logical_not(top), jnp.logical_not(bottom)
        out = []
        for f, field in enumerate(fields):
            s = 2 * f
            out.append((rcopy(field.at[:, slot(H - 1)], field.at[:, slot(-1)],
                              ha_s.at[phase, s], ha_r.at[phase, s], beside(NJ, j, 1), i), north, south))
            out.append((rcopy(field.at[:, slot(0)], field.at[:, slot(H)],
                              ha_s.at[phase, s + 1], ha_r.at[phase, s + 1], beside(NJ, j, -1), i), south, north))
        side = up(8 * len(fields), PAD)
        n = 6
        for di, base, target in ((1, 64, 0), (-1, 0, 64)):
            for dj, off, size in ((0, 0, side), (1, 32, PAD), (-1, 48, PAD)):
                sent, comes = {0: (None, None), 1: (north, south), -1: (south, north)}[dj]
                out.append((rcopy(edge.at[phase, pl.ds(base + off, size)],
                                  edge_in.at[phase, pl.ds(target + off, size)],
                                  ha_s.at[phase, n], ha_r.at[phase, n],
                                  beside(NJ, j, dj), beside(NI, i, di)), sent, comes))
                n += 1
        return out

    def only(condition, fn):
        if condition is None:
            fn()
        else:
            pl.when(condition)(fn)

    def halo_start(copies):
        for copy, sent, _ in copies:
            only(sent, copy.start)

    def halo_wait(copies):
        for copy, _, comes in copies:
            only(comes, copy.wait_recv)

    def halo_sent(copies):
        for copy, sent, _ in copies:
            only(sent, copy.wait_send)

    early = halo_copies(0, (fy, sx.at[center]))
    halo_start(early)

    mirror_send(2, sx.at[center])
    for d in lon_order:
        tile_copy(0, d, None).start()
    wtile[0, i] = wown[0]
    at = lax.broadcasted_iota(jnp.int32, (ROWS, 1), 0)
    half, rest = lax.div(at, NM * RB), lax.rem(at, NM * RB)
    own = lax.rem(rest, RB)
    line = lax.div(own, CJ)
    target = line * C + (2 * lax.div(rest, RB) + half) * CJ + own - line * CJ
    target = jnp.where(own < 3 * CJ, target, -1)
    spread[...] = jnp.where(lax.broadcasted_iota(jnp.int32, (ROWS, 3 * C), 1) == target, 1.0, 0.0).astype(BF16)

    def make_slab(w):
        each(1, NI, lambda d: tile_copy(w, d, lon(d)).wait_recv())
        wlane = lax.broadcasted_iota(jnp.int32, (PAD, W), 1)
        tot[...] = jnp.zeros(tot.shape, F32)
        pieces = [wtile[w, s].astype(F32) for s in range(NI)]
        for a in range(3):
            tiles = [jnp.zeros((PAD, W), F32) for _ in range(LA // W)]
            for s in range(NI):
                for b in range(3):
                    put(tiles, wlane, pieces[s], (3 * a + b) * CI, CI, b * C + s * CI)
            for t, value in enumerate(tiles):
                tot[a * CJ:(a + 1) * CJ, t * W:(t + 1) * W] = value[:CJ]
        wrow[w] = tot[0:RB].astype(BF16)

    def slab_copy(w, d, other):
        return rcopy(wrow.at[w], wfull.at[w, k, m if other is None else other],
                     st2_s.at[w, d], st2_r.at[w, d], 2 * mate(d) + k, i)

    def forward_copy(w, d, mine):
        n = mate(d)
        return rcopy(wfull.at[w, k, n], wfull.at[w, k if mine else 1 - k, n],
                     fw_s.at[w, d], fw_r.at[w, d], j + 1 - 2 * k, i)

    def own_forward(w, mine):
        return rcopy(wrow.at[w], wfull.at[w, k if mine else 1 - k, m], fw_s.at[w, 0], fw_r.at[w, 0],
                     j + 1 - 2 * k, i)

    def send_slab(w):
        for d in mate_order:
            slab_copy(w, d, None).start()
        own_forward(w, True).start()
        wfull[w, k, m] = wrow[w]

    def pass_on(w):
        def step(d):
            slab_copy(w, d, mate(d)).wait_recv()
            forward_copy(w, d, True).start()

        each(1, NM, step)

    def have_weights(w):
        own_forward(w, False).wait_recv()
        each(1, NM, lambda d: forward_copy(w, d, False).wait_recv())
        wt[...] = jnp.transpose(wfull[w].reshape(ROWS, LA).astype(F32)).astype(BF16)

    def columns(got, f):
        result = []
        for base in (0, 64):
            start = base + f * 8
            value = jnp.where((lane >= 1) & (lane <= H), pltpu.roll(got, (1 - start) % W, 1), 0.0)
            lower = pltpu.roll(got, (-(base + 32 + f)) % W, 1)
            upper = pltpu.roll(got, (H + 1 - (base + 48 + f)) % W, 1)
            value = jnp.where((lane == 0) & jnp.logical_not(bottom), lower, value)
            value = jnp.where((lane == H + 1) & jnp.logical_not(top), upper, value)
            result.append(value)
        return result

    def turned_edges(phase):
        return jnp.transpose(edge_in[phase].astype(F32))[:C]

    def clear_ends(field):
        @pl.when(bottom)
        def _():
            field[:, slot(-1)] = jnp.zeros((C, W), BF16)

        @pl.when(top)
        def _():
            field[:, slot(H)] = jnp.zeros((C, W), BF16)

    def shifted(field, west, east):
        for r in range(-1, H + 1):
            blk = field[center, slot(r)].astype(F32)
            lower = jnp.where(lane == 0, pltpu.roll(west, (-(r + 1)) % W, 1), pltpu.roll(blk, 1, 1))
            upper = jnp.where(lane == W - 1, pltpu.roll(east, (W - 2 - r) % W, 1), pltpu.roll(blk, W - 1, 1))
            field[0:C, slot(r)] = lower.astype(BF16)
            field[2 * C:3 * C, slot(r)] = upper.astype(BF16)
        if LA > 3 * C:
            field[3 * C:LA, :] = jnp.zeros((LA - 3 * C, (H + 2) * W), BF16)

    def tap_rows(field, n, size):
        return jnp.concatenate([field[:, (2 - a) * W + n:(2 - a) * W + n + size] for a in range(3)], axis=0)

    def edge_rows(west, east):
        both = []
        for a in range(3):
            at_west = pltpu.roll(west, (a - 2) % W, 1)
            at_east = pltpu.roll(east, (H + a - 2) % W, 1)
            value = jnp.where(lane < H, at_west, jnp.where(lane < 2 * H, at_east, 0.0))
            both.append(value.astype(BF16))
        return jnp.concatenate(both, axis=0)

    def fold_rows(mirror):
        return jnp.concatenate([jnp.zeros((2 * C, 3 * W), BF16), mirror], axis=0)

    step = min(2 * W, N)

    def tap_grad(grad, field):
        for a in range(3):
            nat[a * C:(a + 1) * C, :] = dot_nt(grad[:, W:W + N], field[:, a * W:a * W + N])

    def tap_store():
        for a in range(3):
            for jj in range(NJ):
                tap[jj % 2, jj // 2, a * CJ:(a + 1) * CJ, :] = nat[a * C + jj * CJ:a * C + (jj + 1) * CJ, :]

    def side_store():
        for a in range(3):
            for s in range(NI):
                tapz[s, a * CI:(a + 1) * CI, :] = nat[a * C + s * CI:a * C + (s + 1) * CI, :]

    def add_fold(weight, rows):
        share = dot(weight[0:C, :], rows[:, 0:W])
        for b in (1, 2):
            share = share + dot(weight[b * C:(b + 1) * C, :], rows[:, b * W:(b + 1) * W])
        qs[C:2 * C, N - W:N] += share

    def shift_sum():
        first, last = qs[0:C, N:N + W], qs[2 * C:3 * C, N:N + W]
        result = []
        for r in range(H):
            at = slice(r * W, (r + 1) * W)
            left = jnp.where(lane == W - 1, pltpu.roll(first, (W - 1 - H - r) % W, 1),
                             pltpu.roll(qs[0:C, at], W - 1, 1))
            right = jnp.where(lane == 0, pltpu.roll(last, (-r) % W, 1), pltpu.roll(qs[2 * C:3 * C, at], 1, 1))
            result.append(qs[C:2 * C, at] + left + right)
        return result

    def pair_copy(n):
        return rcopy(given.at[n], tap_in.at[n], r0_s.at[n], r0_r.at[n], j + 1 - 2 * k, i)

    def chip_copy(d, other):
        return rcopy(part.at[mate(d)], part_in.at[m if other is None else other],
                     r1_s.at[d], r1_r.at[d], 2 * mate(d) + k, i)

    def lon_copy(d, other):
        return rcopy(small.at[lon(d)], small_in.at[i if other is None else other], r2_s.at[d], r2_r.at[d], j, lon(d))

    def sum_start():
        given[...] = tap[1 - k].astype(SUM_TYPE)
        for d in mate_order:
            pair_copy(mate(d)).start()
        pair_copy(m).start()

    def sum_chips():
        for d in mate_order:
            n = mate(d)
            pair_copy(n).wait_recv()
            part[n] = (tap[k, n] + tap_in[n].astype(F32)).astype(SUM_TYPE)
            chip_copy(d, None).start()
        pair_copy(m).wait_recv()

    def sum_lon():
        total = tap[k, m] + tap_in[m].astype(F32)
        for d in range(1, NM):
            chip_copy(d, mate(d)).wait_recv()
            total = total + part_in[mate(d)].astype(F32)
        tot[0:RB] = total
        slane = lax.broadcasted_iota(jnp.int32, (PAD, W), 1)
        sources = [[tot[a * CJ:a * CJ + PAD, t * W:(t + 1) * W] for t in range(LA // W)] for a in range(3)]
        for s in range(NI):
            tiles = [jnp.zeros((PAD, W), F32)]
            for a in range(3):
                for b in range(3):
                    put_wide(tiles, slane, sources[a], b * C + s * CI, CI, (3 * a + b) * CI)
            small[s] = tiles[0].astype(SUM_TYPE)
        small_in[i] = small[i]
        for d in lon_order:
            lon_copy(d, None).start()

    def sum_end():
        each(1, NI, lambda d: lon_copy(d, lon(d)).wait_recv())
        total = small_in[0].astype(F32)
        for s in range(1, NI):
            total = total + small_in[s].astype(F32)
        total = total * cfg["factor"]
        for a in range(3):
            for b in range(3):
                n = 3 * a + b
                moved = pltpu.roll(total, (-n * CI) % W, 1) if n else total
                first_ref[a, :, b, :] = moved[:CJ, :CI]

    HR = RB // 2
    mine = pl.ds(pl.multiple_of(k * HR, HR), HR)
    others = pl.ds(pl.multiple_of((1 - k) * HR, HR), HR)

    def side_pair():
        return rcopy(givenz, tapz_in, z0_s, z0_r, j + 1 - 2 * k, i)

    def side_lon(d, other):
        return rcopy(partz.at[lon(d)], partz_in.at[i if other is None else other], z1_s.at[d], z1_r.at[d], j, lon(d))

    def side_lat(d, other):
        return rcopy(smallz.at[lat(d)], smallz_in.at[j if other is None else other], z2_s.at[d], z2_r.at[d], lat(d), i)

    def side_start():
        givenz[...] = tapz[:, others].astype(SUM_TYPE)
        side_pair().start()

    def side_sum_lon():
        side_pair().wait_recv()
        for s in range(NI):
            partz[s] = (tapz[s, mine] + tapz_in[s].astype(F32)).astype(SUM_TYPE)
        side_send(1)

    def side_send(odd):
        for d in lon_order:
            if d % 2 == odd:
                side_lon(d, None).start()

    def side_sum_lat():
        total = tapz[i, mine] + tapz_in[i].astype(F32)
        for d in range(1, NI):
            side_lon(d, lon(d)).wait_recv()
            total = total + partz_in[lon(d)].astype(F32)
        slane = lax.broadcasted_iota(jnp.int32, (HR, W), 1)
        sources = [total[:, t * W:(t + 1) * W] for t in range(LA // W)]
        for s in range(NJ):
            tiles = [jnp.zeros((HR, W), F32)]
            for a in range(3):
                put_wide(tiles, slane, sources, a * C + s * CJ, CJ, a * CJ)
            smallz[s] = tiles[0]
        smallz_in[j] = smallz[j]
        for d in lat_order:
            side_lat(d, None).start()

    def side_end():
        each(1, NJ, lambda d: side_lat(d, lat(d)).wait_recv())
        halves = []
        for h in range(2):
            total = smallz_in[h]
            for s in range(h + 2, NJ, 2):
                total = total + smallz_in[s]
            halves.append(total)
        total = jnp.concatenate(halves + [jnp.zeros((W - RB, W), F32)], axis=0) * cfg["factor"]
        turned[...] = jnp.transpose(total)
        for b in range(3):
            block = turned[(2 - b) * CJ:(3 - b) * CJ, :]
            for a in range(3):
                moved = pltpu.roll(block, (-a * CI) % W, 1) if a else block
                second_ref[a, :, b, :] = moved[:, :CI]

    make_slab(1)
    send_slab(1)
    mirror_turn(0, fy)
    tap[:, :, 3 * CJ:RB, :] = jnp.zeros((2, NM, RB - 3 * CJ, LA), F32)
    tapz[:, 3 * CI:RB, :] = jnp.zeros((NI, RB - 3 * CI, LA), F32)

    halo_wait(early)
    clear_ends(fy)
    clear_ends(sx.at[center])
    got = turned_edges(0)
    west, east = columns(got, 0)
    for n in range(0, N, step):
        gq[:, n:n + step] = dot(spread[...], tap_rows(fy, n, step)).astype(BF16)
    gq[:, N:N + W] = dot(spread[...], edge_rows(west, east)).astype(BF16)
    mirror_turn(2, sx.at[center])
    shifted(sg, west, east)
    west, east = columns(got, 1)
    shifted(sx, west, east)
    for a in range(3):
        nat[a * C:(a + 1) * C, :] = dot_nt(act[...], sg[:, (2 - a) * W:(2 - a) * W + N])
    make_slab(0)
    pass_on(1)
    send_slab(0)
    side_store()
    @pl.when(top)
    def _():
        mirror_wait(0)
        mirror = mirrored(0)
        stacked = jnp.concatenate([mirror[:, 2 * W:3 * W], mirror[:, W:2 * W], mirror[:, 0:W],
                                   jnp.zeros((LA - 3 * C, W), BF16)], axis=0)
        nat[0:C, :] = dot_nt(act[:, N - W:N], stacked)
        for s in range(NI):
            tapz[s, 2 * CI:3 * CI, :] += nat[s * CI:(s + 1) * CI, :]
        gqm[...] = dot(spread[...], fold_rows(mirror)).astype(BF16)

    side_start()
    have_weights(1)
    for n in range(0, N + W, step):
        size = min(step, N + W - n)
        qs[:, n:n + size] = dot(wt[...], gq[:, n:n + size])

    side_sum_lon()

    @pl.when(m != NM - 1)
    def _():
        side_send(0)

    @pl.when(top)
    def _():
        add_fold(wt, gqm)
        mirror_wait(2)
        north = mirrored(2)
        for b in range(3):
            sx[b * C:(b + 1) * C, slot(H)] = north[:, b * W:(b + 1) * W]

    for r, value in enumerate(shift_sum()):
        fh[:, slot(r)] = (value * ocean(r) * slope[:, r * W:(r + 1) * W]).astype(BF16)

    mirror_send(1, fh)

    @pl.when(m == NM - 1)
    def _():
        side_send(0)

    tap_grad(fh, sx)
    tap_store()
    sum_start()
    packed = jnp.zeros((C, W), F32)
    for r in range(H):
        packed = add_edges(packed, 0, r, fh[:, slot(r)].astype(F32))
    turn_edges(1, packed)
    late = halo_copies(1, (fh,))
    halo_start(late)
    sum_chips()


    pass_on(0)
    have_weights(0)
    wp[...] = dot(wt[...], spread[...]).astype(BF16)
    mirror_turn(1, fh)
    side_sum_lat()
    sum_lon()

    halo_wait(late)
    clear_ends(fh)
    west, east = columns(turned_edges(1), 0)
    for n in range(0, N, step):
        qs[:, n:n + step] = dot(wp[...], tap_rows(fh, n, step))
    qs[:, N:N + W] = dot(wp[...], edge_rows(west, east))

    @pl.when(top)
    def _():
        mirror_wait(1)
        add_fold(wp, fold_rows(mirrored(1)))

    cells[...] = g_ref[...].astype(F32).reshape(C * H, W)
    for r, value in enumerate(shift_sum()):
        at = pl.ds(r, C, stride=H)
        out_ref[at, :] = cells[at, :] + value
    results = [
        pltpu.make_async_copy(src, dst, out_s.at[n])
        for n, (src, dst) in enumerate(((out_ref, out_hbm), (second_ref, second_hbm), (first_ref, first_hbm)))
    ]
    results[0].start()

    halo_sent(early + late)
    for w in range(2):
        each(1, NI, lambda d: tile_copy(w, d, None).wait_send())
        own_forward(w, True).wait_send()
        each(1, NM, lambda d: slab_copy(w, d, None).wait_send())
        each(1, NM, lambda d: forward_copy(w, d, True).wait_send())
    each(0, NM, lambda n: pair_copy(n).wait_send())
    each(1, NM, lambda d: chip_copy(d, None).wait_send())
    side_pair().wait_send()
    each(1, NI, lambda d: side_lon(d, None).wait_send())

    @pl.when(top)
    def _():
        for phase in range(3):
            def sent(d):
                @pl.when(lon(d) < NG)
                def _():
                    row_copy(phase, fy, d, None).wait_send()

            each(1, NI, sent)

    @pl.when(worker)
    def _():
        for phase in range(3):
            each(1, NI, lambda d: turned_copy(phase, d, None).wait_send())

    side_end()
    results[1].start()
    sum_end()
    results[2].start()
    each(1, NI, lambda d: lon_copy(d, None).wait_send())
    each(1, NJ, lambda d: side_lat(d, None).wait_send())
    for result in results:
        result.wait()


def hand_over(out_in, first_in, second_in, out_ref, first_ref, second_ref, out_mid, first_mid, second_mid, came, went):
    size = out_in.shape[0] // PARTS
    ways = [(out_in.at[pl.ds(n * size, size)], out_mid.at[pl.ds(n * size, size)], out_ref.at[pl.ds(n * size, size)])
            for n in range(PARTS)]
    ways += [(first_in, first_mid, first_ref), (second_in, second_mid, second_ref)]
    first = [pltpu.make_async_copy(a, b, came.at[n]) for n, (a, b, _) in enumerate(ways)]
    then = [pltpu.make_async_copy(b, c, went.at[n]) for n, (_, b, c) in enumerate(ways)]
    for copy in first:
        copy.start()
    for copy, following in zip(first, then):
        copy.wait()
        following.start()
    for copy in then:
        copy.wait()


def body(x_codes, x_scale, h_codes, h_scale, grad_out, land, partner, w_first, w_second):
    C, H, W = x_codes.shape
    NJ, NI = lax.axis_size("lat"), lax.axis_size("lon")
    CJ, CI, NM = C // NJ, C // NI, NJ // 2
    LA, CL, RB, N = up(3 * C, LANES), up(C, LANES), up(3 * CJ, PAD), H * W
    ROWS = NJ * RB
    cfg = {"C": C, "H": H, "NJ": NJ, "NI": NI, "factor": 1.0 / math.sqrt(NJ * H * NI * W)}
    sem = pltpu.SemaphoreType.DMA
    vm = pltpu.VMEM
    args = (x_codes, x_scale.T, h_codes, h_scale.T, grad_out, land, partner.reshape(NI, W),
            w_first.transpose(0, 2, 1, 3), w_second.transpose(0, 2, 1, 3))
    shapes = (
        jax.ShapeDtypeStruct((C * H, W), F32),
        jax.ShapeDtypeStruct((3, CJ, 3, CI), F32),
        jax.ShapeDtypeStruct((3, CJ, 3, CI), F32),
    )
    scratch = [vm(arg.shape, arg.dtype) for arg in shapes + args] + [
        sem((9,)), sem((3,)),
        vm((C * H, W), F32),
        vm((C, N), F32),
        vm((9, PAD, LANES), F32),
        vm((2, PAD, LANES), BF16),
        vm((2, NI, PAD, LANES), BF16),
        vm((2, RB, LA), BF16),
        vm((2, 2, NM, RB, LA), BF16),
        vm((LA, ROWS), BF16),
        vm((LA, 3 * C), BF16),
        vm((C, N + 2 * W), BF16),
        vm((C, N), BF16),
        vm((LA, N + 2 * W), BF16),
        vm((LA, N + 2 * W), BF16),
        vm((ROWS, N + W), BF16),
        vm((2, W, CL), BF16),
        vm((2, W, CL), BF16),
        vm((3, NI, PAD, W), BF16),
        vm((3, NI, 2, PAD, W), BF16),
        vm((3, C // PAD, 2, PAD, W), BF16),
        vm((ROWS, 3 * W), BF16),
        vm((ROWS, 3 * C), BF16),
        vm((LA, N + W), F32),
        vm((3 * C, LA), F32),
        vm((2, NM, RB, LA), F32),
        vm((NM, RB, LA), SUM_TYPE),
        vm((NM, RB, LA), SUM_TYPE),
        vm((NM, RB, LA), SUM_TYPE),
        vm((NM, RB, LA), SUM_TYPE),
        vm((RB + PAD, LA), F32),
        vm((NI, PAD, LANES), SUM_TYPE),
        vm((NI, PAD, LANES), SUM_TYPE),
        vm((LANES, LANES), F32),
        vm((NI, RB, LA), F32),
        vm((NI, RB // 2, LA), SUM_TYPE),
        vm((NI, RB // 2, LA), SUM_TYPE),
        vm((NI, RB // 2, LA), SUM_TYPE),
        vm((NI, RB // 2, LA), SUM_TYPE),
        vm((NJ, RB // 2, LANES), F32),
        vm((NJ, RB // 2, LANES), F32),
        sem((2, NI)), sem((2, NI)), sem((2, NM)), sem((2, NM)), sem((2, NM)), sem((2, NM)),
        sem((2, 12)), sem((2, 12)), sem((3, NI)), sem((3, NI)), sem((3, NI)), sem((3, NI)),
        sem((NM,)), sem((NM,)), sem((NM,)), sem((NM,)), sem((NI,)), sem((NI,)),
        sem, sem, sem((NI,)), sem((NI,)), sem((NJ,)), sem((NJ,)),
    ]
    results = pl.pallas_call(
        functools.partial(kernel, cfg),
        out_shape=shapes,
        in_specs=[pl.BlockSpec(memory_space=pl.ANY)] * 9,
        out_specs=[pl.BlockSpec(memory_space=pl.ANY)] * 3,
        scratch_shapes=scratch,
        compiler_params=pltpu.CompilerParams(
            collective_id=0, has_side_effects=True, vmem_limit_bytes=GRANT
        ),
    )(*args)
    grad_in, first, second = pl.pallas_call(
        hand_over,
        out_shape=shapes,
        in_specs=[pl.BlockSpec(memory_space=pl.ANY)] * 3,
        out_specs=[pl.BlockSpec(memory_space=pl.ANY)] * 3,
        scratch_shapes=[vm(arg.shape, arg.dtype) for arg in shapes] + [sem((PARTS + 2,))] * 2,
        compiler_params=pltpu.CompilerParams(vmem_limit_bytes=GRANT),
    )(*results)
    return (grad_in.reshape(C, H, W), first.transpose(0, 2, 1, 3), second.transpose(0, 2, 1, 3))


def solution(mesh):
    placed = (
        P(None, "lat", "lon"),
        P(None, "lat"),
        P(None, "lat", "lon"),
        P(None, "lat"),
        P(None, "lat", "lon"),
        P("lat", "lon"),
        P(),
        P(None, None, "lat", "lon"),
        P(None, None, "lat", "lon"),
    )
    return jax.shard_map(
        body,
        mesh=mesh,
        in_specs=placed,
        out_specs=(P(None, "lat", "lon"), P(None, None, "lat", "lon"), P(None, None, "lat", "lon")),
        check_vma=False,
    )
```

```python
import functools
import math

import jax
import jax.numpy as jnp
from jax import lax
from jax.experimental import pallas as pl
from jax.experimental.pallas import tpu as pltpu
from jax.sharding import PartitionSpec as P

MESH = pl.DeviceIdType.MESH
F32, BF16 = jnp.float32, jnp.bfloat16
PAD = 16
LANES = 128
SUM_TYPE = jnp.bfloat16
PARTS = 2
GRANT = 56 * 1024 * 1024


def up(value, unit):
    return -(-value // unit) * unit


def gelu_parts(h):
    k = math.sqrt(2.0 / math.pi)
    tanh_part = jnp.tanh(k * (h + 0.044715 * h * h * h))
    value = 0.5 * h * (1.0 + tanh_part)
    slope = 0.5 * (1.0 + tanh_part) + 0.5 * h * (1.0 - tanh_part * tanh_part) * k * (
        1.0 + 3.0 * 0.044715 * h * h
    )
    return (value, slope)


def dot(a, b):
    return lax.dot_general(a, b, (((1,), (0,)), ((), ())), preferred_element_type=F32)


def dot_nt(a, b):
    return lax.dot_general(a, b, (((1,), (1,)), ((), ())), preferred_element_type=F32)


def put(tiles, lane, source, source_lane, count, target_lane):
    shift = (target_lane - source_lane) % LANES
    moved = pltpu.roll(source, shift, 1) if shift else source
    tile, off = divmod(target_lane, LANES)
    keep = (lane >= off) & (lane < off + count)
    tiles[tile] = jnp.where(keep, moved, tiles[tile])
    over = off + count - LANES
    if over > 0:
        tiles[tile + 1] = jnp.where(lane < over, moved, tiles[tile + 1])


def put_wide(tiles, lane, sources, source_lane, count, target_lane):
    while count > 0:
        tile, off = divmod(source_lane, LANES)
        part = min(count, LANES - off)
        put(tiles, lane, sources[tile], off, part, target_lane)
        source_lane, target_lane, count = source_lane + part, target_lane + part, count - part


def kernel(
    cfg,
    x_hbm, xs_hbm, h_hbm, hs_hbm, g_hbm, land_hbm, partner_hbm, w0_hbm, w1_hbm,
    out_hbm, first_hbm, second_hbm,
    out_ref, first_ref, second_ref, x_ref,
    xs_ref, h_ref, hs_ref, g_ref, land_ref, partner_ref, w0_ref, w1_ref, in_s, out_s,
    cells, slope, wtmp, wown, wtile, wrow, wfull, wt, wp, fh, act, sg, sx, gq, edge, edge_in,
    mrow, mout, mirr, gqm, spread, qs, nat, tap, given, tap_in, part, part_in, tot, small, small_in,
    turned, tapz, givenz, tapz_in, partz, partz_in, smallz, smallz_in,
    st1_s, st1_r, st2_s, st2_r, fw_s, fw_r, ha_s, ha_r, mi_s, mi_r, mo_s, mo_r,
    r0_s, r0_r, r1_s, r1_r, r2_s, r2_r, z0_s, z0_r, z1_s, z1_r, z2_s, z2_r,
):
    C, H, NJ, NI = cfg["C"], cfg["H"], cfg["NJ"], cfg["NI"]
    W = LANES
    CJ, CI, NM, NG = C // NJ, C // NI, NJ // 2, C // PAD
    LA, CL, RB = up(3 * C, LANES), up(C, LANES), up(3 * (C // NJ), PAD)
    ROWS = NJ * RB
    N = H * W
    j, i = lax.axis_index("lat"), lax.axis_index("lon")
    k, m = lax.rem(j, 2), lax.div(j, 2)
    top = j == NJ - 1
    bottom = j == 0
    worker = top & (i < NG)

    def rcopy(src, dst, ss, rs, dj, di):
        return pltpu.make_async_remote_copy(
            src_ref=src, dst_ref=dst, send_sem=ss, recv_sem=rs,
            device_id={"lat": dj, "lon": di}, device_id_type=MESH,
        )

    def each(lo, hi, fn):
        lax.fori_loop(lo, hi, lambda d, c: (fn(d), c)[1], 0)

    def lon(d):
        return jnp.bitwise_xor(i, d)

    def lat(d):
        return jnp.bitwise_xor(j, d)

    def mate(d):
        return jnp.bitwise_xor(m, d)

    def beside(axis, place, d):
        return lax.rem(place + d + axis, axis)

    lon_order = [d for d in (9, 8, 11, 10, 7, 6, 15, 14, 5, 13, 4, 12, 3, 2, 1) if d < NI]
    lat_order = [d for d in (12, 13, 10, 11, 14, 15, 8, 9, 4, 5, 2, 3, 6, 7, 1) if d < NJ]
    mate_order = [d for d in (4, 6, 5, 7, 2, 1, 3) if d < NM]

    barrier = pltpu.get_barrier_semaphore()

    def greet(dj, di):
        pl.semaphore_signal(barrier, inc=1, device_id={"lat": dj, "lon": di}, device_id_type=MESH)

    for d in lon_order:
        greet(j, lon(d))
    for d in lat_order:
        greet(lat(d), i)
    for dj in (1, -1):
        for di in (1, -1):
            greet(beside(NJ, j, dj), beside(NI, i, di))
    loads = [
        pltpu.make_async_copy(src, dst, in_s.at[n])
        for n, (src, dst) in enumerate((
            (w1_hbm, w1_ref), (w0_hbm, w0_ref), (land_hbm, land_ref), (g_hbm, g_ref), (xs_hbm, xs_ref),
            (x_hbm, x_ref), (hs_hbm, hs_ref), (h_hbm, h_ref), (partner_hbm, partner_ref)))
    ]
    for load in loads:
        load.start()

    loads[0].wait()

    def make_tile(ref):
        wtmp[...] = jnp.zeros(wtmp.shape, F32)
        for a in range(3):
            block = ref[a].astype(F32)
            for b in range(3):
                wtmp[3 * a + b, 0:CJ, 0:CI] = block[:, b, :]
        value = wtmp[0]
        for n in range(1, 9):
            value = value + pltpu.roll(wtmp[n], n * CI, 1)
        return value

    wown[1] = make_tile(w1_ref).astype(BF16)

    def blocks(ref):
        cells[...] = ref[...].astype(F32).reshape(C * H, W)
        return [cells[pl.ds(r, C, stride=H), :] for r in range(H)]

    def ocean(r):
        return land_ref[r:r + 1, :].astype(F32)

    def slot(r):
        return pl.ds((r + 1) * W, W)

    lane = lax.broadcasted_iota(jnp.int32, (C, W), 1)
    center = pl.ds(C, C)
    fy = sg.at[center]

    def add_edges(packed, f, r, blk):
        spots = [f * 8 + r]
        if r == H - 1:
            spots.append(32 + f)
        if r == 0:
            spots.append(48 + f)
        for spot in spots:
            packed = jnp.where(lane == spot, pltpu.roll(blk, spot, 1) if spot else blk, packed)
            packed = jnp.where(lane == 64 + spot, pltpu.roll(blk, 65 + spot, 1), packed)
        return packed

    def turn_edges(phase, packed):
        if CL > C:
            packed = jnp.concatenate([packed, jnp.zeros((CL - C, W), F32)], axis=0)
        edge[phase] = jnp.transpose(packed).astype(BF16)

    for load in loads[2:6]:
        load.wait()
    scale = jnp.transpose(xs_ref[...])
    packed = jnp.zeros((C, W), F32)
    for r, blk in enumerate(blocks(g_ref)):
        value = blk * ocean(r)
        fy[:, slot(r)] = value.astype(BF16)
        packed = add_edges(packed, 0, r, value)
    for r, blk in enumerate(blocks(x_ref)):
        x = (blk * scale[:, r:r + 1]).astype(BF16)
        sx[center, slot(r)] = x
        packed = add_edges(packed, 1, r, x.astype(F32))

    pl.semaphore_wait(barrier, NI - 1 + NJ - 1 + 4)

    def tile_copy(w, d, other):
        return rcopy(wown.at[w], wtile.at[w, i if other is None else other],
                     st1_s.at[w, d], st1_r.at[w, d], j, lon(d))

    for d in lon_order:
        tile_copy(1, d, None).start()
    wtile[1, i] = wown[1]
    def row_copy(phase, src, d, other):
        g = lon(d) if other is None else i
        return rcopy(src.at[pl.ds(pl.multiple_of(g * PAD, PAD), PAD), slot(H - 1)],
                     mrow.at[phase, i if other is None else other],
                     mi_s.at[phase, d], mi_r.at[phase, d], j, lon(d))

    def turned_copy(phase, d, other):
        return rcopy(mout.at[phase, lon(d)], mirr.at[phase, i if other is None else other],
                     mo_s.at[phase, d], mo_r.at[phase, d], j, lon(d))

    def mirror_send(phase, src):
        @pl.when(top)
        def _():
            for d in lon_order:
                @pl.when(lon(d) < NG)
                def _():
                    row_copy(phase, src, d, None).start()

            @pl.when(i < NG)
            def _():
                mrow[phase, i] = src[pl.ds(pl.multiple_of(i * PAD, PAD), PAD), slot(H - 1)]

    def mirror_turn(phase, src):
        @pl.when(worker)
        def _():
            ncols = NI * W
            flip = (lax.broadcasted_iota(jnp.int32, (W, W), 0)
                    + lax.broadcasted_iota(jnp.int32, (W, W), 1)) == W - 1
            flip = jnp.where(flip, 1.0, 0.0).astype(BF16)
            tlane = lax.broadcasted_iota(jnp.int32, (PAD, W), 1)
            where = partner_ref[pl.ds(i, 1), :] + lax.broadcasted_iota(jnp.int32, (1, W), 1) + i * W
            turn = (ncols - 1) - (where & (ncols - 1))
            turn = jnp.broadcast_to(turn, (PAD, W))

            def left(tiles, by):
                if by % W == 0:
                    return [tiles[(t + by // W) % NI] for t in range(NI)]
                moved = [pltpu.roll(tile, W - by, 1) for tile in tiles]
                return [jnp.where(tlane < W - by, moved[t], moved[(t + 1) % NI]) for t in range(NI)]

            each(1, NI, lambda d: row_copy(phase, src, d, lon(d)).wait_recv())
            rev = dot(mrow[phase].reshape(NI * PAD, W), flip)
            tiles = [rev[(NI - 1 - v) * PAD:(NI - v) * PAD] for v in range(NI)]
            for bit in range(ncols.bit_length() - 1):
                take = (turn & (1 << bit)) != 0
                tiles = [jnp.where(take, new, old) for new, old in zip(left(tiles, 1 << bit), tiles)]
            for t in range(NI):
                before, after = pltpu.roll(tiles[t - 1], 1, 1), pltpu.roll(tiles[(t + 1) % NI], 1, 1)
                mout[phase, t, 0] = tiles[t].astype(BF16)
                mout[phase, t, 1] = jnp.where(tlane == 0, before, after).astype(BF16)
            mirr[phase, i] = mout[phase, i]
            for d in lon_order:
                turned_copy(phase, d, None).start()

    def mirror_wait(phase):
        def step(d):
            @pl.when(lon(d) < NG)
            def _():
                turned_copy(phase, d, lon(d)).wait_recv()

        each(1, NI, step)

    def mirrored(phase):
        block = mirr[phase, :, 0].reshape(C, W).astype(F32)
        edges = mirr[phase, :, 1].reshape(C, W).astype(F32)
        before = jnp.where(lane == 0, edges, pltpu.roll(block, 1, 1))
        after = jnp.where(lane == W - 1, pltpu.roll(edges, W - 2, 1), pltpu.roll(block, W - 1, 1))
        return jnp.concatenate([before, block, after], axis=1).astype(BF16)

    mirror_send(0, fy)
    loads[1].wait()
    wown[0] = make_tile(w0_ref).astype(BF16)

    for load in loads[6:]:
        load.wait()
    scale = jnp.transpose(hs_ref[...])
    for r, blk in enumerate(blocks(h_ref)):
        h = blk * scale[:, r:r + 1]
        value, deriv = gelu_parts(h)
        act[:, r * W:(r + 1) * W] = (ocean(r) * value).astype(BF16)
        slope[:, r * W:(r + 1) * W] = deriv
    turn_edges(0, packed)

    def halo_copies(phase, fields):
        north, south = jnp.logical_not(top), jnp.logical_not(bottom)
        out = []
        for f, field in enumerate(fields):
            s = 2 * f
            out.append((rcopy(field.at[:, slot(H - 1)], field.at[:, slot(-1)],
                              ha_s.at[phase, s], ha_r.at[phase, s], beside(NJ, j, 1), i), north, south))
            out.append((rcopy(field.at[:, slot(0)], field.at[:, slot(H)],
                              ha_s.at[phase, s + 1], ha_r.at[phase, s + 1], beside(NJ, j, -1), i), south, north))
        side = up(8 * len(fields), PAD)
        n = 6
        for di, base, target in ((1, 64, 0), (-1, 0, 64)):
            for dj, off, size in ((0, 0, side), (1, 32, PAD), (-1, 48, PAD)):
                sent, comes = {0: (None, None), 1: (north, south), -1: (south, north)}[dj]
                out.append((rcopy(edge.at[phase, pl.ds(base + off, size)],
                                  edge_in.at[phase, pl.ds(target + off, size)],
                                  ha_s.at[phase, n], ha_r.at[phase, n],
                                  beside(NJ, j, dj), beside(NI, i, di)), sent, comes))
                n += 1
        return out

    def only(condition, fn):
        if condition is None:
            fn()
        else:
            pl.when(condition)(fn)

    def halo_start(copies):
        for copy, sent, _ in copies:
            only(sent, copy.start)

    def halo_wait(copies):
        for copy, _, comes in copies:
            only(comes, copy.wait_recv)

    def halo_sent(copies):
        for copy, sent, _ in copies:
            only(sent, copy.wait_send)

    early = halo_copies(0, (fy, sx.at[center]))
    halo_start(early)

    mirror_send(2, sx.at[center])
    for d in lon_order:
        tile_copy(0, d, None).start()
    wtile[0, i] = wown[0]
    at = lax.broadcasted_iota(jnp.int32, (ROWS, 1), 0)
    half, rest = lax.div(at, NM * RB), lax.rem(at, NM * RB)
    own = lax.rem(rest, RB)
    line = lax.div(own, CJ)
    target = line * C + (2 * lax.div(rest, RB) + half) * CJ + own - line * CJ
    target = jnp.where(own < 3 * CJ, target, -1)
    spread[...] = jnp.where(lax.broadcasted_iota(jnp.int32, (ROWS, 3 * C), 1) == target, 1.0, 0.0).astype(BF16)

    def make_slab(w):
        each(1, NI, lambda d: tile_copy(w, d, lon(d)).wait_recv())
        wlane = lax.broadcasted_iota(jnp.int32, (PAD, W), 1)
        tot[...] = jnp.zeros(tot.shape, F32)
        pieces = [wtile[w, s].astype(F32) for s in range(NI)]
        for a in range(3):
            tiles = [jnp.zeros((PAD, W), F32) for _ in range(LA // W)]
            for s in range(NI):
                for b in range(3):
                    put(tiles, wlane, pieces[s], (3 * a + b) * CI, CI, b * C + s * CI)
            for t, value in enumerate(tiles):
                tot[a * CJ:(a + 1) * CJ, t * W:(t + 1) * W] = value[:CJ]
        wrow[w] = tot[0:RB].astype(BF16)

    def slab_copy(w, d, other):
        return rcopy(wrow.at[w], wfull.at[w, k, m if other is None else other],
                     st2_s.at[w, d], st2_r.at[w, d], 2 * mate(d) + k, i)

    def forward_copy(w, d, mine):
        n = mate(d)
        return rcopy(wfull.at[w, k, n], wfull.at[w, k if mine else 1 - k, n],
                     fw_s.at[w, d], fw_r.at[w, d], j + 1 - 2 * k, i)

    def own_forward(w, mine):
        return rcopy(wrow.at[w], wfull.at[w, k if mine else 1 - k, m], fw_s.at[w, 0], fw_r.at[w, 0],
                     j + 1 - 2 * k, i)

    def send_slab(w):
        for d in mate_order:
            slab_copy(w, d, None).start()
        own_forward(w, True).start()
        wfull[w, k, m] = wrow[w]

    def pass_on(w):
        def step(d):
            slab_copy(w, d, mate(d)).wait_recv()
            forward_copy(w, d, True).start()

        each(1, NM, step)

    def have_weights(w):
        own_forward(w, False).wait_recv()
        each(1, NM, lambda d: forward_copy(w, d, False).wait_recv())
        wt[...] = jnp.transpose(wfull[w].reshape(ROWS, LA).astype(F32)).astype(BF16)

    def columns(got, f):
        result = []
        for base in (0, 64):
            start = base + f * 8
            value = jnp.where((lane >= 1) & (lane <= H), pltpu.roll(got, (1 - start) % W, 1), 0.0)
            lower = pltpu.roll(got, (-(base + 32 + f)) % W, 1)
            upper = pltpu.roll(got, (H + 1 - (base + 48 + f)) % W, 1)
            value = jnp.where((lane == 0) & jnp.logical_not(bottom), lower, value)
            value = jnp.where((lane == H + 1) & jnp.logical_not(top), upper, value)
            result.append(value)
        return result

    def turned_edges(phase):
        return jnp.transpose(edge_in[phase].astype(F32))[:C]

    def clear_ends(field):
        @pl.when(bottom)
        def _():
            field[:, slot(-1)] = jnp.zeros((C, W), BF16)

        @pl.when(top)
        def _():
            field[:, slot(H)] = jnp.zeros((C, W), BF16)

    def shifted(field, west, east):
        for r in range(-1, H + 1):
            blk = field[center, slot(r)].astype(F32)
            lower = jnp.where(lane == 0, pltpu.roll(west, (-(r + 1)) % W, 1), pltpu.roll(blk, 1, 1))
            upper = jnp.where(lane == W - 1, pltpu.roll(east, (W - 2 - r) % W, 1), pltpu.roll(blk, W - 1, 1))
            field[0:C, slot(r)] = lower.astype(BF16)
            field[2 * C:3 * C, slot(r)] = upper.astype(BF16)
        if LA > 3 * C:
            field[3 * C:LA, :] = jnp.zeros((LA - 3 * C, (H + 2) * W), BF16)

    def tap_rows(field, n, size):
        return jnp.concatenate([field[:, (2 - a) * W + n:(2 - a) * W + n + size] for a in range(3)], axis=0)

    def edge_rows(west, east):
        both = []
        for a in range(3):
            at_west = pltpu.roll(west, (a - 2) % W, 1)
            at_east = pltpu.roll(east, (H + a - 2) % W, 1)
            value = jnp.where(lane < H, at_west, jnp.where(lane < 2 * H, at_east, 0.0))
            both.append(value.astype(BF16))
        return jnp.concatenate(both, axis=0)

    def fold_rows(mirror):
        return jnp.concatenate([jnp.zeros((2 * C, 3 * W), BF16), mirror], axis=0)

    step = min(2 * W, N)

    def tap_grad(grad, field):
        for a in range(3):
            nat[a * C:(a + 1) * C, :] = dot_nt(grad[:, W:W + N], field[:, a * W:a * W + N])

    def tap_store():
        for a in range(3):
            for jj in range(NJ):
                tap[jj % 2, jj // 2, a * CJ:(a + 1) * CJ, :] = nat[a * C + jj * CJ:a * C + (jj + 1) * CJ, :]

    def side_store():
        for a in range(3):
            for s in range(NI):
                tapz[s, a * CI:(a + 1) * CI, :] = nat[a * C + s * CI:a * C + (s + 1) * CI, :]

    def add_fold(weight, rows):
        share = dot(weight[0:C, :], rows[:, 0:W])
        for b in (1, 2):
            share = share + dot(weight[b * C:(b + 1) * C, :], rows[:, b * W:(b + 1) * W])
        qs[C:2 * C, N - W:N] += share

    def shift_sum():
        first, last = qs[0:C, N:N + W], qs[2 * C:3 * C, N:N + W]
        result = []
        for r in range(H):
            at = slice(r * W, (r + 1) * W)
            left = jnp.where(lane == W - 1, pltpu.roll(first, (W - 1 - H - r) % W, 1),
                             pltpu.roll(qs[0:C, at], W - 1, 1))
            right = jnp.where(lane == 0, pltpu.roll(last, (-r) % W, 1), pltpu.roll(qs[2 * C:3 * C, at], 1, 1))
            result.append(qs[C:2 * C, at] + left + right)
        return result

    def pair_copy(n):
        return rcopy(given.at[n], tap_in.at[n], r0_s.at[n], r0_r.at[n], j + 1 - 2 * k, i)

    def chip_copy(d, other):
        return rcopy(part.at[mate(d)], part_in.at[m if other is None else other],
                     r1_s.at[d], r1_r.at[d], 2 * mate(d) + k, i)

    def lon_copy(d, other):
        return rcopy(small.at[lon(d)], small_in.at[i if other is None else other], r2_s.at[d], r2_r.at[d], j, lon(d))

    def sum_start():
        given[...] = tap[1 - k].astype(SUM_TYPE)
        for d in mate_order:
            pair_copy(mate(d)).start()
        pair_copy(m).start()

    def sum_chips():
        for d in mate_order:
            n = mate(d)
            pair_copy(n).wait_recv()
            part[n] = (tap[k, n] + tap_in[n].astype(F32)).astype(SUM_TYPE)
            chip_copy(d, None).start()
        pair_copy(m).wait_recv()

    def sum_lon():
        total = tap[k, m] + tap_in[m].astype(F32)
        for d in range(1, NM):
            chip_copy(d, mate(d)).wait_recv()
            total = total + part_in[mate(d)].astype(F32)
        tot[0:RB] = total
        slane = lax.broadcasted_iota(jnp.int32, (PAD, W), 1)
        sources = [[tot[a * CJ:a * CJ + PAD, t * W:(t + 1) * W] for t in range(LA // W)] for a in range(3)]
        for s in range(NI):
            tiles = [jnp.zeros((PAD, W), F32)]
            for a in range(3):
                for b in range(3):
                    put_wide(tiles, slane, sources[a], b * C + s * CI, CI, (3 * a + b) * CI)
            small[s] = tiles[0].astype(SUM_TYPE)
        small_in[i] = small[i]
        for d in sorted(lon_order, key=lambda d: d % 2 == 0):
            lon_copy(d, None).start()

    def sum_end():
        each(1, NI, lambda d: lon_copy(d, lon(d)).wait_recv())
        total = small_in[0].astype(F32)
        for s in range(1, NI):
            total = total + small_in[s].astype(F32)
        total = total * cfg["factor"]
        for a in range(3):
            for b in range(3):
                n = 3 * a + b
                moved = pltpu.roll(total, (-n * CI) % W, 1) if n else total
                first_ref[a, :, b, :] = moved[:CJ, :CI]

    HR = RB // 2
    mine = pl.ds(pl.multiple_of(k * HR, HR), HR)
    others = pl.ds(pl.multiple_of((1 - k) * HR, HR), HR)

    def side_pair():
        return rcopy(givenz, tapz_in, z0_s, z0_r, j + 1 - 2 * k, i)

    def side_lon(d, other):
        return rcopy(partz.at[lon(d)], partz_in.at[i if other is None else other], z1_s.at[d], z1_r.at[d], j, lon(d))

    def side_lat(d, other):
        return rcopy(smallz.at[lat(d)], smallz_in.at[j if other is None else other], z2_s.at[d], z2_r.at[d], lat(d), i)

    def side_start():
        givenz[...] = tapz[:, others].astype(SUM_TYPE)
        side_pair().start()

    def side_sum_lon():
        side_pair().wait_recv()
        for s in range(NI):
            partz[s] = (tapz[s, mine] + tapz_in[s].astype(F32)).astype(SUM_TYPE)
        side_send(1)

    def side_send(odd):
        for d in lon_order:
            if d % 2 == odd:
                side_lon(d, None).start()

    def side_sum_lat():
        total = tapz[i, mine] + tapz_in[i].astype(F32)
        for d in range(1, NI):
            side_lon(d, lon(d)).wait_recv()
            total = total + partz_in[lon(d)].astype(F32)
        slane = lax.broadcasted_iota(jnp.int32, (HR, W), 1)
        sources = [total[:, t * W:(t + 1) * W] for t in range(LA // W)]
        for s in range(NJ):
            tiles = [jnp.zeros((HR, W), F32)]
            for a in range(3):
                put_wide(tiles, slane, sources, a * C + s * CJ, CJ, a * CJ)
            smallz[s] = tiles[0]
        smallz_in[j] = smallz[j]
        for d in lat_order:
            side_lat(d, None).start()

    def side_end():
        each(1, NJ, lambda d: side_lat(d, lat(d)).wait_recv())
        halves = []
        for h in range(2):
            total = smallz_in[h]
            for s in range(h + 2, NJ, 2):
                total = total + smallz_in[s]
            halves.append(total)
        total = jnp.concatenate(halves + [jnp.zeros((W - RB, W), F32)], axis=0) * cfg["factor"]
        turned[...] = jnp.transpose(total)
        for b in range(3):
            block = turned[(2 - b) * CJ:(3 - b) * CJ, :]
            for a in range(3):
                moved = pltpu.roll(block, (-a * CI) % W, 1) if a else block
                second_ref[a, :, b, :] = moved[:, :CI]

    make_slab(1)
    send_slab(1)
    mirror_turn(0, fy)
    tap[:, :, 3 * CJ:RB, :] = jnp.zeros((2, NM, RB - 3 * CJ, LA), F32)
    tapz[:, 3 * CI:RB, :] = jnp.zeros((NI, RB - 3 * CI, LA), F32)

    halo_wait(early)
    clear_ends(fy)
    clear_ends(sx.at[center])
    got = turned_edges(0)
    west, east = columns(got, 0)
    for n in range(0, N, step):
        gq[:, n:n + step] = dot(spread[...], tap_rows(fy, n, step)).astype(BF16)
    gq[:, N:N + W] = dot(spread[...], edge_rows(west, east)).astype(BF16)
    mirror_turn(2, sx.at[center])
    shifted(sg, west, east)
    west, east = columns(got, 1)
    shifted(sx, west, east)
    for a in range(3):
        nat[a * C:(a + 1) * C, :] = dot_nt(act[...], sg[:, (2 - a) * W:(2 - a) * W + N])
    make_slab(0)
    pass_on(1)
    send_slab(0)
    side_store()
    @pl.when(top)
    def _():
        mirror_wait(0)
        mirror = mirrored(0)
        stacked = jnp.concatenate([mirror[:, 2 * W:3 * W], mirror[:, W:2 * W], mirror[:, 0:W],
                                   jnp.zeros((LA - 3 * C, W), BF16)], axis=0)
        nat[0:C, :] = dot_nt(act[:, N - W:N], stacked)
        for s in range(NI):
            tapz[s, 2 * CI:3 * CI, :] += nat[s * CI:(s + 1) * CI, :]
        gqm[...] = dot(spread[...], fold_rows(mirror)).astype(BF16)

    side_start()
    have_weights(1)
    for n in range(0, N + W, step):
        size = min(step, N + W - n)
        qs[:, n:n + size] = dot(wt[...], gq[:, n:n + size])

    side_sum_lon()

    @pl.when(m != NM - 1)
    def _():
        side_send(0)

    @pl.when(top)
    def _():
        add_fold(wt, gqm)
        mirror_wait(2)
        north = mirrored(2)
        for b in range(3):
            sx[b * C:(b + 1) * C, slot(H)] = north[:, b * W:(b + 1) * W]

    for r, value in enumerate(shift_sum()):
        fh[:, slot(r)] = (value * ocean(r) * slope[:, r * W:(r + 1) * W]).astype(BF16)

    mirror_send(1, fh)

    @pl.when(m == NM - 1)
    def _():
        side_send(0)

    tap_grad(fh, sx)
    tap_store()
    sum_start()
    packed = jnp.zeros((C, W), F32)
    for r in range(H):
        packed = add_edges(packed, 0, r, fh[:, slot(r)].astype(F32))
    turn_edges(1, packed)
    late = halo_copies(1, (fh,))
    sum_chips()
    halo_start(late)


    pass_on(0)
    have_weights(0)
    wp[...] = dot(wt[...], spread[...]).astype(BF16)
    mirror_turn(1, fh)
    side_sum_lat()
    sum_lon()

    halo_wait(late)
    clear_ends(fh)
    west, east = columns(turned_edges(1), 0)
    for n in range(0, N, step):
        qs[:, n:n + step] = dot(wp[...], tap_rows(fh, n, step))
    qs[:, N:N + W] = dot(wp[...], edge_rows(west, east))

    @pl.when(top)
    def _():
        mirror_wait(1)
        add_fold(wp, fold_rows(mirrored(1)))

    cells[...] = g_ref[...].astype(F32).reshape(C * H, W)
    for r, value in enumerate(shift_sum()):
        at = pl.ds(r, C, stride=H)
        out_ref[at, :] = cells[at, :] + value
    results = [
        pltpu.make_async_copy(src, dst, out_s.at[n])
        for n, (src, dst) in enumerate(((out_ref, out_hbm), (second_ref, second_hbm), (first_ref, first_hbm)))
    ]
    results[0].start()

    halo_sent(early + late)
    for w in range(2):
        each(1, NI, lambda d: tile_copy(w, d, None).wait_send())
        own_forward(w, True).wait_send()
        each(1, NM, lambda d: slab_copy(w, d, None).wait_send())
        each(1, NM, lambda d: forward_copy(w, d, True).wait_send())
    each(0, NM, lambda n: pair_copy(n).wait_send())
    each(1, NM, lambda d: chip_copy(d, None).wait_send())
    side_pair().wait_send()
    each(1, NI, lambda d: side_lon(d, None).wait_send())

    @pl.when(top)
    def _():
        for phase in range(3):
            def sent(d):
                @pl.when(lon(d) < NG)
                def _():
                    row_copy(phase, fy, d, None).wait_send()

            each(1, NI, sent)

    @pl.when(worker)
    def _():
        for phase in range(3):
            each(1, NI, lambda d: turned_copy(phase, d, None).wait_send())

    side_end()
    results[1].start()
    sum_end()
    results[2].start()
    each(1, NI, lambda d: lon_copy(d, None).wait_send())
    each(1, NJ, lambda d: side_lat(d, None).wait_send())
    for result in results:
        result.wait()


def hand_over(out_in, first_in, second_in, out_ref, first_ref, second_ref, out_mid, first_mid, second_mid, came, went):
    size = out_in.shape[0] // PARTS
    ways = [(out_in.at[pl.ds(n * size, size)], out_mid.at[pl.ds(n * size, size)], out_ref.at[pl.ds(n * size, size)])
            for n in range(PARTS)]
    ways += [(first_in, first_mid, first_ref), (second_in, second_mid, second_ref)]
    first = [pltpu.make_async_copy(a, b, came.at[n]) for n, (a, b, _) in enumerate(ways)]
    then = [pltpu.make_async_copy(b, c, went.at[n]) for n, (_, b, c) in enumerate(ways)]
    for copy in first:
        copy.start()
    for copy, following in zip(first, then):
        copy.wait()
        following.start()
    for copy in then:
        copy.wait()


def body(x_codes, x_scale, h_codes, h_scale, grad_out, land, partner, w_first, w_second):
    C, H, W = x_codes.shape
    NJ, NI = lax.axis_size("lat"), lax.axis_size("lon")
    CJ, CI, NM = C // NJ, C // NI, NJ // 2
    LA, CL, RB, N = up(3 * C, LANES), up(C, LANES), up(3 * CJ, PAD), H * W
    ROWS = NJ * RB
    cfg = {"C": C, "H": H, "NJ": NJ, "NI": NI, "factor": 1.0 / math.sqrt(NJ * H * NI * W)}
    sem = pltpu.SemaphoreType.DMA
    vm = pltpu.VMEM
    args = (x_codes, x_scale.T, h_codes, h_scale.T, grad_out, land, partner.reshape(NI, W),
            w_first.transpose(0, 2, 1, 3), w_second.transpose(0, 2, 1, 3))
    shapes = (
        jax.ShapeDtypeStruct((C * H, W), F32),
        jax.ShapeDtypeStruct((3, CJ, 3, CI), F32),
        jax.ShapeDtypeStruct((3, CJ, 3, CI), F32),
    )
    scratch = [vm(arg.shape, arg.dtype) for arg in shapes + args] + [
        sem((9,)), sem((3,)),
        vm((C * H, W), F32),
        vm((C, N), F32),
        vm((9, PAD, LANES), F32),
        vm((2, PAD, LANES), BF16),
        vm((2, NI, PAD, LANES), BF16),
        vm((2, RB, LA), BF16),
        vm((2, 2, NM, RB, LA), BF16),
        vm((LA, ROWS), BF16),
        vm((LA, 3 * C), BF16),
        vm((C, N + 2 * W), BF16),
        vm((C, N), BF16),
        vm((LA, N + 2 * W), BF16),
        vm((LA, N + 2 * W), BF16),
        vm((ROWS, N + W), BF16),
        vm((2, W, CL), BF16),
        vm((2, W, CL), BF16),
        vm((3, NI, PAD, W), BF16),
        vm((3, NI, 2, PAD, W), BF16),
        vm((3, C // PAD, 2, PAD, W), BF16),
        vm((ROWS, 3 * W), BF16),
        vm((ROWS, 3 * C), BF16),
        vm((LA, N + W), F32),
        vm((3 * C, LA), F32),
        vm((2, NM, RB, LA), F32),
        vm((NM, RB, LA), SUM_TYPE),
        vm((NM, RB, LA), SUM_TYPE),
        vm((NM, RB, LA), SUM_TYPE),
        vm((NM, RB, LA), SUM_TYPE),
        vm((RB + PAD, LA), F32),
        vm((NI, PAD, LANES), SUM_TYPE),
        vm((NI, PAD, LANES), SUM_TYPE),
        vm((LANES, LANES), F32),
        vm((NI, RB, LA), F32),
        vm((NI, RB // 2, LA), SUM_TYPE),
        vm((NI, RB // 2, LA), SUM_TYPE),
        vm((NI, RB // 2, LA), SUM_TYPE),
        vm((NI, RB // 2, LA), SUM_TYPE),
        vm((NJ, RB // 2, LANES), F32),
        vm((NJ, RB // 2, LANES), F32),
        sem((2, NI)), sem((2, NI)), sem((2, NM)), sem((2, NM)), sem((2, NM)), sem((2, NM)),
        sem((2, 12)), sem((2, 12)), sem((3, NI)), sem((3, NI)), sem((3, NI)), sem((3, NI)),
        sem((NM,)), sem((NM,)), sem((NM,)), sem((NM,)), sem((NI,)), sem((NI,)),
        sem, sem, sem((NI,)), sem((NI,)), sem((NJ,)), sem((NJ,)),
    ]
    results = pl.pallas_call(
        functools.partial(kernel, cfg),
        out_shape=shapes,
        in_specs=[pl.BlockSpec(memory_space=pl.ANY)] * 9,
        out_specs=[pl.BlockSpec(memory_space=pl.ANY)] * 3,
        scratch_shapes=scratch,
        compiler_params=pltpu.CompilerParams(
            collective_id=0, has_side_effects=True, vmem_limit_bytes=GRANT
        ),
    )(*args)
    grad_in, first, second = pl.pallas_call(
        hand_over,
        out_shape=shapes,
        in_specs=[pl.BlockSpec(memory_space=pl.ANY)] * 3,
        out_specs=[pl.BlockSpec(memory_space=pl.ANY)] * 3,
        scratch_shapes=[vm(arg.shape, arg.dtype) for arg in shapes] + [sem((PARTS + 2,))] * 2,
        compiler_params=pltpu.CompilerParams(vmem_limit_bytes=GRANT),
    )(*results)
    return (grad_in.reshape(C, H, W), first.transpose(0, 2, 1, 3), second.transpose(0, 2, 1, 3))


def solution(mesh):
    placed = (
        P(None, "lat", "lon"),
        P(None, "lat"),
        P(None, "lat", "lon"),
        P(None, "lat"),
        P(None, "lat", "lon"),
        P("lat", "lon"),
        P(),
        P(None, None, "lat", "lon"),
        P(None, None, "lat", "lon"),
    )
    return jax.shard_map(
        body,
        mesh=mesh,
        in_specs=placed,
        out_specs=(P(None, "lat", "lon"), P(None, None, "lat", "lon"), P(None, None, "lat", "lon")),
        check_vma=False,
    )
```

```python
import functools
import math

import jax
import jax.numpy as jnp
from jax import lax
from jax.experimental import pallas as pl
from jax.experimental.pallas import tpu as pltpu
from jax.sharding import PartitionSpec as P

MESH = pl.DeviceIdType.MESH
F32, BF16 = jnp.float32, jnp.bfloat16
PAD = 16
LANES = 128
SUM_TYPE = jnp.bfloat16
PARTS = 2
GRANT = 56 * 1024 * 1024


def up(value, unit):
    return -(-value // unit) * unit


def gelu_parts(h):
    k = math.sqrt(2.0 / math.pi)
    tanh_part = jnp.tanh(k * (h + 0.044715 * h * h * h))
    value = 0.5 * h * (1.0 + tanh_part)
    slope = 0.5 * (1.0 + tanh_part) + 0.5 * h * (1.0 - tanh_part * tanh_part) * k * (
        1.0 + 3.0 * 0.044715 * h * h
    )
    return (value, slope)


def dot(a, b):
    return lax.dot_general(a, b, (((1,), (0,)), ((), ())), preferred_element_type=F32)


def dot_nt(a, b):
    return lax.dot_general(a, b, (((1,), (1,)), ((), ())), preferred_element_type=F32)


def put(tiles, lane, source, source_lane, count, target_lane):
    shift = (target_lane - source_lane) % LANES
    moved = pltpu.roll(source, shift, 1) if shift else source
    tile, off = divmod(target_lane, LANES)
    keep = (lane >= off) & (lane < off + count)
    tiles[tile] = jnp.where(keep, moved, tiles[tile])
    over = off + count - LANES
    if over > 0:
        tiles[tile + 1] = jnp.where(lane < over, moved, tiles[tile + 1])


def put_wide(tiles, lane, sources, source_lane, count, target_lane):
    while count > 0:
        tile, off = divmod(source_lane, LANES)
        part = min(count, LANES - off)
        put(tiles, lane, sources[tile], off, part, target_lane)
        source_lane, target_lane, count = source_lane + part, target_lane + part, count - part


def kernel(
    cfg,
    x_hbm, xs_hbm, h_hbm, hs_hbm, g_hbm, land_hbm, partner_hbm, w0_hbm, w1_hbm,
    out_hbm, first_hbm, second_hbm,
    out_ref, first_ref, second_ref, x_ref,
    xs_ref, h_ref, hs_ref, g_ref, land_ref, partner_ref, w0_ref, w1_ref, in_s, out_s,
    cells, slope, wtmp, wown, wtile, wrow, wfull, wt, wp, fh, act, sg, sx, gq, edge, edge_in,
    mrow, mout, mirr, gqm, spread, qs, nat, tap, given, tap_in, part, part_in, tot, small, small_in,
    turned, tapz, givenz, tapz_in, partz, partz_in, smallz, smallz_in,
    st1_s, st1_r, st2_s, st2_r, fw_s, fw_r, ha_s, ha_r, mi_s, mi_r, mo_s, mo_r,
    r0_s, r0_r, r1_s, r1_r, r2_s, r2_r, z0_s, z0_r, z1_s, z1_r, z2_s, z2_r,
):
    C, H, NJ, NI = cfg["C"], cfg["H"], cfg["NJ"], cfg["NI"]
    W = LANES
    CJ, CI, NM, NG = C // NJ, C // NI, NJ // 2, C // PAD
    LA, CL, RB = up(3 * C, LANES), up(C, LANES), up(3 * (C // NJ), PAD)
    ROWS = NJ * RB
    N = H * W
    j, i = lax.axis_index("lat"), lax.axis_index("lon")
    k, m = lax.rem(j, 2), lax.div(j, 2)
    top = j == NJ - 1
    bottom = j == 0
    worker = top & (i < NG)

    def rcopy(src, dst, ss, rs, dj, di):
        return pltpu.make_async_remote_copy(
            src_ref=src, dst_ref=dst, send_sem=ss, recv_sem=rs,
            device_id={"lat": dj, "lon": di}, device_id_type=MESH,
        )

    def each(lo, hi, fn):
        lax.fori_loop(lo, hi, lambda d, c: (fn(d), c)[1], 0)

    def lon(d):
        return jnp.bitwise_xor(i, d)

    def lat(d):
        return jnp.bitwise_xor(j, d)

    def mate(d):
        return jnp.bitwise_xor(m, d)

    def beside(axis, place, d):
        return lax.rem(place + d + axis, axis)

    lon_order = [d for d in (9, 8, 11, 10, 7, 6, 15, 14, 5, 13, 4, 12, 3, 2, 1) if d < NI]
    lat_order = [d for d in (12, 13, 10, 11, 14, 15, 8, 9, 4, 5, 2, 3, 6, 7, 1) if d < NJ]
    mate_order = [d for d in (4, 6, 5, 7, 2, 1, 3) if d < NM]

    barrier = pltpu.get_barrier_semaphore()

    def greet(dj, di):
        pl.semaphore_signal(barrier, inc=1, device_id={"lat": dj, "lon": di}, device_id_type=MESH)

    for d in lon_order:
        greet(j, lon(d))
    for d in lat_order:
        greet(lat(d), i)
    for dj in (1, -1):
        for di in (1, -1):
            greet(beside(NJ, j, dj), beside(NI, i, di))
    loads = [
        pltpu.make_async_copy(src, dst, in_s.at[n])
        for n, (src, dst) in enumerate((
            (w1_hbm, w1_ref), (w0_hbm, w0_ref), (land_hbm, land_ref), (g_hbm, g_ref), (xs_hbm, xs_ref),
            (x_hbm, x_ref), (hs_hbm, hs_ref), (h_hbm, h_ref), (partner_hbm, partner_ref)))
    ]
    for load in loads:
        load.start()

    loads[0].wait()

    def make_tile(ref):
        wtmp[...] = jnp.zeros(wtmp.shape, F32)
        for a in range(3):
            block = ref[a].astype(F32)
            for b in range(3):
                wtmp[3 * a + b, 0:CJ, 0:CI] = block[:, b, :]
        value = wtmp[0]
        for n in range(1, 9):
            value = value + pltpu.roll(wtmp[n], n * CI, 1)
        return value

    wown[1] = make_tile(w1_ref).astype(BF16)

    def blocks(ref):
        cells[...] = ref[...].astype(F32).reshape(C * H, W)
        return [cells[pl.ds(r, C, stride=H), :] for r in range(H)]

    def ocean(r):
        return land_ref[r:r + 1, :].astype(F32)

    def slot(r):
        return pl.ds((r + 1) * W, W)

    lane = lax.broadcasted_iota(jnp.int32, (C, W), 1)
    center = pl.ds(C, C)
    fy = sg.at[center]

    def add_edges(packed, f, r, blk):
        spots = [f * 8 + r]
        if r == H - 1:
            spots.append(32 + f)
        if r == 0:
            spots.append(48 + f)
        for spot in spots:
            packed = jnp.where(lane == spot, pltpu.roll(blk, spot, 1) if spot else blk, packed)
            packed = jnp.where(lane == 64 + spot, pltpu.roll(blk, 65 + spot, 1), packed)
        return packed

    def turn_edges(phase, packed):
        if CL > C:
            packed = jnp.concatenate([packed, jnp.zeros((CL - C, W), F32)], axis=0)
        edge[phase] = jnp.transpose(packed).astype(BF16)

    for load in loads[2:6]:
        load.wait()
    scale = jnp.transpose(xs_ref[...])
    for r, blk in enumerate(blocks(g_ref)):
        value = blk * ocean(r)
        fy[:, slot(r)] = value.astype(BF16)
    for r, blk in enumerate(blocks(x_ref)):
        x = (blk * scale[:, r:r + 1]).astype(BF16)
        sx[center, slot(r)] = x

    pl.semaphore_wait(barrier, NI - 1 + NJ - 1 + 4)

    def tile_copy(w, d, other):
        return rcopy(wown.at[w], wtile.at[w, i if other is None else other],
                     st1_s.at[w, d], st1_r.at[w, d], j, lon(d))

    for d in lon_order:
        tile_copy(1, d, None).start()
    wtile[1, i] = wown[1]
    def row_copy(phase, src, d, other):
        g = lon(d) if other is None else i
        return rcopy(src.at[pl.ds(pl.multiple_of(g * PAD, PAD), PAD), slot(H - 1)],
                     mrow.at[phase, i if other is None else other],
                     mi_s.at[phase, d], mi_r.at[phase, d], j, lon(d))

    def turned_copy(phase, d, other):
        return rcopy(mout.at[phase, lon(d)], mirr.at[phase, i if other is None else other],
                     mo_s.at[phase, d], mo_r.at[phase, d], j, lon(d))

    def mirror_send(phase, src):
        @pl.when(top)
        def _():
            for d in lon_order:
                @pl.when(lon(d) < NG)
                def _():
                    row_copy(phase, src, d, None).start()

            @pl.when(i < NG)
            def _():
                mrow[phase, i] = src[pl.ds(pl.multiple_of(i * PAD, PAD), PAD), slot(H - 1)]

    def mirror_turn(phase, src):
        @pl.when(worker)
        def _():
            ncols = NI * W
            flip = (lax.broadcasted_iota(jnp.int32, (W, W), 0)
                    + lax.broadcasted_iota(jnp.int32, (W, W), 1)) == W - 1
            flip = jnp.where(flip, 1.0, 0.0).astype(BF16)
            tlane = lax.broadcasted_iota(jnp.int32, (PAD, W), 1)
            where = partner_ref[pl.ds(i, 1), :] + lax.broadcasted_iota(jnp.int32, (1, W), 1) + i * W
            turn = (ncols - 1) - (where & (ncols - 1))
            turn = jnp.broadcast_to(turn, (PAD, W))

            def left(tiles, by):
                if by % W == 0:
                    return [tiles[(t + by // W) % NI] for t in range(NI)]
                moved = [pltpu.roll(tile, W - by, 1) for tile in tiles]
                return [jnp.where(tlane < W - by, moved[t], moved[(t + 1) % NI]) for t in range(NI)]

            each(1, NI, lambda d: row_copy(phase, src, d, lon(d)).wait_recv())
            rev = dot(mrow[phase].reshape(NI * PAD, W), flip)
            tiles = [rev[(NI - 1 - v) * PAD:(NI - v) * PAD] for v in range(NI)]
            for bit in range(ncols.bit_length() - 1):
                take = (turn & (1 << bit)) != 0
                tiles = [jnp.where(take, new, old) for new, old in zip(left(tiles, 1 << bit), tiles)]
            for t in range(NI):
                before, after = pltpu.roll(tiles[t - 1], 1, 1), pltpu.roll(tiles[(t + 1) % NI], 1, 1)
                mout[phase, t, 0] = tiles[t].astype(BF16)
                mout[phase, t, 1] = jnp.where(tlane == 0, before, after).astype(BF16)
            mirr[phase, i] = mout[phase, i]
            for d in lon_order:
                turned_copy(phase, d, None).start()

    def mirror_wait(phase):
        def step(d):
            @pl.when(lon(d) < NG)
            def _():
                turned_copy(phase, d, lon(d)).wait_recv()

        each(1, NI, step)

    def mirrored(phase):
        block = mirr[phase, :, 0].reshape(C, W).astype(F32)
        edges = mirr[phase, :, 1].reshape(C, W).astype(F32)
        before = jnp.where(lane == 0, edges, pltpu.roll(block, 1, 1))
        after = jnp.where(lane == W - 1, pltpu.roll(edges, W - 2, 1), pltpu.roll(block, W - 1, 1))
        return jnp.concatenate([before, block, after], axis=1).astype(BF16)

    mirror_send(0, fy)
    mirror_send(2, sx.at[center])
    def halo_copies(phase, fields):
        north, south = jnp.logical_not(top), jnp.logical_not(bottom)
        out = []
        for f, field in enumerate(fields):
            s = 2 * f
            out.append((rcopy(field.at[:, slot(H - 1)], field.at[:, slot(-1)],
                              ha_s.at[phase, s], ha_r.at[phase, s], beside(NJ, j, 1), i), north, south))
            out.append((rcopy(field.at[:, slot(0)], field.at[:, slot(H)],
                              ha_s.at[phase, s + 1], ha_r.at[phase, s + 1], beside(NJ, j, -1), i), south, north))
        side = up(8 * len(fields), PAD)
        n = 6
        for di, base, target in ((1, 64, 0), (-1, 0, 64)):
            for dj, off, size in ((0, 0, side), (1, 32, PAD), (-1, 48, PAD)):
                sent, comes = {0: (None, None), 1: (north, south), -1: (south, north)}[dj]
                out.append((rcopy(edge.at[phase, pl.ds(base + off, size)],
                                  edge_in.at[phase, pl.ds(target + off, size)],
                                  ha_s.at[phase, n], ha_r.at[phase, n],
                                  beside(NJ, j, dj), beside(NI, i, di)), sent, comes))
                n += 1
        return out

    def only(condition, fn):
        if condition is None:
            fn()
        else:
            pl.when(condition)(fn)

    def halo_start(copies):
        for copy, sent, _ in copies:
            only(sent, copy.start)

    def halo_wait(copies):
        for copy, _, comes in copies:
            only(comes, copy.wait_recv)

    def halo_sent(copies):
        for copy, sent, _ in copies:
            only(sent, copy.wait_send)

    early = halo_copies(0, (fy, sx.at[center]))
    halo_start(early[:4])
    packed = jnp.zeros((C, W), F32)
    for r in range(H):
        packed = add_edges(packed, 0, r, fy[:, slot(r)].astype(F32))
        packed = add_edges(packed, 1, r, sx[center, slot(r)].astype(F32))
    turn_edges(0, packed)
    halo_start(early[4:])
    loads[1].wait()
    wown[0] = make_tile(w0_ref).astype(BF16)

    for load in loads[6:]:
        load.wait()
    scale = jnp.transpose(hs_ref[...])
    for r, blk in enumerate(blocks(h_ref)):
        h = blk * scale[:, r:r + 1]
        value, deriv = gelu_parts(h)
        act[:, r * W:(r + 1) * W] = (ocean(r) * value).astype(BF16)
        slope[:, r * W:(r + 1) * W] = deriv


    for d in lon_order:
        tile_copy(0, d, None).start()
    wtile[0, i] = wown[0]
    at = lax.broadcasted_iota(jnp.int32, (ROWS, 1), 0)
    half, rest = lax.div(at, NM * RB), lax.rem(at, NM * RB)
    own = lax.rem(rest, RB)
    line = lax.div(own, CJ)
    target = line * C + (2 * lax.div(rest, RB) + half) * CJ + own - line * CJ
    target = jnp.where(own < 3 * CJ, target, -1)
    spread[...] = jnp.where(lax.broadcasted_iota(jnp.int32, (ROWS, 3 * C), 1) == target, 1.0, 0.0).astype(BF16)

    def make_slab(w):
        each(1, NI, lambda d: tile_copy(w, d, lon(d)).wait_recv())
        wlane = lax.broadcasted_iota(jnp.int32, (PAD, W), 1)
        tot[...] = jnp.zeros(tot.shape, F32)
        pieces = [wtile[w, s].astype(F32) for s in range(NI)]
        for a in range(3):
            tiles = [jnp.zeros((PAD, W), F32) for _ in range(LA // W)]
            for s in range(NI):
                for b in range(3):
                    put(tiles, wlane, pieces[s], (3 * a + b) * CI, CI, b * C + s * CI)
            for t, value in enumerate(tiles):
                tot[a * CJ:(a + 1) * CJ, t * W:(t + 1) * W] = value[:CJ]
        wrow[w] = tot[0:RB].astype(BF16)

    def slab_copy(w, d, other):
        return rcopy(wrow.at[w], wfull.at[w, k, m if other is None else other],
                     st2_s.at[w, d], st2_r.at[w, d], 2 * mate(d) + k, i)

    def forward_copy(w, d, mine):
        n = mate(d)
        return rcopy(wfull.at[w, k, n], wfull.at[w, k if mine else 1 - k, n],
                     fw_s.at[w, d], fw_r.at[w, d], j + 1 - 2 * k, i)

    def own_forward(w, mine):
        return rcopy(wrow.at[w], wfull.at[w, k if mine else 1 - k, m], fw_s.at[w, 0], fw_r.at[w, 0],
                     j + 1 - 2 * k, i)

    def send_slab(w):
        for d in mate_order:
            slab_copy(w, d, None).start()
        own_forward(w, True).start()
        wfull[w, k, m] = wrow[w]

    def pass_on(w):
        def step(d):
            slab_copy(w, d, mate(d)).wait_recv()
            forward_copy(w, d, True).start()

        each(1, NM, step)

    def have_weights(w):
        own_forward(w, False).wait_recv()
        each(1, NM, lambda d: forward_copy(w, d, False).wait_recv())
        wt[...] = jnp.transpose(wfull[w].reshape(ROWS, LA).astype(F32)).astype(BF16)

    def columns(got, f):
        result = []
        for base in (0, 64):
            start = base + f * 8
            value = jnp.where((lane >= 1) & (lane <= H), pltpu.roll(got, (1 - start) % W, 1), 0.0)
            lower = pltpu.roll(got, (-(base + 32 + f)) % W, 1)
            upper = pltpu.roll(got, (H + 1 - (base + 48 + f)) % W, 1)
            value = jnp.where((lane == 0) & jnp.logical_not(bottom), lower, value)
            value = jnp.where((lane == H + 1) & jnp.logical_not(top), upper, value)
            result.append(value)
        return result

    def turned_edges(phase):
        return jnp.transpose(edge_in[phase].astype(F32))[:C]

    def clear_ends(field):
        @pl.when(bottom)
        def _():
            field[:, slot(-1)] = jnp.zeros((C, W), BF16)

        @pl.when(top)
        def _():
            field[:, slot(H)] = jnp.zeros((C, W), BF16)

    def shifted(field, west, east):
        for r in range(-1, H + 1):
            blk = field[center, slot(r)].astype(F32)
            lower = jnp.where(lane == 0, pltpu.roll(west, (-(r + 1)) % W, 1), pltpu.roll(blk, 1, 1))
            upper = jnp.where(lane == W - 1, pltpu.roll(east, (W - 2 - r) % W, 1), pltpu.roll(blk, W - 1, 1))
            field[0:C, slot(r)] = lower.astype(BF16)
            field[2 * C:3 * C, slot(r)] = upper.astype(BF16)
        if LA > 3 * C:
            field[3 * C:LA, :] = jnp.zeros((LA - 3 * C, (H + 2) * W), BF16)

    def tap_rows(field, n, size):
        return jnp.concatenate([field[:, (2 - a) * W + n:(2 - a) * W + n + size] for a in range(3)], axis=0)

    def edge_rows(west, east):
        both = []
        for a in range(3):
            at_west = pltpu.roll(west, (a - 2) % W, 1)
            at_east = pltpu.roll(east, (H + a - 2) % W, 1)
            value = jnp.where(lane < H, at_west, jnp.where(lane < 2 * H, at_east, 0.0))
            both.append(value.astype(BF16))
        return jnp.concatenate(both, axis=0)

    def fold_rows(mirror):
        return jnp.concatenate([jnp.zeros((2 * C, 3 * W), BF16), mirror], axis=0)

    step = min(2 * W, N)

    def tap_grad(grad, field):
        for a in range(3):
            nat[a * C:(a + 1) * C, :] = dot_nt(grad[:, W:W + N], field[:, a * W:a * W + N])

    def tap_store():
        for a in range(3):
            for jj in range(NJ):
                tap[jj % 2, jj // 2, a * CJ:(a + 1) * CJ, :] = nat[a * C + jj * CJ:a * C + (jj + 1) * CJ, :]

    def side_store():
        for a in range(3):
            for s in range(NI):
                tapz[s, a * CI:(a + 1) * CI, :] = nat[a * C + s * CI:a * C + (s + 1) * CI, :]

    def add_fold(weight, rows):
        share = dot(weight[0:C, :], rows[:, 0:W])
        for b in (1, 2):
            share = share + dot(weight[b * C:(b + 1) * C, :], rows[:, b * W:(b + 1) * W])
        qs[C:2 * C, N - W:N] += share

    def shift_sum():
        first, last = qs[0:C, N:N + W], qs[2 * C:3 * C, N:N + W]
        result = []
        for r in range(H):
            at = slice(r * W, (r + 1) * W)
            left = jnp.where(lane == W - 1, pltpu.roll(first, (W - 1 - H - r) % W, 1),
                             pltpu.roll(qs[0:C, at], W - 1, 1))
            right = jnp.where(lane == 0, pltpu.roll(last, (-r) % W, 1), pltpu.roll(qs[2 * C:3 * C, at], 1, 1))
            result.append(qs[C:2 * C, at] + left + right)
        return result

    def pair_copy(n):
        return rcopy(given.at[n], tap_in.at[n], r0_s.at[n], r0_r.at[n], j + 1 - 2 * k, i)

    def chip_copy(d, other):
        return rcopy(part.at[mate(d)], part_in.at[m if other is None else other],
                     r1_s.at[d], r1_r.at[d], 2 * mate(d) + k, i)

    def lon_copy(d, other):
        return rcopy(small.at[lon(d)], small_in.at[i if other is None else other], r2_s.at[d], r2_r.at[d], j, lon(d))

    def sum_start():
        given[...] = tap[1 - k].astype(SUM_TYPE)
        for d in mate_order:
            pair_copy(mate(d)).start()
        pair_copy(m).start()

    def sum_chips():
        for d in mate_order:
            n = mate(d)
            pair_copy(n).wait_recv()
            part[n] = (tap[k, n] + tap_in[n].astype(F32)).astype(SUM_TYPE)
            chip_copy(d, None).start()
        pair_copy(m).wait_recv()

    def sum_lon():
        total = tap[k, m] + tap_in[m].astype(F32)
        for d in range(1, NM):
            chip_copy(d, mate(d)).wait_recv()
            total = total + part_in[mate(d)].astype(F32)
        tot[0:RB] = total
        slane = lax.broadcasted_iota(jnp.int32, (PAD, W), 1)
        sources = [[tot[a * CJ:a * CJ + PAD, t * W:(t + 1) * W] for t in range(LA // W)] for a in range(3)]
        for s in range(NI):
            tiles = [jnp.zeros((PAD, W), F32)]
            for a in range(3):
                for b in range(3):
                    put_wide(tiles, slane, sources[a], b * C + s * CI, CI, (3 * a + b) * CI)
            small[s] = tiles[0].astype(SUM_TYPE)
        small_in[i] = small[i]
        for d in sorted(lon_order, key=lambda d: d % 2 == 0):
            lon_copy(d, None).start()

    def sum_end():
        each(1, NI, lambda d: lon_copy(d, lon(d)).wait_recv())
        total = small_in[0].astype(F32)
        for s in range(1, NI):
            total = total + small_in[s].astype(F32)
        total = total * cfg["factor"]
        for a in range(3):
            for b in range(3):
                n = 3 * a + b
                moved = pltpu.roll(total, (-n * CI) % W, 1) if n else total
                first_ref[a, :, b, :] = moved[:CJ, :CI]

    HR = RB // 2
    mine = pl.ds(pl.multiple_of(k * HR, HR), HR)
    others = pl.ds(pl.multiple_of((1 - k) * HR, HR), HR)

    def side_pair():
        return rcopy(givenz, tapz_in, z0_s, z0_r, j + 1 - 2 * k, i)

    def side_lon(d, other):
        return rcopy(partz.at[lon(d)], partz_in.at[i if other is None else other], z1_s.at[d], z1_r.at[d], j, lon(d))

    def side_lat(d, other):
        return rcopy(smallz.at[lat(d)], smallz_in.at[j if other is None else other], z2_s.at[d], z2_r.at[d], lat(d), i)

    def side_start():
        givenz[...] = tapz[:, others].astype(SUM_TYPE)
        side_pair().start()

    def side_sum_lon():
        side_pair().wait_recv()
        for s in range(NI):
            partz[s] = (tapz[s, mine] + tapz_in[s].astype(F32)).astype(SUM_TYPE)
        side_send(1)

    def side_send(odd):
        for d in lon_order:
            if d % 2 == odd:
                side_lon(d, None).start()

    def side_sum_lat():
        total = tapz[i, mine] + tapz_in[i].astype(F32)
        for d in range(1, NI):
            side_lon(d, lon(d)).wait_recv()
            total = total + partz_in[lon(d)].astype(F32)
        slane = lax.broadcasted_iota(jnp.int32, (HR, W), 1)
        sources = [total[:, t * W:(t + 1) * W] for t in range(LA // W)]
        for s in range(NJ):
            tiles = [jnp.zeros((HR, W), F32)]
            for a in range(3):
                put_wide(tiles, slane, sources, a * C + s * CJ, CJ, a * CJ)
            smallz[s] = tiles[0]
        smallz_in[j] = smallz[j]
        for d in lat_order:
            side_lat(d, None).start()

    def side_end():
        each(1, NJ, lambda d: side_lat(d, lat(d)).wait_recv())
        halves = []
        for h in range(2):
            total = smallz_in[h]
            for s in range(h + 2, NJ, 2):
                total = total + smallz_in[s]
            halves.append(total)
        total = jnp.concatenate(halves + [jnp.zeros((W - RB, W), F32)], axis=0) * cfg["factor"]
        turned[...] = jnp.transpose(total)
        for b in range(3):
            block = turned[(2 - b) * CJ:(3 - b) * CJ, :]
            for a in range(3):
                moved = pltpu.roll(block, (-a * CI) % W, 1) if a else block
                second_ref[a, :, b, :] = moved[:, :CI]

    make_slab(1)
    send_slab(1)
    mirror_turn(0, fy)
    tap[:, :, 3 * CJ:RB, :] = jnp.zeros((2, NM, RB - 3 * CJ, LA), F32)
    tapz[:, 3 * CI:RB, :] = jnp.zeros((NI, RB - 3 * CI, LA), F32)

    halo_wait(early)
    clear_ends(fy)
    clear_ends(sx.at[center])
    got = turned_edges(0)
    west, east = columns(got, 0)
    for n in range(0, N, step):
        gq[:, n:n + step] = dot(spread[...], tap_rows(fy, n, step)).astype(BF16)
    gq[:, N:N + W] = dot(spread[...], edge_rows(west, east)).astype(BF16)
    mirror_turn(2, sx.at[center])
    shifted(sg, west, east)
    west, east = columns(got, 1)
    shifted(sx, west, east)
    for a in range(3):
        nat[a * C:(a + 1) * C, :] = dot_nt(act[...], sg[:, (2 - a) * W:(2 - a) * W + N])
    make_slab(0)
    pass_on(1)
    send_slab(0)
    side_store()
    @pl.when(top)
    def _():
        mirror_wait(0)
        mirror = mirrored(0)
        stacked = jnp.concatenate([mirror[:, 2 * W:3 * W], mirror[:, W:2 * W], mirror[:, 0:W],
                                   jnp.zeros((LA - 3 * C, W), BF16)], axis=0)
        nat[0:C, :] = dot_nt(act[:, N - W:N], stacked)
        for s in range(NI):
            tapz[s, 2 * CI:3 * CI, :] += nat[s * CI:(s + 1) * CI, :]
        gqm[...] = dot(spread[...], fold_rows(mirror)).astype(BF16)

    side_start()
    have_weights(1)
    for n in range(0, N + W, step):
        size = min(step, N + W - n)
        qs[:, n:n + size] = dot(wt[...], gq[:, n:n + size])

    side_sum_lon()

    @pl.when(m != NM - 1)
    def _():
        side_send(0)

    @pl.when(top)
    def _():
        add_fold(wt, gqm)
        mirror_wait(2)
        north = mirrored(2)
        for b in range(3):
            sx[b * C:(b + 1) * C, slot(H)] = north[:, b * W:(b + 1) * W]

    for r, value in enumerate(shift_sum()):
        fh[:, slot(r)] = (value * ocean(r) * slope[:, r * W:(r + 1) * W]).astype(BF16)

    mirror_send(1, fh)

    @pl.when(m == NM - 1)
    def _():
        side_send(0)

    tap_grad(fh, sx)
    tap_store()
    sum_start()
    packed = jnp.zeros((C, W), F32)
    for r in range(H):
        packed = add_edges(packed, 0, r, fh[:, slot(r)].astype(F32))
    turn_edges(1, packed)
    late = halo_copies(1, (fh,))
    sum_chips()
    halo_start(late)


    pass_on(0)
    have_weights(0)
    wp[...] = dot(wt[...], spread[...]).astype(BF16)
    mirror_turn(1, fh)
    side_sum_lat()
    sum_lon()

    halo_wait(late)
    clear_ends(fh)
    west, east = columns(turned_edges(1), 0)
    for n in range(0, N, step):
        qs[:, n:n + step] = dot(wp[...], tap_rows(fh, n, step))
    qs[:, N:N + W] = dot(wp[...], edge_rows(west, east))

    @pl.when(top)
    def _():
        mirror_wait(1)
        add_fold(wp, fold_rows(mirrored(1)))

    cells[...] = g_ref[...].astype(F32).reshape(C * H, W)
    for r, value in enumerate(shift_sum()):
        at = pl.ds(r, C, stride=H)
        out_ref[at, :] = cells[at, :] + value
    results = [
        pltpu.make_async_copy(src, dst, out_s.at[n])
        for n, (src, dst) in enumerate(((out_ref, out_hbm), (second_ref, second_hbm), (first_ref, first_hbm)))
    ]
    results[0].start()

    halo_sent(early + late)
    for w in range(2):
        each(1, NI, lambda d: tile_copy(w, d, None).wait_send())
        own_forward(w, True).wait_send()
        each(1, NM, lambda d: slab_copy(w, d, None).wait_send())
        each(1, NM, lambda d: forward_copy(w, d, True).wait_send())
    each(0, NM, lambda n: pair_copy(n).wait_send())
    each(1, NM, lambda d: chip_copy(d, None).wait_send())
    side_pair().wait_send()
    each(1, NI, lambda d: side_lon(d, None).wait_send())

    @pl.when(top)
    def _():
        for phase in range(3):
            def sent(d):
                @pl.when(lon(d) < NG)
                def _():
                    row_copy(phase, fy, d, None).wait_send()

            each(1, NI, sent)

    @pl.when(worker)
    def _():
        for phase in range(3):
            each(1, NI, lambda d: turned_copy(phase, d, None).wait_send())

    side_end()
    results[1].start()
    sum_end()
    results[2].start()
    each(1, NI, lambda d: lon_copy(d, None).wait_send())
    each(1, NJ, lambda d: side_lat(d, None).wait_send())
    for result in results:
        result.wait()


def hand_over(out_in, first_in, second_in, out_ref, first_ref, second_ref, out_mid, first_mid, second_mid, came, went):
    size = out_in.shape[0] // PARTS
    ways = [(out_in.at[pl.ds(n * size, size)], out_mid.at[pl.ds(n * size, size)], out_ref.at[pl.ds(n * size, size)])
            for n in range(PARTS)]
    ways += [(first_in, first_mid, first_ref), (second_in, second_mid, second_ref)]
    first = [pltpu.make_async_copy(a, b, came.at[n]) for n, (a, b, _) in enumerate(ways)]
    then = [pltpu.make_async_copy(b, c, went.at[n]) for n, (_, b, c) in enumerate(ways)]
    for copy in first:
        copy.start()
    for copy, following in zip(first, then):
        copy.wait()
        following.start()
    for copy in then:
        copy.wait()


def body(x_codes, x_scale, h_codes, h_scale, grad_out, land, partner, w_first, w_second):
    C, H, W = x_codes.shape
    NJ, NI = lax.axis_size("lat"), lax.axis_size("lon")
    CJ, CI, NM = C // NJ, C // NI, NJ // 2
    LA, CL, RB, N = up(3 * C, LANES), up(C, LANES), up(3 * CJ, PAD), H * W
    ROWS = NJ * RB
    cfg = {"C": C, "H": H, "NJ": NJ, "NI": NI, "factor": 1.0 / math.sqrt(NJ * H * NI * W)}
    sem = pltpu.SemaphoreType.DMA
    vm = pltpu.VMEM
    args = (x_codes, x_scale.T, h_codes, h_scale.T, grad_out, land, partner.reshape(NI, W),
            w_first.transpose(0, 2, 1, 3), w_second.transpose(0, 2, 1, 3))
    shapes = (
        jax.ShapeDtypeStruct((C * H, W), F32),
        jax.ShapeDtypeStruct((3, CJ, 3, CI), F32),
        jax.ShapeDtypeStruct((3, CJ, 3, CI), F32),
    )
    scratch = [vm(arg.shape, arg.dtype) for arg in shapes + args] + [
        sem((9,)), sem((3,)),
        vm((C * H, W), F32),
        vm((C, N), F32),
        vm((9, PAD, LANES), F32),
        vm((2, PAD, LANES), BF16),
        vm((2, NI, PAD, LANES), BF16),
        vm((2, RB, LA), BF16),
        vm((2, 2, NM, RB, LA), BF16),
        vm((LA, ROWS), BF16),
        vm((LA, 3 * C), BF16),
        vm((C, N + 2 * W), BF16),
        vm((C, N), BF16),
        vm((LA, N + 2 * W), BF16),
        vm((LA, N + 2 * W), BF16),
        vm((ROWS, N + W), BF16),
        vm((2, W, CL), BF16),
        vm((2, W, CL), BF16),
        vm((3, NI, PAD, W), BF16),
        vm((3, NI, 2, PAD, W), BF16),
        vm((3, C // PAD, 2, PAD, W), BF16),
        vm((ROWS, 3 * W), BF16),
        vm((ROWS, 3 * C), BF16),
        vm((LA, N + W), F32),
        vm((3 * C, LA), F32),
        vm((2, NM, RB, LA), F32),
        vm((NM, RB, LA), SUM_TYPE),
        vm((NM, RB, LA), SUM_TYPE),
        vm((NM, RB, LA), SUM_TYPE),
        vm((NM, RB, LA), SUM_TYPE),
        vm((RB + PAD, LA), F32),
        vm((NI, PAD, LANES), SUM_TYPE),
        vm((NI, PAD, LANES), SUM_TYPE),
        vm((LANES, LANES), F32),
        vm((NI, RB, LA), F32),
        vm((NI, RB // 2, LA), SUM_TYPE),
        vm((NI, RB // 2, LA), SUM_TYPE),
        vm((NI, RB // 2, LA), SUM_TYPE),
        vm((NI, RB // 2, LA), SUM_TYPE),
        vm((NJ, RB // 2, LANES), F32),
        vm((NJ, RB // 2, LANES), F32),
        sem((2, NI)), sem((2, NI)), sem((2, NM)), sem((2, NM)), sem((2, NM)), sem((2, NM)),
        sem((2, 12)), sem((2, 12)), sem((3, NI)), sem((3, NI)), sem((3, NI)), sem((3, NI)),
        sem((NM,)), sem((NM,)), sem((NM,)), sem((NM,)), sem((NI,)), sem((NI,)),
        sem, sem, sem((NI,)), sem((NI,)), sem((NJ,)), sem((NJ,)),
    ]
    results = pl.pallas_call(
        functools.partial(kernel, cfg),
        out_shape=shapes,
        in_specs=[pl.BlockSpec(memory_space=pl.ANY)] * 9,
        out_specs=[pl.BlockSpec(memory_space=pl.ANY)] * 3,
        scratch_shapes=scratch,
        compiler_params=pltpu.CompilerParams(
            collective_id=0, has_side_effects=True, vmem_limit_bytes=GRANT
        ),
    )(*args)
    grad_in, first, second = pl.pallas_call(
        hand_over,
        out_shape=shapes,
        in_specs=[pl.BlockSpec(memory_space=pl.ANY)] * 3,
        out_specs=[pl.BlockSpec(memory_space=pl.ANY)] * 3,
        scratch_shapes=[vm(arg.shape, arg.dtype) for arg in shapes] + [sem((PARTS + 2,))] * 2,
        compiler_params=pltpu.CompilerParams(vmem_limit_bytes=GRANT),
    )(*results)
    return (grad_in.reshape(C, H, W), first.transpose(0, 2, 1, 3), second.transpose(0, 2, 1, 3))


def solution(mesh):
    placed = (
        P(None, "lat", "lon"),
        P(None, "lat"),
        P(None, "lat", "lon"),
        P(None, "lat"),
        P(None, "lat", "lon"),
        P("lat", "lon"),
        P(),
        P(None, None, "lat", "lon"),
        P(None, None, "lat", "lon"),
    )
    return jax.shard_map(
        body,
        mesh=mesh,
        in_specs=placed,
        out_specs=(P(None, "lat", "lon"), P(None, None, "lat", "lon"), P(None, None, "lat", "lon")),
        check_vma=False,
    )
```
